32 devices in a mesh: section: 2 (over core), row: 4 (over z), col: 4 (over y, x).
Axes of the slice: x: 2, y: 2, z: 4, core: 2. Of those that a mesh axis runs over, the one named last changes fastest.
Arguments:
- hidden_in: bfloat16 [2, 4, 1024, 1024], P(None, 'col', 'row'), may hold values from -6 to 6
- doc_ids: int32 [2, 4, 1024], P(None, 'col'), may hold values from 0 to 3, never falling along the last dimension, each value on 1 to 512 neighbouring positions
- qkv_weight: bfloat16 [2, 1024, 3, 1024], P('section', 'col', None, 'row'), may hold values from -0.1875 to 0.1875
- out_weight: bfloat16 [2, 1024, 1024], P('section', 'row', 'col'), may hold values from -1.5 to 1.5
- up_weight: bfloat16 [2, 1024, 4096], P('section', 'col', 'row'), may hold values from -0.1875 to 0.1875
- down_weight: bfloat16 [2, 4096, 1024], P('section', 'row', 'col'), may hold values from -0.09375 to 0.09375
- attn_gain: float32 [2, 1024], P('section', ('row', 'col')), may hold values from 0.5 to 1.5
- attn_shift: float32 [2, 1024], P('section', ('row', 'col')), may hold values from -1.75 to 1.75
- mlp_gain: float32 [2, 1024], P('section', ('row', 'col')), may hold values from 0.5 to 1.5
- mlp_shift: float32 [2, 1024], P('section', ('row', 'col')), may hold values from -1.75 to 1.75
- out_cotangent: bfloat16 [2, 4, 1024, 1024], P(None, 'col', 'row'), may hold values from -6 to 6
Outputs:
- layer_outputs: bfloat16 [2, 2, 4, 1024, 1024], P('section', None, 'col', 'row')
- input_grads: bfloat16 [2, 2, 4, 1024, 1024], P('section', None, 'col', 'row')
- qkv_grad: float32 [2, 1024, 3, 1024], P('section', 'col', None, 'row')
- out_grad: float32 [2, 1024, 1024], P('section', 'row', 'col')
- up_grad: float32 [2, 1024, 4096], P('section', 'col', 'row')
- down_grad: float32 [2, 4096, 1024], P('section', 'row', 'col')
- attn_gain_grad: float32 [2, 1024], P('section', ('row', 'col'))
- attn_shift_grad: float32 [2, 1024], P('section', ('row', 'col'))
- mlp_gain_grad: float32 [2, 1024], P('section', ('row', 'col'))
- mlp_shift_grad: float32 [2, 1024], P('section', ('row', 'col'))
The draws below stay inside these ranges and needn't reach their ends.
Inputs may be any that keep to these rules, and one draw needn't show every extreme that they name: `doc_ids`: in each sequence the document numbers never fall, every number appears, each document has 1 to 512 tokens and one has exactly 512.
All inputs are finite; a program needn't handle non-finite values.
Results may differ from the reference program's by a relative error of at most 0.02.
Values may be sent and summed in bfloat16 or wider, within the bound.
No kernel may reach another device: no remote copies, remote signals or barrier semaphores. Data moves between devices by JAX's collectives and lax.ppermute only.
A program may use at most 256 MiB of HBM per device.

```python
import math
import jax
import jax.numpy as jnp
import numpy as np
from jax import lax

D = 1024
FF = 4096
HEAD_DIM = 64
ROT = 16
SEQ = 1024
MICRO = 2
DOCS = 4
SEQS = 4


def steps_of(stream_key, shape, cuts, least, largest):
    loudness, own = 1.0, jax.random.fold_in(stream_key, 6)
    for dim, shards_of in cuts:
        heights = jnp.exp(jax.random.uniform(jax.random.fold_in(own, dim), (shards_of,), jnp.float32, least / len(cuts), largest / len(cuts)))
        loudness = loudness * jnp.repeat(heights, shape[dim] // shards_of).reshape([-1 if axis == dim else 1 for axis in range(len(shape))])
    return loudness


def profile(number_of, total, limit, lean):
    portions = [(1 << 20) // math.isqrt(grade ** lean) + 1 for grade in range(2, number_of + 1)]
    spare, counts = total - limit - (number_of - 1), [1] * (number_of - 1)
    while spare > 0:
        candidates = [i for i in range(number_of - 1) if counts[i] < limit]
        mass, left = sum([portions[i] for i in candidates]), spare
        for i in candidates:
            more = min(limit - counts[i], max(1, left * portions[i] // mass), spare)
            counts[i] = counts[i] + more
            spare = spare - more
    return np.array([limit] + counts)


def uneven_parts(rng, number_of, total, bound, slope):
    if number_of == 2:
        one = jax.random.randint(rng, (), max(1, total - bound), min(bound, total - 1) + 1)
        return jnp.stack([one, total - one])
    tallies = jnp.asarray(profile(number_of, total, bound, slope), jnp.int32)
    couples = (number_of - 1) // 2
    giver, receiver = tallies[1:1 + 2 * couples:2], tallies[2:2 + 2 * couples:2]
    room = jnp.minimum(giver - 1, bound - receiver)
    shifted = jax.random.randint(jax.random.fold_in(rng, 1), (couples,), 0, 1 << 20) % (room + 1)
    tallies = tallies.at[1:1 + 2 * couples:2].set(giver - shifted).at[2:2 + 2 * couples:2].set(receiver + shifted)
    return tallies[jax.random.permutation(jax.random.fold_in(rng, 2), number_of)]


def gaussian(rng, shape, spread, limit, shards=(), kind=jnp.bfloat16):
    result = jax.random.normal(rng, shape, jnp.float32) * spread
    if len(shards) > 0:
        result = steps_of(rng, shape, shards, -0.22, 0.18) * result
    return jnp.clip(result, min=-limit, max=limit).astype(kind)


def setup_inputs(seed: int = 0) -> dict:
    key_of = jax.random.split(jax.random.key(seed), 12)
    return {
        "hidden_in": gaussian(key_of[0], (MICRO, SEQS, SEQ, D), 1.0, 6.0, ((1, 4), (2, 4))),
        "doc_ids": jax.vmap(lambda own: jnp.searchsorted(jnp.cumsum(uneven_parts(own, DOCS, SEQ, SEQ // 2, 0)), jnp.arange(SEQ), side="right"))(jax.random.split(key_of[1], MICRO * SEQS)).reshape((MICRO, SEQS, SEQ)).astype(jnp.int32),
        "qkv_weight": gaussian(key_of[2], (2, D, 3, D), D ** -0.5, 0.1875, ((0, 2), (1, 4), (3, 4))),
        "out_weight": gaussian(key_of[3], (2, D, D), (D * 16 // SEQ) ** -0.5, 1.5, ((0, 2), (1, 4), (2, 4))),
        "up_weight": gaussian(key_of[4], (2, D, FF), D ** -0.5, 0.1875, ((0, 2), (1, 4), (2, 4))),
        "down_weight": gaussian(key_of[5], (2, FF, D), FF ** -0.5, 0.09375, ((0, 2), (1, 4), (2, 4))),
        "attn_gain": jnp.clip(1.0 + 0.1 * jax.random.normal(key_of[6], (2, D), jnp.float32), 0.5, 1.5),
        "attn_shift": gaussian(key_of[7], (2, D), 0.3, 1.75, ((0, 2), (1, 16)), jnp.float32),
        "mlp_gain": jnp.clip(1.0 + 0.1 * jax.random.normal(key_of[8], (2, D), jnp.float32), 0.5, 1.5),
        "mlp_shift": gaussian(key_of[9], (2, D), 0.3, 1.75, ((0, 2), (1, 16)), jnp.float32),
        "out_cotangent": gaussian(key_of[10], (MICRO, SEQS, SEQ, D), 1.0, 6.0, ((1, 4), (2, 4))),
    }


@jax.custom_vjp
def low(v):
    return lax.optimization_barrier(v.astype(jnp.bfloat16)).astype(jnp.float32)

@jax.custom_vjp
def low_back(v):
    return v

def low_keep(v):
    return (low(v), None)

def low_pass(kept, grad):
    return (grad,)

def back_keep(v):
    return (v, None)

def back_low(kept, grad):
    return (low(grad),)
low.defvjp(low_keep, low_pass)
low_back.defvjp(back_keep, back_low)
EPSILON = 1e-05
NEG_FILL = -1e+30
HIGH = lax.Precision.HIGHEST

def positions_of(docs):
    length = docs.shape[0]
    index = jnp.arange(length, dtype=jnp.int32)
    starts = jnp.concatenate([jnp.ones((1,), jnp.bool_), docs[1:] != docs[:-1]])
    first = lax.cummax(jnp.where(starts, index, 0).astype(jnp.int32), axis=0)
    return index - first

def rotary_tables(docs):
    half = ROT // 2
    freqs = 10000.0 ** (-2.0 * jnp.arange(half, dtype=jnp.float32) / ROT)
    angles = positions_of(docs).astype(jnp.float32)[:, None] * freqs[None, :]
    return (jnp.cos(angles)[:, None, :], jnp.sin(angles)[:, None, :])

def rotate(values, cosine, sine):
    half = ROT // 2
    front = values[..., :half]
    back = values[..., half:ROT]
    return jnp.concatenate([front * cosine - back * sine, back * cosine + front * sine, values[..., ROT:]], axis=-1)

def attend(query, key, value, docs):
    length = query.shape[0]
    index = jnp.arange(length, dtype=jnp.int32)
    allowed = (docs[:, None] == docs[None, :]) & (index[None, :] <= index[:, None])
    factor = 1.0 / math.sqrt(query.shape[2])

    def one_head(operands):
        head_query, head_key, head_value = operands
        scores = low_back(jnp.dot(head_query, head_key.T, precision=HIGH) * factor)
        scores = jnp.where(allowed, scores, NEG_FILL)
        peak = lax.optimization_barrier(jnp.max(scores, axis=-1, keepdims=True))
        raised = jnp.exp(scores - peak)
        probs = low(raised / lax.optimization_barrier(jnp.sum(raised, axis=-1, keepdims=True)))
        return jnp.dot(probs, head_value, precision=HIGH)
    heads_out = lax.map(jax.checkpoint(one_head), (query.transpose(1, 0, 2), key.transpose(1, 0, 2), value.transpose(1, 0, 2)))
    return heads_out.transpose(1, 0, 2)

def one_sequence(operands):
    query, key, value, docs = operands
    return attend(query, key, value, docs)

def layer(hidden, qkv_w, out_w, up_w, down_w, gain_a, shift_a, gain_m, shift_m, docs, cosine, sine):
    count, length, width = hidden.shape
    center = hidden - lax.optimization_barrier(jnp.mean(hidden, axis=-1, keepdims=True))
    normed = center * lax.rsqrt(lax.optimization_barrier(jnp.mean(center * center, axis=-1, keepdims=True)) + EPSILON)
    attn_in = low(normed * gain_a + shift_a)
    feed_in = low(normed * gain_m + shift_m)
    project = jnp.einsum('nld,dke->nlke', attn_in, qkv_w, precision=HIGH)
    heads = width // HEAD_DIM
    shaped = project.reshape(count, length, 3, heads, HEAD_DIM)
    query = low(rotate(low_back(shaped[:, :, 0]), cosine, sine))
    key = low(rotate(low_back(shaped[:, :, 1]), cosine, sine))
    value = low(low_back(shaped[:, :, 2]))
    context = lax.map(jax.checkpoint(one_sequence), (query, key, value, docs))
    context = low(low_back(context.reshape(count, length, width)))
    pre = low_back(jnp.einsum('nld,df->nlf', feed_in, up_w, precision=HIGH))
    active = low(jax.nn.gelu(pre, approximate=False))
    attention = jnp.einsum('nle,ed->nld', context, out_w, precision=HIGH)
    feed = jnp.einsum('nlf,fd->nld', active, down_w, precision=HIGH)
    return hidden + attention + feed

def reference(hidden_in, doc_ids, qkv_weight, out_weight, up_weight, down_weight, attn_gain, attn_shift, mlp_gain, mlp_shift, out_cotangent):
    micro, seqs, length, width = hidden_in.shape
    count = micro * seqs
    docs = doc_ids.reshape(count, length)
    cosine, sine = jax.vmap(rotary_tables)(docs)
    hidden = hidden_in.reshape(count, length, width).astype(jnp.float32)

    def params(section):
        return tuple((array[section].astype(jnp.float32) for array in (qkv_weight, out_weight, up_weight, down_weight, attn_gain, attn_shift, mlp_gain, mlp_shift)))

    def run(inputs, *weights):
        return layer(inputs, *weights, docs, cosine, sine)
    first_out, first_pull = jax.vjp(run, hidden, *params(0))
    middle = first_out.astype(jnp.bfloat16)
    second_out, second_pull = jax.vjp(run, middle.astype(jnp.float32), *params(1))
    second_grads = second_pull(out_cotangent.reshape(count, length, width).astype(jnp.float32))
    middle_grad = second_grads[0].astype(jnp.bfloat16)
    first_grads = first_pull(middle_grad.astype(jnp.float32))
    shape = (2, micro, seqs, length, width)
    layer_outputs = jnp.stack([middle, second_out.astype(jnp.bfloat16)]).reshape(shape)
    input_grads = jnp.stack([first_grads[0].astype(jnp.bfloat16), middle_grad]).reshape(shape)
    rest = [jnp.stack([first_grads[number], second_grads[number]]) for number in range(1, 9)]
    return (layer_outputs, input_grads, rest[0], rest[1], rest[2], rest[3], rest[4], rest[5], rest[6], rest[7])
```

```python
from functools import partial
import math

import jax
import jax.numpy as jnp
from jax import lax
from jax.experimental import pallas as pl
from jax.experimental.pallas import tpu as pltpu
from jax.sharding import PartitionSpec as P

HEAD_DIM = 64
ROT = 16
EPSILON = 1e-05
NEG_FILL = -1e30
BF16 = jnp.bfloat16
F32 = jnp.float32
TOKENS = 256
LONGEST_DOC = 512


def mm(a, b):
    return lax.dot_general(a, b, (((1,), (0,)), ((), ())), preferred_element_type=F32)


def mm_nt(a, b):
    return lax.dot_general(a, b, (((1,), (1,)), ((), ())), preferred_element_type=F32)


def normalize(full):
    wide = full.astype(F32)
    center = wide - jnp.mean(wide, axis=-1, keepdims=True)
    scale = lax.rsqrt(jnp.mean(center * center, axis=-1, keepdims=True) + EPSILON)
    return (center * scale, scale)


ERFC = (
    0.17087277,
    -0.82215223,
    1.48851587,
    -1.13520398,
    0.27886807,
    -0.18628806,
    0.09678418,
    0.37409196,
    1.00002368,
    -1.26551223,
)


def gelu_and_slope(pre):
    size = jnp.abs(pre) * math.sqrt(0.5)
    t = 1.0 / (1.0 + 0.5 * size)
    poly = jnp.full_like(t, ERFC[0])
    for coefficient in ERFC[1:]:
        poly = poly * t + coefficient
    bell = jnp.exp(-(size * size))
    tail = (0.5 * t) * (bell * jnp.exp(poly))
    below = jnp.where(pre >= 0, 1.0 - tail, tail)
    return (pre * below, below + pre * (bell * (1.0 / math.sqrt(2.0 * math.pi))))


def turn(values, cosine, sine, sign):
    width = values.shape[-1]
    half = ROT // 2
    lane = lax.broadcasted_iota(jnp.int32, values.shape, 1) % HEAD_DIM
    other = jnp.where(
        lane < half, -pltpu.roll(values, width - half, 1), pltpu.roll(values, half, 1)
    )
    return values * cosine + (sign * other) * sine


def rope_tables(docs, starts):
    half = ROT // 2
    lane = jnp.arange(128, dtype=jnp.int32) % HEAD_DIM
    freqs = 10000.0 ** (-2.0 * (lane % half).astype(F32) / ROT)
    position = (jnp.arange(docs.shape[0], dtype=jnp.int32) - starts).astype(F32)
    angles = position[:, None] * freqs[None, :]
    rotated = (lane < ROT)[None, :]
    return (jnp.where(rotated, jnp.cos(angles), 1.0), jnp.where(rotated, jnp.sin(angles), 0.0))


def project_kernel(x, norms, wqkv, wup, cosine, sine, attn_in, feed_in, qkv, active, slope):
    normed, _ = normalize(x[...])
    attn = (normed * norms[0:1] + norms[1:2]).astype(BF16)
    feed = (normed * norms[2:3] + norms[3:4]).astype(BF16)
    attn_in[...] = attn
    feed_in[...] = feed
    width = qkv.shape[2]
    for part in range(3):
        piece = mm(attn, wqkv[:, part * width : (part + 1) * width])
        for pair in range(width // 128):
            lanes = slice(pair * 128, (pair + 1) * 128)
            one = piece[:, lanes]
            if part < 2:
                one = turn(one, cosine[...], sine[...], 1.0)
            qkv[part, :, lanes] = one.astype(BF16)
    hidden = wup.shape[1]
    for start in range(0, hidden, 256):
        lanes = slice(start, start + 256)
        act, der = gelu_and_slope(mm(feed, wup[:, lanes]))
        active[:, lanes] = act.astype(BF16)
        slope[:, lanes] = der.astype(BF16)


def project(x, norms, pack, cosine, sine, heads_width, hidden):
    tokens, model = x.shape
    row = lambda n: pl.BlockSpec((TOKENS, n), lambda i: (i, 0))
    whole = lambda shape, at: pl.BlockSpec(shape, lambda i: at)
    return pl.pallas_call(
        project_kernel,
        grid=(tokens // TOKENS,),
        in_specs=[
            row(model),
            whole((4, model), (0, 0)),
            whole((model, 3 * heads_width), (0, 0)),
            whole((model, hidden), (0, 4 * heads_width // hidden)),
            row(128),
            row(128),
        ],
        out_specs=[
            row(model),
            row(model),
            pl.BlockSpec((3, TOKENS, heads_width), lambda i: (0, i, 0)),
            row(hidden),
            row(hidden),
        ],
        out_shape=[
            jax.ShapeDtypeStruct((tokens, model), BF16),
            jax.ShapeDtypeStruct((tokens, model), BF16),
            jax.ShapeDtypeStruct((3, tokens, heads_width), BF16),
            jax.ShapeDtypeStruct((tokens, hidden), BF16),
            jax.ShapeDtypeStruct((tokens, hidden), BF16),
        ],
        compiler_params=pltpu.CompilerParams(vmem_limit_bytes=48 << 20),
        name="project",
    )(x, norms, pack, pack, cosine, sine)


def window_of(block, size):
    last = (block + 1) * size
    first = max(0, block * size - LONGEST_DOC)
    return (first, last)


def allowed_keys(starts, first, last, block, size):
    shape = (last - first, size)
    key_at = first + lax.broadcasted_iota(jnp.int32, shape, 0)
    query_at = block * size + lax.broadcasted_iota(jnp.int32, shape, 1)
    begins = starts[0:1, block * size : (block + 1) * size]
    return (key_at <= query_at) & (key_at >= begins)


def own_lanes(values, head, factor=None):
    lane = lax.broadcasted_iota(jnp.int32, values.shape, 1) // HEAD_DIM
    if factor is not None:
        values = values * jnp.asarray(factor, values.dtype)
    return jnp.where(lane == head, values, jnp.zeros_like(values))


def attend_kernel(starts, qkv, context, logsum):
    size = TOKENS
    factor = 1.0 / math.sqrt(HEAD_DIM)
    tokens = qkv.shape[1]
    value_t = qkv[2].astype(F32).T.astype(BF16)
    for block in range(tokens // size):
        first, last = window_of(block, size)
        rows = slice(block * size, (block + 1) * size)
        allowed = allowed_keys(starts, first, last, block, size)
        outs = []
        for head in range(128 // HEAD_DIM):
            query = own_lanes(qkv[0, rows], head, factor)
            scores = jnp.where(allowed, mm_nt(qkv[1, first:last], query), NEG_FILL)
            peak = jnp.max(scores, axis=0, keepdims=True)
            raised = jnp.exp(scores - peak)
            total = jnp.sum(raised, axis=0, keepdims=True)
            logsum[0, head : head + 1, rows] = peak + jnp.log(total)
            mixed = mm(value_t[head * HEAD_DIM : (head + 1) * HEAD_DIM, first:last], raised.astype(BF16))
            outs.append(mixed * (1.0 / total))
        context[rows, :] = jnp.concatenate(outs, axis=0).T.astype(BF16)


def attend(starts, qkv):
    _, tokens, width = qkv.shape
    pairs = width // 128
    return pl.pallas_call(
        attend_kernel,
        grid=(pairs,),
        in_specs=[
            pl.BlockSpec((1, tokens), lambda p: (0, 0)),
            pl.BlockSpec((3, tokens, 128), lambda p: (0, 0, p)),
        ],
        out_specs=[
            pl.BlockSpec((tokens, 128), lambda p: (0, p)),
            pl.BlockSpec((1, 128 // HEAD_DIM, tokens), lambda p: (p, 0, 0)),
        ],
        out_shape=[
            jax.ShapeDtypeStruct((tokens, width), BF16),
            jax.ShapeDtypeStruct((pairs, 128 // HEAD_DIM, tokens), F32),
        ],
        compiler_params=pltpu.CompilerParams(vmem_limit_bytes=48 << 20),
        name="attend",
    )(starts, qkv)


def branch_kernel(context, active, wout, wdown, partial_sum):
    partial_sum[...] = (mm_nt(context[...], wout[...]) + mm_nt(active[...], wdown[...])).astype(BF16)


def branch(context, active, pack):
    tokens, width = context.shape
    hidden = active.shape[1]
    model = pack.shape[0]
    row = lambda n: pl.BlockSpec((TOKENS, n), lambda i: (i, 0))
    return pl.pallas_call(
        branch_kernel,
        grid=(tokens // TOKENS,),
        in_specs=[
            row(width),
            row(hidden),
            pl.BlockSpec((model, width), lambda i: (0, 3)),
            pl.BlockSpec((model, hidden), lambda i: (0, 4 * width // hidden + 1)),
        ],
        out_specs=row(model),
        out_shape=jax.ShapeDtypeStruct((tokens, model), BF16),
        compiler_params=pltpu.CompilerParams(vmem_limit_bytes=48 << 20),
        name="branch",
    )(context, active, pack, pack)


def upstream_kernel(upstream, wout, wdown, slope, pre_grad, context_grad):
    grads = upstream[...]
    pre_grad[...] = (mm(grads, wdown[...]) * slope[...].astype(F32)).astype(BF16)
    context_grad[...] = mm(grads, wout[...]).astype(BF16)


def through_branch(upstream, pack, slope, width):
    tokens, model = upstream.shape
    hidden = slope.shape[1]
    row = lambda n: pl.BlockSpec((TOKENS, n), lambda i: (i, 0))
    return pl.pallas_call(
        upstream_kernel,
        grid=(tokens // TOKENS,),
        in_specs=[
            row(model),
            pl.BlockSpec((model, width), lambda i: (0, 3)),
            pl.BlockSpec((model, hidden), lambda i: (0, 4 * width // hidden + 1)),
            row(hidden),
        ],
        out_specs=[row(hidden), row(width)],
        out_shape=[
            jax.ShapeDtypeStruct((tokens, hidden), BF16),
            jax.ShapeDtypeStruct((tokens, width), BF16),
        ],
        compiler_params=pltpu.CompilerParams(vmem_limit_bytes=48 << 20),
        name="through_branch",
    )(upstream, pack, pack, slope)


def attend_back_kernel(starts, qkv, grads, logsum, cosine, sine, out, key_sum, value_sum):
    size = TOKENS
    factor = 1.0 / math.sqrt(HEAD_DIM)
    tokens = qkv.shape[1]
    key_t = qkv[1].astype(F32).T.astype(BF16)
    key_sum[...] = jnp.zeros_like(key_sum)
    value_sum[...] = jnp.zeros_like(value_sum)
    for block in range(tokens // size):
        first, last = window_of(block, size)
        rows = slice(block * size, (block + 1) * size)
        allowed = allowed_keys(starts, first, last, block, size)
        key_part, value_part, query_parts = (0.0, 0.0, [])
        for head in range(128 // HEAD_DIM):
            query = own_lanes(qkv[0, rows], head, factor)
            grad = own_lanes(grads[rows], head)
            scores = jnp.where(allowed, mm_nt(qkv[1, first:last], query), NEG_FILL)
            probs = jnp.exp(scores - logsum[0, head : head + 1, rows])
            probs_grad = mm_nt(qkv[2, first:last], grad)
            inner = jnp.sum(probs_grad * probs, axis=0, keepdims=True)
            score_grad = (probs * (probs_grad - inner)).astype(BF16)
            key_part += mm(score_grad, query)
            value_part += mm(probs.astype(BF16), grad)
            query_parts.append(
                mm(key_t[head * HEAD_DIM : (head + 1) * HEAD_DIM, first:last], score_grad)
            )
        key_sum[first:last] += key_part
        value_sum[first:last] += value_part
        query_grad = jnp.concatenate(query_parts, axis=0).T * factor
        out[0, rows] = turn(query_grad, cosine[rows], sine[rows], -1.0).astype(BF16)
    out[1] = turn(key_sum[...], cosine[...], sine[...], -1.0).astype(BF16)
    out[2] = value_sum[...].astype(BF16)


def attend_back(starts, qkv, context_grad, logsum, cosine, sine):
    _, tokens, width = qkv.shape
    pairs = width // 128
    return pl.pallas_call(
        attend_back_kernel,
        grid=(pairs,),
        in_specs=[
            pl.BlockSpec((1, tokens), lambda p: (0, 0)),
            pl.BlockSpec((3, tokens, 128), lambda p: (0, 0, p)),
            pl.BlockSpec((tokens, 128), lambda p: (0, p)),
            pl.BlockSpec((1, 128 // HEAD_DIM, tokens), lambda p: (p, 0, 0)),
            pl.BlockSpec((tokens, 128), lambda p: (0, 0)),
            pl.BlockSpec((tokens, 128), lambda p: (0, 0)),
        ],
        out_specs=pl.BlockSpec((3, tokens, 128), lambda p: (0, 0, p)),
        out_shape=jax.ShapeDtypeStruct((3, tokens, width), BF16),
        scratch_shapes=[pltpu.VMEM((tokens, 128), F32), pltpu.VMEM((tokens, 128), F32)],
        compiler_params=pltpu.CompilerParams(vmem_limit_bytes=48 << 20),
        name="attend_back",
    )(starts, qkv, context_grad, logsum, cosine, sine)


def inputs_kernel(x, norms, project_grad, pre_grad, wqkv, wup, normed_grad, terms):
    normed, _ = normalize(x[...])
    width = project_grad.shape[2]
    attn = mm_nt(project_grad[0], wqkv[:, :width])
    attn += mm_nt(project_grad[1], wqkv[:, width : 2 * width])
    attn += mm_nt(project_grad[2], wqkv[:, 2 * width :])
    feed = mm_nt(pre_grad[...], wup[...])
    normed_grad[...] = (attn * norms[0:1] + feed * norms[2:3]).astype(BF16)

    @pl.when(pl.program_id(0) == 0)
    def _():
        terms[...] = jnp.zeros_like(terms)

    terms[0:1] += jnp.sum(attn * normed, axis=0, keepdims=True)
    terms[1:2] += jnp.sum(attn, axis=0, keepdims=True)
    terms[2:3] += jnp.sum(feed * normed, axis=0, keepdims=True)
    terms[3:4] += jnp.sum(feed, axis=0, keepdims=True)


def through_inputs(x, norms, project_grad, pre_grad, pack):
    tokens, model = x.shape
    hidden = pre_grad.shape[1]
    width = project_grad.shape[2]
    row = lambda n: pl.BlockSpec((TOKENS, n), lambda i: (i, 0))
    whole = lambda shape, at: pl.BlockSpec(shape, lambda i: at)
    return pl.pallas_call(
        inputs_kernel,
        grid=(tokens // TOKENS,),
        in_specs=[
            row(model),
            whole((4, model), (0, 0)),
            pl.BlockSpec((3, TOKENS, width), lambda i: (0, i, 0)),
            row(hidden),
            whole((model, 3 * width), (0, 0)),
            whole((model, hidden), (0, 4 * width // hidden)),
        ],
        out_specs=[row(model), whole((4, model), (0, 0))],
        out_shape=[
            jax.ShapeDtypeStruct((tokens, model), BF16),
            jax.ShapeDtypeStruct((4, model), F32),
        ],
        compiler_params=pltpu.CompilerParams(vmem_limit_bytes=48 << 20),
        name="through_inputs",
    )(x, norms, project_grad, pre_grad, pack, pack)


def swap(block, axis, bit):
    return lax.ppermute(block, axis, [(i, i ^ bit) for i in range(lax.axis_size(axis))])


def total_of(value):
    for axis in ("section", "col", "row"):
        bit = 1
        while bit < lax.axis_size(axis):
            value = value + swap(value, axis, bit)
            bit *= 2
    return value


def pick(stack, index):
    return lax.dynamic_index_in_dim(stack, index, 0, keepdims=False)


def spread_layer(half):
    sec, col = (lax.axis_index("section"), lax.axis_index("col"))
    rows, width = half.shape
    side = swap(half, "col", 1)
    ahead = swap(half, "col", 2)
    across = jnp.concatenate(
        [swap(side[: rows // 2], "col", 2), swap(ahead[rows // 2 :], "col", 1)], axis=0
    )
    mine = jnp.stack([half, side, ahead, across])
    theirs = swap(mine, "section", 1)
    full = jnp.zeros((4, 2, rows, width), half.dtype)
    for number in range(4):
        full = lax.dynamic_update_slice(full, mine[number][None, None], (col ^ number, sec, 0, 0))
        full = lax.dynamic_update_slice(
            full, theirs[number][None, None], (col ^ number, 1 - sec, 0, 0)
        )
    return full.reshape(8 * rows, width)


def gather_layer_sum(pack):
    sec, col = (lax.axis_index("section"), lax.axis_index("col"))
    model, width = pack.shape
    split = pack.reshape(4, 2, model // 8, width)
    take = lambda which: lax.dynamic_index_in_dim(split, which, 1, keepdims=False)
    sums = (take(sec).astype(F32) + swap(take(1 - sec), "section", 1).astype(F32)).astype(BF16)
    half = model // 16
    upper = [pick(sums, col ^ number)[:half] for number in range(4)]
    lower = [pick(sums, col ^ number)[half:] for number in range(4)]
    first = swap(jnp.stack([upper[1], upper[3]]), "col", 1).astype(F32)
    second = swap(jnp.stack([lower[2], lower[3]]), "col", 2).astype(F32)
    own_upper = upper[0].astype(F32) + first[0]
    own_lower = lower[0].astype(F32) + second[0]
    pass_upper = swap((upper[2].astype(F32) + first[1]).astype(BF16), "col", 2).astype(F32)
    pass_lower = swap((lower[1].astype(F32) + second[1]).astype(BF16), "col", 1).astype(F32)
    return jnp.concatenate([own_upper + pass_upper, own_lower + pass_lower], axis=0)


def gather_tokens(own):
    return lax.all_gather(own, "row", axis=0, tiled=True)


def scatter_tokens(whole):
    return lax.psum_scatter(whole, "row", scatter_dimension=0, tiled=True).astype(F32)


def weight_grads(saved, upstream, pre_grad, project_grad):
    outer = lambda a, b: lax.dot_general(
        a, b, (((0,), (0,)), ((), ())), preferred_element_type=F32
    ).astype(BF16)
    attn_in, feed_in, active, context = saved
    return jnp.concatenate(
        [outer(attn_in, project_grad[part]) for part in range(3)]
        + [outer(upstream, context), outer(feed_in, pre_grad), outer(upstream, active)],
        axis=1,
    )


def fast_shards(
    hidden_in,
    doc_ids,
    qkv_weight,
    out_weight,
    up_weight,
    down_weight,
    attn_gain,
    attn_shift,
    mlp_gain,
    mlp_shift,
    out_cotangent,
):
    sec, row, col = (lax.axis_index("section"), lax.axis_index("row"), lax.axis_index("col"))
    cols = lax.axis_size("col")
    model = hidden_in.shape[3]
    width = qkv_weight.shape[3]
    hidden = up_weight.shape[2]
    block = qkv_weight.shape[1]
    own_tokens = hidden_in.shape[2]
    x_own = pick(hidden_in[:, 0], sec)
    docs = pick(doc_ids[:, 0], sec)
    given = pick(out_cotangent[:, 0], sec)

    own_pack = jnp.concatenate(
        [
            qkv_weight[0].reshape(block, 3 * width),
            out_weight[0].T,
            up_weight[0],
            down_weight[0].T,
        ],
        axis=1,
    )
    kept = lax.dynamic_slice_in_dim(own_pack, sec * (block // 2), block // 2)
    sent = lax.dynamic_slice_in_dim(own_pack, (1 - sec) * (block // 2), block // 2)
    other = swap(sent, "section", 1)
    packs = [
        spread_layer(jnp.where(sec == 0, kept, other)),
        spread_layer(jnp.where(sec == 0, other, kept)),
    ]
    part = attn_gain.shape[1]
    vectors = jnp.stack([attn_gain[0], attn_shift[0], mlp_gain[0], mlp_shift[0]])
    norms = total_of(
        lax.dynamic_update_slice(
            jnp.zeros((2, 4, model), F32), vectors[None], (sec, 0, (row * cols + col) * part)
        )
    )

    starts = jnp.sum((docs[None, :] < docs[:, None]).astype(jnp.int32), axis=1)
    cosine, sine = rope_tables(docs, starts)
    starts = starts[None]

    def forward(x, own, layer):
        attn_in, feed_in, qkv, active, slope = project(
            x, norms[layer], packs[layer], cosine, sine, width, hidden
        )
        context, logsum = attend(starts, qkv)
        result = own.astype(F32) + scatter_tokens(branch(context, active, packs[layer]))
        return (result.astype(BF16), (attn_in, feed_in, active, context), (qkv, slope, logsum))

    def backward(x, own, layer, saved, kept, grads, own_grads):
        qkv, slope, logsum = kept
        pre_grad, context_grad = through_branch(grads, packs[layer], slope, width)
        project_grad = attend_back(starts, qkv, context_grad, logsum, cosine, sine)
        normed_grad, terms = through_inputs(x, norms[layer], project_grad, pre_grad, packs[layer])
        piece = scatter_tokens(normed_grad)
        normed, scale = normalize(own)
        result = own_grads.astype(F32) + scale * (
            piece
            - jnp.mean(piece, axis=-1, keepdims=True)
            - normed * jnp.mean(piece * normed, axis=-1, keepdims=True)
        )
        sums = gather_layer_sum(weight_grads(saved, grads, pre_grad, project_grad))
        return (result.astype(BF16), sums, terms)

    x0 = gather_tokens(x_own)
    y0_own, saved0, kept0 = forward(x0, x_own, 0)
    x1 = gather_tokens(y0_own)
    grads1 = gather_tokens(given)
    y1_own, saved1, kept1 = forward(x1, y0_own, 1)
    dx1_own, sums1, terms1 = backward(x1, y0_own, 1, saved1, kept1, grads1, given)
    grads0 = gather_tokens(dx1_own)
    dx0_own, sums0, terms0 = backward(x0, x_own, 0, saved0, kept0, grads0, dx1_own)

    first = sec == 0
    mine = jnp.where(first, sums0, sums1)
    got = swap(jnp.where(first, sums1, sums0).astype(BF16), "section", 1).astype(F32)
    grad = jnp.concatenate([jnp.where(first, mine, got), jnp.where(first, got, mine)], axis=0)
    terms = pick(total_of(jnp.stack([terms0, terms1])), sec)
    terms = lax.dynamic_slice_in_dim(terms, (row * cols + col) * part, part, 1)

    def by_layer(zero, one):
        away = swap(jnp.where(first, one, zero), "section", 1)
        here = jnp.where(first, zero, one)
        return jnp.stack([jnp.where(first, here, away), jnp.where(first, away, here)])

    return (
        by_layer(y0_own, y1_own)[None, :, None],
        by_layer(dx0_own, dx1_own)[None, :, None],
        grad[:, : 3 * width].reshape(1, block, 3, width),
        grad[:, 3 * width : 4 * width].T[None],
        grad[None, :, 4 * width : 4 * width + hidden],
        grad[:, 4 * width + hidden :].T[None],
        terms[None, 0],
        terms[None, 1],
        terms[None, 2],
        terms[None, 3],
    )


def from_behind(block, axis, distance):
    devices = range(lax.axis_size(axis))
    route = [(i - distance, i) for i in devices if i - distance in devices]
    return lax.ppermute(block, axis, route)


def positions_of(docs):
    length = docs.shape[0]
    index = jnp.arange(length, dtype=jnp.int32)
    starts = jnp.concatenate([jnp.ones((1,), jnp.bool_), docs[1:] != docs[:-1]])
    first = lax.cummax(jnp.where(starts, index, 0), axis=0)
    return index - first


def rotary_tables(docs):
    half = ROT // 2
    freqs = 10000.0 ** (-2.0 * jnp.arange(half, dtype=jnp.float32) / ROT)
    angles = positions_of(docs).astype(jnp.float32)[:, None] * freqs[None, :]
    return (jnp.cos(angles)[:, None, :], jnp.sin(angles)[:, None, :])


def rotate(values, cosine, sine):
    half = ROT // 2
    front = values[..., :half]
    back = values[..., half:ROT]
    return jnp.concatenate(
        [front * cosine - back * sine, back * cosine + front * sine, values[..., ROT:]], axis=-1
    )


def rotate_back(grads, cosine, sine):
    half = ROT // 2
    front = grads[..., :half]
    back = grads[..., half:ROT]
    return jnp.concatenate(
        [front * cosine + back * sine, back * cosine - front * sine, grads[..., ROT:]], axis=-1
    )


def block_mask(docs, start, size):
    rows = start + jnp.arange(size, dtype=jnp.int32)
    cols = jnp.arange(docs.shape[0], dtype=jnp.int32)
    row_docs = lax.dynamic_slice_in_dim(docs, start, size)
    return (row_docs[:, None] == docs[None, :]) & (cols[None, :] <= rows[:, None])


def block_scores(query, key, docs, start, block):
    factor = 1.0 / math.sqrt(query.shape[2])
    rows = lax.dynamic_slice_in_dim(query, start, block)
    scores = jnp.einsum("qhd,khd->hqk", rows, key, preferred_element_type=jnp.float32) * factor
    allowed = block_mask(docs, start, block)[None]
    return (rows, jnp.where(allowed, scores, NEG_FILL))


def attend_forward(query, key, value, docs):
    length, heads, width = query.shape
    block = min(512, length)

    def one_block(number):
        start = number * block
        rows, scores = block_scores(query, key, docs, start, block)
        peak = jnp.max(scores, axis=-1, keepdims=True)
        raised = jnp.exp(scores - peak)
        total = jnp.sum(raised, axis=-1, keepdims=True)
        probs = (raised / total).astype(jnp.bfloat16)
        context = jnp.einsum(
            "hqk,khd->qhd", probs, value, preferred_element_type=jnp.float32
        ).astype(jnp.bfloat16)
        return (context, (peak + jnp.log(total))[..., 0])

    context, logsum = lax.map(one_block, jnp.arange(length // block, dtype=jnp.int32))
    return (context.reshape(length, heads, width), logsum)


def attend_backward(query, key, value, docs, logsum, context_grad):
    length, heads, width = query.shape
    block = min(512, length)
    factor = 1.0 / math.sqrt(width)

    def one_block(carry, inputs):
        key_grad, value_grad = carry
        number, block_logsum = inputs
        start = number * block
        rows, scores = block_scores(query, key, docs, start, block)
        rows_grad = lax.dynamic_slice_in_dim(context_grad, start, block)
        probs_full = jnp.exp(scores - block_logsum[:, :, None])
        probs = probs_full.astype(jnp.bfloat16)
        context = jnp.einsum(
            "hqk,khd->qhd", probs, value, preferred_element_type=jnp.float32
        ).astype(jnp.bfloat16)
        probs_grad = jnp.einsum(
            "qhd,khd->hqk", rows_grad, value, preferred_element_type=jnp.float32
        )
        inner = jnp.sum(probs_grad * probs_full, axis=-1, keepdims=True)
        score_grad = (probs_full * (probs_grad - inner)).astype(jnp.bfloat16)
        query_grad = (
            jnp.einsum("hqk,khd->qhd", score_grad, key, preferred_element_type=jnp.float32) * factor
        )
        key_grad = (
            key_grad
            + jnp.einsum("hqk,qhd->khd", score_grad, rows, preferred_element_type=jnp.float32)
            * factor
        )
        value_grad = value_grad + jnp.einsum(
            "hqk,qhd->khd", probs, rows_grad, preferred_element_type=jnp.float32
        )
        return ((key_grad, value_grad), (context, query_grad))

    zeros = jnp.zeros((length, heads, width), jnp.float32)
    numbers = jnp.arange(length // block, dtype=jnp.int32)
    (key_grad, value_grad), (context, query_grad) = lax.scan(
        one_block, (zeros, zeros), (numbers, logsum)
    )
    return (
        context.reshape(length, heads * width),
        query_grad.reshape(length, heads, width),
        key_grad,
        value_grad,
    )


def gather_features(shard):
    return lax.all_gather(shard, "row", axis=0, tiled=True)


def recompute_inputs(full, docs, norms, weights):
    gain_a, shift_a, gain_m, shift_m = norms
    qkv_full = weights[0]
    normed, scale = normalize(full)
    attn_in = (normed * gain_a + shift_a).astype(jnp.bfloat16)
    feed_in = (normed * gain_m + shift_m).astype(jnp.bfloat16)
    length = full.shape[0]
    heads_here = qkv_full.shape[2] // HEAD_DIM
    project = jnp.einsum("td,dke->tke", attn_in, qkv_full, preferred_element_type=jnp.float32)
    cosine, sine = rotary_tables(docs)
    query = rotate(project[:, 0].reshape(length, heads_here, HEAD_DIM), cosine, sine).astype(
        jnp.bfloat16
    )
    key = rotate(project[:, 1].reshape(length, heads_here, HEAD_DIM), cosine, sine).astype(
        jnp.bfloat16
    )
    value = project[:, 2].reshape(length, heads_here, HEAD_DIM).astype(jnp.bfloat16)
    pre = jnp.dot(feed_in, weights[2], preferred_element_type=jnp.float32)
    return (normed, scale, attn_in, feed_in, query, key, value, pre, cosine, sine)


def layer_forward(shard, docs, full, norms, weights):
    normed, scale, attn_in, feed_in, query, key, value, pre, cosine, sine = recompute_inputs(
        full, docs, norms, weights
    )
    length = full.shape[0]
    context, logsum = attend_forward(query, key, value, docs)
    active = jax.nn.gelu(pre, approximate=False).astype(jnp.bfloat16)
    partial_sum = jnp.dot(
        context.reshape(length, -1), weights[1], preferred_element_type=jnp.float32
    )
    partial_sum = partial_sum + jnp.dot(active, weights[3], preferred_element_type=jnp.float32)
    branch = lax.psum_scatter(
        partial_sum.astype(jnp.bfloat16), "row", scatter_dimension=0, tiled=True
    ).astype(jnp.float32)
    return ((shard.astype(jnp.float32) + branch).astype(jnp.bfloat16), logsum)


def layer_backward(docs, full, logsum, upstream, norms, weights):
    gain_a, shift_a, gain_m, shift_m = norms
    qkv_full, out_full, up_full, down_full = weights
    normed, scale, attn_in, feed_in, query, key, value, pre, cosine, sine = recompute_inputs(
        full, docs, norms, weights
    )
    length = full.shape[0]
    heads_here = query.shape[1]
    active = jax.nn.gelu(pre, approximate=False).astype(jnp.bfloat16)
    upstream_full = lax.all_gather(upstream, "row", axis=0, tiled=True)
    down_part = jnp.einsum("tf,td->fd", active, upstream_full, preferred_element_type=jnp.float32)
    act_grad = jnp.einsum("td,fd->tf", upstream_full, down_full, preferred_element_type=jnp.float32)
    pre_grad = jax.vjp(partial(jax.nn.gelu, approximate=False), pre)[1](act_grad)[0].astype(
        jnp.bfloat16
    )
    up_part = jnp.einsum("td,tf->df", feed_in, pre_grad, preferred_element_type=jnp.float32)
    feed_grad = jnp.einsum("tf,df->td", pre_grad, up_full, preferred_element_type=jnp.float32)
    context_grad = jnp.einsum(
        "td,ed->te", upstream_full, out_full, preferred_element_type=jnp.float32
    ).astype(jnp.bfloat16)
    context_grad = context_grad.reshape(length, heads_here, HEAD_DIM)
    context, query_grad, key_grad, value_grad = attend_backward(
        query, key, value, docs, logsum, context_grad
    )
    out_part = jnp.einsum("te,td->ed", context, upstream_full, preferred_element_type=jnp.float32)
    project_grad = jnp.stack(
        [
            rotate_back(query_grad, cosine, sine).reshape(length, -1),
            rotate_back(key_grad, cosine, sine).reshape(length, -1),
            value_grad.reshape(length, -1),
        ],
        axis=1,
    ).astype(jnp.bfloat16)
    qkv_part = jnp.einsum("td,tke->dke", attn_in, project_grad, preferred_element_type=jnp.float32)
    attn_grad = jnp.einsum(
        "tke,dke->td", project_grad, qkv_full, preferred_element_type=jnp.float32
    )
    own_rows = upstream.shape[0]
    offset = lax.axis_index("row") * own_rows
    normed_part = lax.dynamic_slice_in_dim(normed, offset, own_rows, 0)
    scale_part = lax.dynamic_slice_in_dim(scale, offset, own_rows, 0)
    attn_piece, feed_piece = (
        lax.psum_scatter(
            attn_grad.astype(jnp.bfloat16), "row", scatter_dimension=0, tiled=True
        ).astype(jnp.float32),
        lax.psum_scatter(
            feed_grad.astype(jnp.bfloat16), "row", scatter_dimension=0, tiled=True
        ).astype(jnp.float32),
    )
    normed_grad = attn_piece * gain_a + feed_piece * gain_m
    gain_terms = (
        jnp.sum(attn_piece * normed_part, axis=0),
        jnp.sum(attn_piece, axis=0),
        jnp.sum(feed_piece * normed_part, axis=0),
        jnp.sum(feed_piece, axis=0),
    )
    row_sum = jnp.sum(normed_grad, axis=-1)
    cross_sum = jnp.sum(normed_grad * normed_part, axis=-1)
    count = full.shape[1]
    input_grad = upstream.astype(jnp.float32) + scale_part * (
        normed_grad - row_sum[:, None] / count - normed_part * cross_sum[:, None] / count
    )
    return (input_grad, (qkv_part, out_part, up_part, down_part), gain_terms)


def general_shards(
    hidden_in,
    doc_ids,
    qkv_weight,
    out_weight,
    up_weight,
    down_weight,
    attn_gain,
    attn_shift,
    mlp_gain,
    mlp_shift,
    out_cotangent,
):
    micro = hidden_in.shape[0]
    first_section = lax.axis_index("section") == 0
    norms = (
        lax.all_gather(attn_gain[0], ("row", "col"), axis=0, tiled=True),
        lax.all_gather(attn_shift[0], ("row", "col"), axis=0, tiled=True),
        lax.all_gather(mlp_gain[0], ("row", "col"), axis=0, tiled=True),
        lax.all_gather(mlp_shift[0], ("row", "col"), axis=0, tiled=True),
    )
    weights = (
        lax.all_gather(qkv_weight[0], "col", axis=0, tiled=True),
        lax.all_gather(out_weight[0], "col", axis=1, tiled=True),
        lax.all_gather(up_weight[0], "col", axis=0, tiled=True),
        lax.all_gather(down_weight[0], "col", axis=1, tiled=True),
    )
    received = jnp.zeros_like(hidden_in[0, 0])
    tick_inputs, tick_docs, tick_fulls, tick_outputs, tick_logsums = ([], [], [], [], [])
    for tick in range(micro + 1):
        own = hidden_in[min(tick, micro - 1), 0]
        shard = jnp.where(first_section, own, received)
        docs = jnp.where(
            first_section, doc_ids[min(tick, micro - 1), 0], doc_ids[max(tick - 1, 0), 0]
        )
        full = gather_features(shard)
        result, logsum = layer_forward(shard, docs, full, norms, weights)
        tick_inputs.append(shard)
        tick_docs.append(docs)
        tick_fulls.append(full)
        tick_outputs.append(result)
        tick_logsums.append(logsum)
        if tick < micro:
            received = from_behind(result, "section", 1)
    outputs = jnp.stack(
        [
            jnp.where(first_section, tick_outputs[number], tick_outputs[number + 1])
            for number in range(micro)
        ]
    )
    received = jnp.zeros_like(hidden_in[0, 0])
    matrix_totals = None
    gain_totals = None
    tick_grads = []
    for tick in range(micro + 1):
        early = max(tick - 1, 0)
        later = min(tick + 1, micro)
        if tick < micro:
            given = out_cotangent[tick, 0]
        else:
            given = jnp.zeros_like(out_cotangent[0, 0])
        upstream = jnp.where(first_section, received, given)
        shard = jnp.where(first_section, tick_inputs[early], tick_inputs[later])
        docs = jnp.where(first_section, tick_docs[early], tick_docs[later])
        logsum = jnp.where(first_section, tick_logsums[early], tick_logsums[later])
        full = gather_features(shard)
        input_grad, matrices, gain_terms = layer_backward(
            docs, full, logsum, upstream, norms, weights
        )
        if matrix_totals is None:
            matrix_totals = matrices
            gain_totals = gain_terms
        else:
            matrix_totals = jax.tree.map(jnp.add, matrix_totals, matrices)
            gain_totals = jax.tree.map(jnp.add, gain_totals, gain_terms)
        grad_low = input_grad.astype(jnp.bfloat16)
        tick_grads.append(grad_low)
        if tick < micro:
            received = from_behind(grad_low, "section", -1)
    grads_in = jnp.stack(
        [
            jnp.where(first_section, tick_grads[number + 1], tick_grads[number])
            for number in range(micro)
        ]
    )
    qkv_sum, out_sum, up_sum, down_sum = matrix_totals
    gain_a_sum, shift_a_sum, gain_m_sum, shift_m_sum = gain_totals
    qkv_total, out_total, up_total, down_total = (
        lax.psum_scatter(
            qkv_sum.astype(jnp.bfloat16), "col", scatter_dimension=0, tiled=True
        ).astype(jnp.float32),
        lax.psum_scatter(
            out_sum.astype(jnp.bfloat16), "col", scatter_dimension=1, tiled=True
        ).astype(jnp.float32),
        lax.psum_scatter(
            up_sum.astype(jnp.bfloat16), "col", scatter_dimension=0, tiled=True
        ).astype(jnp.float32),
        lax.psum_scatter(
            down_sum.astype(jnp.bfloat16), "col", scatter_dimension=1, tiled=True
        ).astype(jnp.float32),
    )
    gain_a_total, shift_a_total, gain_m_total, shift_m_total = (
        lax.psum_scatter(gain_a_sum, ("row", "col"), scatter_dimension=0, tiled=True),
        lax.psum_scatter(shift_a_sum, ("row", "col"), scatter_dimension=0, tiled=True),
        lax.psum_scatter(gain_m_sum, ("row", "col"), scatter_dimension=0, tiled=True),
        lax.psum_scatter(shift_m_sum, ("row", "col"), scatter_dimension=0, tiled=True),
    )
    return (
        outputs[None, :, None],
        grads_in[None, :, None],
        qkv_total[None],
        out_total[None],
        up_total[None],
        down_total[None],
        gain_a_total[None],
        shift_a_total[None],
        gain_m_total[None],
        shift_m_total[None],
    )


def shards(*arrays):
    hidden_in, qkv_weight, up_weight = (arrays[0], arrays[2], arrays[4])
    micro, seqs, own_tokens, model = hidden_in.shape
    width, hidden = (qkv_weight.shape[3], up_weight.shape[2])
    fits = (
        (lax.axis_size("section"), micro, lax.axis_size("col"), seqs) == (2, 2, 4, 1)
        and own_tokens == TOKENS
        and width % 128 == 0
        and 4 * width == hidden
    )
    return fast_shards(*arrays) if fits else general_shards(*arrays)


def solution(mesh):
    placed = (
        P(None, "col", "row", None),
        P(None, "col", None),
        P("section", "col", None, "row"),
        P("section", "row", "col"),
        P("section", "col", "row"),
        P("section", "row", "col"),
        P("section", ("row", "col")),
        P("section", ("row", "col")),
        P("section", ("row", "col")),
        P("section", ("row", "col")),
        P(None, "col", "row", None),
    )
    return jax.shard_map(
        shards,
        mesh=mesh,
        in_specs=placed,
        out_specs=(
            P("section", None, "col", "row", None),
            P("section", None, "col", "row", None),
            P("section", "col", None, "row"),
            P("section", "row", "col"),
            P("section", "col", "row"),
            P("section", "row", "col"),
            P("section", ("row", "col")),
            P("section", ("row", "col")),
            P("section", ("row", "col")),
            P("section", ("row", "col")),
        ),
        check_vma=False,
    )
```

```python
from functools import partial
import math

import jax
import jax.numpy as jnp
from jax import lax
from jax.experimental import pallas as pl
from jax.experimental.pallas import tpu as pltpu
from jax.sharding import PartitionSpec as P

HEAD_DIM = 64
ROT = 16
EPSILON = 1e-05
NEG_FILL = -1e30
BF16 = jnp.bfloat16
F32 = jnp.float32
TOKENS = 256
LONGEST_DOC = 512


def mm(a, b):
    return lax.dot_general(a, b, (((1,), (0,)), ((), ())), preferred_element_type=F32)


def mm_nt(a, b):
    return lax.dot_general(a, b, (((1,), (1,)), ((), ())), preferred_element_type=F32)


def normalize(full):
    wide = full.astype(F32)
    center = wide - jnp.mean(wide, axis=-1, keepdims=True)
    scale = lax.rsqrt(jnp.mean(center * center, axis=-1, keepdims=True) + EPSILON)
    return (center * scale, scale)


ERFC = (
    0.17087277,
    -0.82215223,
    1.48851587,
    -1.13520398,
    0.27886807,
    -0.18628806,
    0.09678418,
    0.37409196,
    1.00002368,
    -1.26551223,
)


def gelu_and_slope(pre):
    size = jnp.abs(pre) * math.sqrt(0.5)
    t = 1.0 / (1.0 + 0.5 * size)
    poly = jnp.full_like(t, ERFC[0])
    for coefficient in ERFC[1:]:
        poly = poly * t + coefficient
    bell = jnp.exp(-(size * size))
    tail = (0.5 * t) * (bell * jnp.exp(poly))
    below = jnp.where(pre >= 0, 1.0 - tail, tail)
    return (pre * below, below + pre * (bell * (1.0 / math.sqrt(2.0 * math.pi))))


def turn(values, cosine, sine, sign):
    width = values.shape[-1]
    half = ROT // 2
    lane = lax.broadcasted_iota(jnp.int32, values.shape, 1) % HEAD_DIM
    other = jnp.where(
        lane < half, -pltpu.roll(values, width - half, 1), pltpu.roll(values, half, 1)
    )
    return values * cosine + (sign * other) * sine


def rope_tables(docs, starts):
    half = ROT // 2
    lane = jnp.arange(128, dtype=jnp.int32) % HEAD_DIM
    freqs = 10000.0 ** (-2.0 * (lane % half).astype(F32) / ROT)
    position = (jnp.arange(docs.shape[0], dtype=jnp.int32) - starts).astype(F32)
    angles = position[:, None] * freqs[None, :]
    rotated = (lane < ROT)[None, :]
    return (jnp.where(rotated, jnp.cos(angles), 1.0), jnp.where(rotated, jnp.sin(angles), 0.0))


def params(mib=24):
    return pltpu.CompilerParams(vmem_limit_bytes=mib << 20)


def chunk_call(body, name, index, outs, inputs, kept=()):
    given = len(inputs)

    def kernel(number, *refs):
        body(number, *refs[:given], *refs[given + len(kept) :])

    spec = lambda block, at: pl.BlockSpec(block, lambda i, number: at(number[0]))
    return pl.pallas_call(
        kernel,
        grid_spec=pltpu.PrefetchScalarGridSpec(
            num_scalar_prefetch=1,
            grid=(1,),
            in_specs=[spec(block, at) for _, block, at in inputs]
            + [pl.BlockSpec(memory_space=pl.ANY) for _ in kept],
            out_specs=[spec(block, at) for _, _, block, at in outs],
        ),
        out_shape=[jax.ShapeDtypeStruct(shape, dtype) for shape, dtype, _, _ in outs],
        input_output_aliases={1 + given + i: i for i in range(len(kept))},
        compiler_params=params(),
        name=name,
    )(index.reshape(1).astype(jnp.int32), *[array for array, _, _ in inputs], *kept)


HERE = lambda i: (0, 0)
ROWS = lambda i: (i, 0)
LANES = lambda i: (0, i)


def added(refs):
    whole = refs[0][...]
    for ref in refs[1:]:
        whole = whole + ref[...]
    return whole


def project_body(ways, number, *refs):
    norms, wqkv, wup, cosine, sine, attn_in, feed_in, qkv, value_t, active, slope = refs[ways:]
    normed, _ = normalize(added(refs[:ways]))
    attn = (normed * norms[0:1] + norms[1:2]).astype(BF16)
    feed = (normed * norms[2:3] + norms[3:4]).astype(BF16)
    attn_in[...] = attn
    feed_in[...] = feed
    width = qkv.shape[2]
    for part in range(3):
        piece = mm(attn, wqkv[:, part * width : (part + 1) * width])
        for pair in range(width // 128):
            lanes = slice(pair * 128, (pair + 1) * 128)
            one = piece[:, lanes]
            if part < 2:
                one = turn(one, cosine[...], sine[...], 1.0)
            else:
                value_t[lanes, :] = one.T.astype(BF16)
            qkv[part, :, lanes] = one.astype(BF16)
    hidden = wup.shape[1]
    for start in range(0, hidden, 256):
        lanes = slice(start, start + 256)
        act, der = gelu_and_slope(mm(feed, wup[:, lanes]))
        active[:, lanes] = act.astype(BF16)
        slope[:, lanes] = der.astype(BF16)


def project(chunk, index, tokens, norms, pack, tables, width, hidden, kept):
    model = pack.shape[0]
    return chunk_call(
        partial(project_body, len(chunk)),
        "project",
        index,
        [
            ((tokens, model), BF16, (TOKENS, model), ROWS),
            ((tokens, model), BF16, (TOKENS, model), ROWS),
            ((3, tokens, width), BF16, (3, TOKENS, width), lambda i: (0, i, 0)),
            ((width, tokens), BF16, (width, TOKENS), LANES),
            ((tokens, hidden), BF16, (TOKENS, hidden), ROWS),
            ((tokens, hidden), BF16, (TOKENS, hidden), ROWS),
        ],
        [(way, (TOKENS, model), HERE) for way in chunk]
        + [
            (norms, (4, model), HERE),
            (pack, (model, 3 * width), HERE),
            (pack, (model, hidden), lambda i: (0, 1)),
            (tables[0], (TOKENS, 128), ROWS),
            (tables[1], (TOKENS, 128), ROWS),
        ],
        kept,
    )


def own_lanes(values, head, factor=None):
    lane = lax.broadcasted_iota(jnp.int32, values.shape, 1) // HEAD_DIM
    if factor is not None:
        values = values * jnp.asarray(factor, values.dtype)
    return jnp.where(lane == head, values, jnp.zeros_like(values))


def attend_body(number, starts, qkv, value_t, active, wout, wdown, context, logsum, partial_sum):
    index = number[0]
    tokens, width = (qkv.shape[1], qkv.shape[2])
    reach = min(tokens, TOKENS + LONGEST_DOC)
    first = pl.multiple_of(jnp.maximum(index * TOKENS + TOKENS - reach, 0), TOKENS)
    at = pl.multiple_of(index * TOKENS, TOKENS)
    key_at = first + lax.broadcasted_iota(jnp.int32, (reach, TOKENS), 0)
    query_at = at + lax.broadcasted_iota(jnp.int32, (reach, TOKENS), 1)
    allowed = (key_at <= query_at) & (key_at >= starts[0:1, pl.ds(at, TOKENS)])
    outs, sums = ([], [])
    for pair in range(width // 128):
        lanes = slice(pair * 128, (pair + 1) * 128)
        keys = qkv[1, pl.ds(first, reach), lanes]
        queries = qkv[0, pl.ds(at, TOKENS), lanes]
        for head in range(128 // HEAD_DIM):
            query = own_lanes(queries, head, 1.0 / math.sqrt(HEAD_DIM))
            scores = jnp.where(allowed, mm_nt(keys, query), NEG_FILL)
            peak = jnp.max(scores, axis=0, keepdims=True)
            raised = jnp.exp(scores - peak)
            total = jnp.sum(raised, axis=0, keepdims=True)
            sums.append(peak + jnp.log(total))
            begin = pair * 128 + head * HEAD_DIM
            values = value_t[begin : begin + HEAD_DIM, pl.ds(first, reach)]
            outs.append(mm(values, raised.astype(BF16)) * (1.0 / total))
    mixed = jnp.concatenate(outs, axis=0).T.astype(BF16)
    context[...] = mixed
    for head, one in enumerate(sums):
        logsum[head : head + 1, :] = one
    partial_sum[...] = (mm_nt(mixed, wout[...]) + mm_nt(active[...], wdown[...])).astype(BF16)


def attend(index, starts, qkv, value_t, active, pack, kept):
    _, tokens, width = qkv.shape
    hidden = active.shape[1]
    model = pack.shape[0]
    heads = width // HEAD_DIM
    return chunk_call(
        attend_body,
        "attend",
        index,
        [
            ((tokens, width), BF16, (TOKENS, width), ROWS),
            ((heads, tokens), F32, (heads, TOKENS), LANES),
            ((TOKENS, model), BF16, (TOKENS, model), HERE),
        ],
        [
            (starts, (1, tokens), HERE),
            (qkv, (3, tokens, width), lambda i: (0, 0, 0)),
            (value_t, (width, tokens), HERE),
            (active, (TOKENS, hidden), ROWS),
            (pack, (model, width), lambda i: (0, 3)),
            (pack, (model, hidden), lambda i: (0, 2)),
        ],
        kept,
    )


def through_branch_body(ways, number, *refs):
    wout, wdown, slope, pre_grad, context_grad, copied = refs[ways:]
    grads = added(refs[:ways])
    copied[...] = grads
    pre_grad[...] = (mm(grads, wdown[...]) * slope[...].astype(F32)).astype(BF16)
    context_grad[...] = mm(grads, wout[...]).astype(BF16)


def through_branch(chunk, index, pack, slope, width, kept):
    tokens, hidden = slope.shape
    model = pack.shape[0]
    return chunk_call(
        partial(through_branch_body, len(chunk)),
        "through_branch",
        index,
        [
            ((tokens, hidden), BF16, (TOKENS, hidden), ROWS),
            ((tokens, width), BF16, (TOKENS, width), ROWS),
            ((tokens, model), BF16, (TOKENS, model), ROWS),
        ],
        [(way, (TOKENS, model), HERE) for way in chunk]
        + [
            (pack, (model, width), lambda i: (0, 3)),
            (pack, (model, hidden), lambda i: (0, 2)),
            (slope, (TOKENS, hidden), ROWS),
        ],
        kept,
    )


def window_of(block, size):
    return (max(0, block * size - LONGEST_DOC), (block + 1) * size)


def attend_back_kernel(starts, qkv, grads, logsum, cosine, sine, out, key_sum, value_sum):
    size = TOKENS
    factor = 1.0 / math.sqrt(HEAD_DIM)
    tokens = qkv.shape[1]
    heads = 128 // HEAD_DIM
    key_t = qkv[1].astype(F32).T.astype(BF16)
    key_sum[...] = jnp.zeros_like(key_sum)
    value_sum[...] = jnp.zeros_like(value_sum)
    for block in range(tokens // size):
        first, last = window_of(block, size)
        rows = slice(block * size, (block + 1) * size)
        shape = (last - first, size)
        key_at = first + lax.broadcasted_iota(jnp.int32, shape, 0)
        query_at = block * size + lax.broadcasted_iota(jnp.int32, shape, 1)
        allowed = (key_at <= query_at) & (key_at >= starts[0:1, rows])
        key_part, value_part, query_parts = (0.0, 0.0, [])
        for head in range(heads):
            query = own_lanes(qkv[0, rows], head, factor)
            grad = own_lanes(grads[rows], head)
            scores = jnp.where(allowed, mm_nt(qkv[1, first:last], query), NEG_FILL)
            probs = jnp.exp(scores - logsum[0, head : head + 1, rows])
            probs_grad = mm_nt(qkv[2, first:last], grad)
            inner = jnp.sum(probs_grad * probs, axis=0, keepdims=True)
            score_grad = (probs * (probs_grad - inner)).astype(BF16)
            key_part += mm(score_grad, query)
            value_part += mm(probs.astype(BF16), grad)
            query_parts.append(
                mm(key_t[head * HEAD_DIM : (head + 1) * HEAD_DIM, first:last], score_grad)
            )
        key_sum[first:last] += key_part
        value_sum[first:last] += value_part
        query_grad = jnp.concatenate(query_parts, axis=0).T * factor
        out[0, rows] = turn(query_grad, cosine[rows], sine[rows], -1.0).astype(BF16)
    out[1] = turn(key_sum[...], cosine[...], sine[...], -1.0).astype(BF16)
    out[2] = value_sum[...].astype(BF16)


def attend_back(starts, qkv, context_grad, logsum, tables):
    _, tokens, width = qkv.shape
    pairs = width // 128
    heads = 128 // HEAD_DIM
    return pl.pallas_call(
        attend_back_kernel,
        grid=(pairs,),
        in_specs=[
            pl.BlockSpec((1, tokens), lambda p: (0, 0)),
            pl.BlockSpec((3, tokens, 128), lambda p: (0, 0, p)),
            pl.BlockSpec((tokens, 128), lambda p: (0, p)),
            pl.BlockSpec((1, heads, tokens), lambda p: (p, 0, 0)),
            pl.BlockSpec((tokens, 128), lambda p: (0, 0)),
            pl.BlockSpec((tokens, 128), lambda p: (0, 0)),
        ],
        out_specs=pl.BlockSpec((3, tokens, 128), lambda p: (0, 0, p)),
        out_shape=jax.ShapeDtypeStruct((3, tokens, width), BF16),
        scratch_shapes=[pltpu.VMEM((tokens, 128), F32), pltpu.VMEM((tokens, 128), F32)],
        compiler_params=params(),
        name="attend_back",
    )(starts, qkv, context_grad, logsum.reshape(pairs, heads, tokens), *tables)


def through_inputs_body(ways, number, *refs):
    norms, project_grad, pre_grad, wqkv, wup, normed_grad, terms = refs[ways:]
    normed, _ = normalize(added(refs[:ways]))
    width = project_grad.shape[2]
    attn = mm_nt(project_grad[0], wqkv[:, :width])
    attn += mm_nt(project_grad[1], wqkv[:, width : 2 * width])
    attn += mm_nt(project_grad[2], wqkv[:, 2 * width :])
    feed = mm_nt(pre_grad[...], wup[...])
    normed_grad[...] = (attn * norms[0:1] + feed * norms[2:3]).astype(BF16)
    terms[0:1] = jnp.sum(attn * normed, axis=0, keepdims=True)
    terms[1:2] = jnp.sum(attn, axis=0, keepdims=True)
    terms[2:3] = jnp.sum(feed * normed, axis=0, keepdims=True)
    terms[3:4] = jnp.sum(feed, axis=0, keepdims=True)


def through_inputs(chunk, index, norms, project_grad, pre_grad, pack):
    model = pack.shape[0]
    hidden = pre_grad.shape[1]
    width = project_grad.shape[2]
    return chunk_call(
        partial(through_inputs_body, len(chunk)),
        "through_inputs",
        index,
        [
            ((TOKENS, model), BF16, (TOKENS, model), HERE),
            ((4, model), F32, (4, model), HERE),
        ],
        [(way, (TOKENS, model), HERE) for way in chunk]
        + [
            (norms, (4, model), HERE),
            (project_grad, (3, TOKENS, width), lambda i: (0, i, 0)),
            (pre_grad, (TOKENS, hidden), ROWS),
            (pack, (model, 3 * width), HERE),
            (pack, (model, hidden), lambda i: (0, 1)),
        ],
    )


def outer_kernel(blocks, attn_in, feed_in, upstream, project_grad, context, pre_grad, active, out):
    step = pl.program_id(0)

    def fill(left, right):
        for number in range(4):
            lanes = pl.ds(pl.multiple_of(blocks[number] * 128, 128), 128)
            out[number] = lax.dot_general(
                left[:, lanes], right, (((0,), (0,)), ((), ())), preferred_element_type=F32
            ).astype(BF16)

    @pl.when(step < 3)
    def _():
        fill(attn_in, project_grad[0])

    @pl.when(step == 3)
    def _():
        fill(upstream, context[...])

    @pl.when((step >= 4) & (step < 8))
    def _():
        fill(feed_in, pre_grad[...])

    @pl.when(step >= 8)
    def _():
        fill(upstream, active[...])


def weight_grads(blocks, saved, upstream, pre_grad, project_grad):
    attn_in, feed_in, active, context = saved
    tokens, model = attn_in.shape
    width = context.shape[1]
    steps = 4 + 2 * active.shape[1] // width
    whole = pl.BlockSpec((tokens, model), lambda j, blocks: (0, 0))
    return pl.pallas_call(
        outer_kernel,
        grid_spec=pltpu.PrefetchScalarGridSpec(
            num_scalar_prefetch=1,
            grid=(steps,),
            in_specs=[
                whole,
                whole,
                whole,
                pl.BlockSpec((1, tokens, width), lambda j, blocks: (jnp.minimum(j, 2), 0, 0)),
                pl.BlockSpec((tokens, width), lambda j, blocks: (0, 0)),
                pl.BlockSpec((tokens, width), lambda j, blocks: (0, jnp.clip(j - 4, 0, 3))),
                pl.BlockSpec((tokens, width), lambda j, blocks: (0, jnp.clip(j - 8, 0, 3))),
            ],
            out_specs=pl.BlockSpec((4, model // 8, width), lambda j, blocks: (0, 0, j)),
        ),
        out_shape=jax.ShapeDtypeStruct((4, model // 8, steps * width), BF16),
        compiler_params=params(32),
        name="weight_grads",
    )(blocks.astype(jnp.int32), attn_in, feed_in, upstream, project_grad, context, pre_grad, active)


def fold_kernel(kept, came, side, ahead, rest):
    half = kept.shape[1] // 2
    both = (kept[...].astype(F32) + came[...].astype(F32)).astype(BF16)
    side[0] = both[1, :half]
    side[1] = both[3, :half]
    ahead[0] = both[2, half:]
    ahead[1] = both[3, half:]
    rest[0] = both[0, :half]
    rest[1] = both[2, :half]
    rest[2] = both[0, half:]
    rest[3] = both[1, half:]


def fold(kept, came):
    _, rows, width = kept.shape
    step = width // 6
    block = lambda n, r: pl.BlockSpec((n, r, step), lambda j: (0, 0, j))
    shape = lambda n: jax.ShapeDtypeStruct((n, rows // 2, width), BF16)
    return pl.pallas_call(
        fold_kernel,
        grid=(6,),
        in_specs=[block(4, rows), block(4, rows)],
        out_specs=[block(2, rows // 2), block(2, rows // 2), block(4, rows // 2)],
        out_shape=[shape(2), shape(2), shape(4)],
        compiler_params=params(),
        name="fold",
    )(kept, came)


def assemble_kernel(place, *refs):
    pieces, whole = (refs[:-1], refs[-1])
    rows = pieces[0].shape[0]
    for order, piece in enumerate(pieces):
        core, number, part = (order // 8, (order % 8) // 2, order % 2)
        at = ((place[1] ^ number) * 2 + (place[0] ^ core)) * (2 * rows) + part * rows
        whole[pl.ds(pl.multiple_of(at, rows), rows), :] = piece[...]


def assemble(place, pieces):
    rows, width = pieces[0].shape
    step = width // 6
    return pl.pallas_call(
        assemble_kernel,
        grid_spec=pltpu.PrefetchScalarGridSpec(
            num_scalar_prefetch=1,
            grid=(6,),
            in_specs=[pl.BlockSpec((rows, step), lambda j, place: (0, j)) for _ in pieces],
            out_specs=pl.BlockSpec((len(pieces) * rows, step), lambda j, place: (0, j)),
        ),
        out_shape=jax.ShapeDtypeStruct((len(pieces) * rows, width), BF16),
        compiler_params=params(),
        name="assemble",
    )(place.astype(jnp.int32), *pieces)


def unpack_kernel(place, upper, lower, came, qkv, out, up, down):
    width, hidden = (out.shape[0], up.shape[1])
    half = came.shape[0]
    own = jnp.concatenate([upper[...], lower[...]], axis=0)
    for core, block in ((place[0], own), (1 - place[0], came[...].astype(F32))):
        rows = pl.ds(pl.multiple_of(core * half, half), half)
        qkv[rows, :] = block[:, : 3 * width]
        out[:, rows] = block[:, 3 * width : 4 * width].T
        up[rows, :] = block[:, 4 * width : 4 * width + hidden]
        down[:, rows] = block[:, 4 * width + hidden :].T


def unpack(sec, upper, lower, came, width, hidden):
    half = came.shape[0]
    shapes = [(2 * half, 3 * width), (width, 2 * half), (2 * half, hidden), (hidden, 2 * half)]
    return pl.pallas_call(
        unpack_kernel,
        grid_spec=pltpu.PrefetchScalarGridSpec(
            num_scalar_prefetch=1,
            grid=(1,),
            in_specs=[
                pl.BlockSpec(array.shape, lambda i, place: (0, 0)) for array in (upper, lower, came)
            ],
            out_specs=[pl.BlockSpec(shape, lambda i, place: (0, 0)) for shape in shapes],
        ),
        out_shape=[jax.ShapeDtypeStruct(shape, F32) for shape in shapes],
        compiler_params=params(32),
        name="unpack",
    )(sec.reshape(1).astype(jnp.int32), upper, lower, came)


def swap(block, axis, bit):
    return lax.ppermute(block, axis, [(i, i ^ bit) for i in range(lax.axis_size(axis))])


def after(values, *earlier):
    flat, tree = jax.tree.flatten(values)
    held = lax.optimization_barrier((*flat, *earlier))
    return jax.tree.unflatten(tree, held[: len(flat)])


def total_of(value):
    for axis in ("section", "col", "row"):
        bit = 1
        while bit < lax.axis_size(axis):
            value = value + swap(value, axis, bit)
            bit *= 2
    return value


def pick(stack, index):
    return lax.dynamic_index_in_dim(stack, index, 0, keepdims=False)


def spread_layer(parts, meanwhile):
    upper, lower = parts
    side = [swap(part, "col", 1) for part in parts]
    ahead = [swap(part, "col", 2) for part in parts]
    if meanwhile is not None:
        side, ahead = after((side, ahead), meanwhile)
    across = [swap(side[0], "col", 2), swap(ahead[1], "col", 1)]
    mine = [*parts, *side, *ahead, *across]
    theirs = [swap(piece, "section", 1) for piece in mine]
    return (mine + theirs, across)


def sum_layer(sec, col, saved, upstream, pre_grad, project_grad):
    order = col ^ jnp.arange(4, dtype=jnp.int32)
    leaving = weight_grads(order * 2 + 1 - sec, saved, upstream, pre_grad, project_grad)
    came = swap(leaving, "section", 1)
    kept = weight_grads(order * 2 + sec, saved, upstream, pre_grad, project_grad)
    side, ahead, rest = fold(kept, came)
    first = swap(side, "col", 1)
    second = swap(ahead, "col", 2)
    add = lambda a, b: a.astype(F32) + b.astype(F32)
    upper = swap(add(rest[1], first[1]).astype(BF16), "col", 2)
    lower = swap(add(rest[3], second[1]).astype(BF16), "col", 1)
    return (add(add(rest[0], first[0]), upper), add(add(rest[2], second[0]), lower))


def along_row(block, pairs):
    return lax.ppermute(block, "row", pairs)


ONE_OVER = [(0, 1), (1, 0), (2, 3), (3, 2)]
TWO_OVER = [(0, 2), (2, 0), (1, 3), (3, 1)]
MIDDLE = [(1, 2), (2, 1)]
OUTWARD = [(1, 0), (2, 3)]
INWARD = [(0, 1), (3, 2)]


def gather_tokens(own):
    far = along_row(own, TWO_OVER)
    near = along_row(own, ONE_OVER)
    middle = along_row(own, MIDDLE)
    passed = along_row(far, OUTWARD)
    return [(own,), (near,), (far,), (middle, passed)]


def scatter_tokens(chunk_of):
    last = chunk_of(3)
    passed = along_row(last, INWARD)
    middle = along_row(last, MIDDLE)
    far = chunk_of(2)
    near = along_row(chunk_of(1), ONE_OVER)
    far = along_row((far.astype(F32) + passed.astype(F32)).astype(BF16), TWO_OVER)
    own = chunk_of(0)
    return (own.astype(F32) + near.astype(F32)) + (middle.astype(F32) + far.astype(F32))


def fast_shards(
    hidden_in,
    doc_ids,
    qkv_weight,
    out_weight,
    up_weight,
    down_weight,
    attn_gain,
    attn_shift,
    mlp_gain,
    mlp_shift,
    out_cotangent,
):
    sec, row, col = (lax.axis_index("section"), lax.axis_index("row"), lax.axis_index("col"))
    cols, rows = (lax.axis_size("col"), lax.axis_size("row"))
    model = hidden_in.shape[3]
    tokens = doc_ids.shape[2]
    width = qkv_weight.shape[3]
    hidden = up_weight.shape[2]
    block = qkv_weight.shape[1]
    first = sec == 0
    x_own = pick(hidden_in[:, 0], sec)
    docs = pick(doc_ids[:, 0], sec)
    given = pick(out_cotangent[:, 0], sec)

    own_pack = jnp.concatenate(
        [
            qkv_weight[0].reshape(block, 3 * width),
            out_weight[0].T,
            up_weight[0],
            down_weight[0].T,
        ],
        axis=1,
    )
    quarter = block // 4
    part_of = lambda core, part: lax.dynamic_slice_in_dim(
        own_pack, core * (block // 2) + part * quarter, quarter
    )
    own_parts = [part_of(sec, part) for part in range(2)]
    other_parts = [swap(part_of(1 - sec, part), "section", 1) for part in range(2)]
    parts0 = [jnp.where(first, a, b) for a, b in zip(own_parts, other_parts)]
    parts1 = [jnp.where(first, b, a) for a, b in zip(own_parts, other_parts)]
    share = attn_gain.shape[1]
    vectors = jnp.stack([attn_gain[0], attn_shift[0], mlp_gain[0], mlp_shift[0]])
    norms = total_of(
        lax.dynamic_update_slice(
            jnp.zeros((2, 4, model), F32), vectors[None], (sec, 0, (row * cols + col) * share)
        )
    )
    chunks_x0 = gather_tokens(x_own)
    pieces0, across0 = spread_layer(parts0, norms)
    pieces1, _ = spread_layer(after(parts1, *across0), None)
    place = jnp.stack([sec, col])
    packs = [assemble(place, pieces0), assemble(place, pieces1)]

    starts = jnp.sum((docs[None, :] < docs[:, None]).astype(jnp.int32), axis=1)
    tables = rope_tables(docs, starts)
    starts = starts[None]

    def forward(chunks, own, layer):
        kept = ()
        for number, chunk in enumerate(chunks):
            kept = project(
                chunk, row ^ number, tokens, norms[layer], packs[layer], tables, width, hidden, kept
            )
        attn_in, feed_in, qkv, value_t, active, slope = kept
        results = []

        def chunk_of(number):
            *now, share_of = attend(
                row ^ number, starts, qkv, value_t, active, packs[layer], tuple(results)
            )
            results[:] = now
            return share_of

        result = own.astype(F32) + scatter_tokens(chunk_of)
        context, logsum = results
        return (result.astype(BF16), (attn_in, feed_in, active, context), (qkv, slope, logsum))

    def backward(chunks, own, layer, saved, held, chunks_grads, own_grads):
        qkv, slope, logsum = held
        kept = ()
        for number, chunk in enumerate(chunks_grads):
            kept = through_branch(chunk, row ^ number, packs[layer], slope, width, kept)
        pre_grad, context_grad, grads = kept
        project_grad = attend_back(starts, qkv, context_grad, logsum, tables)
        terms, pieces = ([], [])

        def chunk_of(number):
            piece, term = through_inputs(
                chunks[number], row ^ number, norms[layer], project_grad, pre_grad, packs[layer]
            )
            terms.append(term)
            pieces.append(piece)
            return piece

        total = scatter_tokens(chunk_of)
        normed, scale = normalize(own)
        result = own_grads.astype(F32) + scale * (
            total
            - jnp.mean(total, axis=-1, keepdims=True)
            - normed * jnp.mean(total * normed, axis=-1, keepdims=True)
        )
        pre_grad, project_grad = after((pre_grad, project_grad), *pieces)
        sums = sum_layer(sec, col, saved, grads, pre_grad, project_grad)
        return (result.astype(BF16), sums, sum(terms))

    y0_own, saved0, held0 = forward(chunks_x0, x_own, 0)
    chunks_x1 = gather_tokens(y0_own)
    chunks_g1 = gather_tokens(after(given, chunks_x0[3][1]))
    y1_own, saved1, held1 = forward(chunks_x1, y0_own, 1)
    dx1_own, sums1, terms1 = backward(chunks_x1, y0_own, 1, saved1, held1, chunks_g1, given)
    chunks_g0 = gather_tokens(dx1_own)
    dx0_own, sums0, terms0 = backward(chunks_x0, x_own, 0, saved0, held0, chunks_g0, dx1_own)

    choose = lambda here, there: jnp.where(first, here, there)
    leaving = jnp.concatenate([choose(b, a) for a, b in zip(sums0, sums1)]).astype(BF16)
    upper, lower = [choose(a, b) for a, b in zip(sums0, sums1)]
    qkv_grad, out_grad, up_grad, down_grad = unpack(
        sec, upper, lower, swap(leaving, "section", 1), width, hidden
    )
    terms = pick(total_of(jnp.stack([terms0, terms1])), sec)
    terms = lax.dynamic_slice_in_dim(terms, (row * cols + col) * share, share, 1)

    def by_layer(zero, one):
        away = swap(choose(one, zero), "section", 1)
        here = choose(zero, one)
        return jnp.stack([choose(here, away), choose(away, here)])

    return (
        by_layer(y0_own, y1_own)[None, :, None],
        by_layer(dx0_own, dx1_own)[None, :, None],
        qkv_grad.reshape(1, block, 3, width),
        out_grad[None],
        up_grad[None],
        down_grad[None],
        terms[None, 0],
        terms[None, 1],
        terms[None, 2],
        terms[None, 3],
    )


def from_behind(block, axis, distance):
    devices = range(lax.axis_size(axis))
    route = [(i - distance, i) for i in devices if i - distance in devices]
    return lax.ppermute(block, axis, route)


def positions_of(docs):
    length = docs.shape[0]
    index = jnp.arange(length, dtype=jnp.int32)
    starts = jnp.concatenate([jnp.ones((1,), jnp.bool_), docs[1:] != docs[:-1]])
    first = lax.cummax(jnp.where(starts, index, 0), axis=0)
    return index - first


def rotary_tables(docs):
    half = ROT // 2
    freqs = 10000.0 ** (-2.0 * jnp.arange(half, dtype=jnp.float32) / ROT)
    angles = positions_of(docs).astype(jnp.float32)[:, None] * freqs[None, :]
    return (jnp.cos(angles)[:, None, :], jnp.sin(angles)[:, None, :])


def rotate(values, cosine, sine):
    half = ROT // 2
    front = values[..., :half]
    back = values[..., half:ROT]
    return jnp.concatenate(
        [front * cosine - back * sine, back * cosine + front * sine, values[..., ROT:]], axis=-1
    )


def rotate_back(grads, cosine, sine):
    half = ROT // 2
    front = grads[..., :half]
    back = grads[..., half:ROT]
    return jnp.concatenate(
        [front * cosine + back * sine, back * cosine - front * sine, grads[..., ROT:]], axis=-1
    )


def block_mask(docs, start, size):
    rows = start + jnp.arange(size, dtype=jnp.int32)
    cols = jnp.arange(docs.shape[0], dtype=jnp.int32)
    row_docs = lax.dynamic_slice_in_dim(docs, start, size)
    return (row_docs[:, None] == docs[None, :]) & (cols[None, :] <= rows[:, None])


def block_scores(query, key, docs, start, block):
    factor = 1.0 / math.sqrt(query.shape[2])
    rows = lax.dynamic_slice_in_dim(query, start, block)
    scores = jnp.einsum("qhd,khd->hqk", rows, key, preferred_element_type=jnp.float32) * factor
    allowed = block_mask(docs, start, block)[None]
    return (rows, jnp.where(allowed, scores, NEG_FILL))


def attend_forward(query, key, value, docs):
    length, heads, width = query.shape
    block = min(512, length)

    def one_block(number):
        start = number * block
        rows, scores = block_scores(query, key, docs, start, block)
        peak = jnp.max(scores, axis=-1, keepdims=True)
        raised = jnp.exp(scores - peak)
        total = jnp.sum(raised, axis=-1, keepdims=True)
        probs = (raised / total).astype(jnp.bfloat16)
        context = jnp.einsum(
            "hqk,khd->qhd", probs, value, preferred_element_type=jnp.float32
        ).astype(jnp.bfloat16)
        return (context, (peak + jnp.log(total))[..., 0])

    context, logsum = lax.map(one_block, jnp.arange(length // block, dtype=jnp.int32))
    return (context.reshape(length, heads, width), logsum)


def attend_backward(query, key, value, docs, logsum, context_grad):
    length, heads, width = query.shape
    block = min(512, length)
    factor = 1.0 / math.sqrt(width)

    def one_block(carry, inputs):
        key_grad, value_grad = carry
        number, block_logsum = inputs
        start = number * block
        rows, scores = block_scores(query, key, docs, start, block)
        rows_grad = lax.dynamic_slice_in_dim(context_grad, start, block)
        probs_full = jnp.exp(scores - block_logsum[:, :, None])
        probs = probs_full.astype(jnp.bfloat16)
        context = jnp.einsum(
            "hqk,khd->qhd", probs, value, preferred_element_type=jnp.float32
        ).astype(jnp.bfloat16)
        probs_grad = jnp.einsum(
            "qhd,khd->hqk", rows_grad, value, preferred_element_type=jnp.float32
        )
        inner = jnp.sum(probs_grad * probs_full, axis=-1, keepdims=True)
        score_grad = (probs_full * (probs_grad - inner)).astype(jnp.bfloat16)
        query_grad = (
            jnp.einsum("hqk,khd->qhd", score_grad, key, preferred_element_type=jnp.float32) * factor
        )
        key_grad = (
            key_grad
            + jnp.einsum("hqk,qhd->khd", score_grad, rows, preferred_element_type=jnp.float32)
            * factor
        )
        value_grad = value_grad + jnp.einsum(
            "hqk,qhd->khd", probs, rows_grad, preferred_element_type=jnp.float32
        )
        return ((key_grad, value_grad), (context, query_grad))

    zeros = jnp.zeros((length, heads, width), jnp.float32)
    numbers = jnp.arange(length // block, dtype=jnp.int32)
    (key_grad, value_grad), (context, query_grad) = lax.scan(
        one_block, (zeros, zeros), (numbers, logsum)
    )
    return (
        context.reshape(length, heads * width),
        query_grad.reshape(length, heads, width),
        key_grad,
        value_grad,
    )


def gather_features(shard):
    return lax.all_gather(shard, "row", axis=0, tiled=True)


def recompute_inputs(full, docs, norms, weights):
    gain_a, shift_a, gain_m, shift_m = norms
    qkv_full = weights[0]
    normed, scale = normalize(full)
    attn_in = (normed * gain_a + shift_a).astype(jnp.bfloat16)
    feed_in = (normed * gain_m + shift_m).astype(jnp.bfloat16)
    length = full.shape[0]
    heads_here = qkv_full.shape[2] // HEAD_DIM
    project = jnp.einsum("td,dke->tke", attn_in, qkv_full, preferred_element_type=jnp.float32)
    cosine, sine = rotary_tables(docs)
    query = rotate(project[:, 0].reshape(length, heads_here, HEAD_DIM), cosine, sine).astype(
        jnp.bfloat16
    )
    key = rotate(project[:, 1].reshape(length, heads_here, HEAD_DIM), cosine, sine).astype(
        jnp.bfloat16
    )
    value = project[:, 2].reshape(length, heads_here, HEAD_DIM).astype(jnp.bfloat16)
    pre = jnp.dot(feed_in, weights[2], preferred_element_type=jnp.float32)
    return (normed, scale, attn_in, feed_in, query, key, value, pre, cosine, sine)


def layer_forward(shard, docs, full, norms, weights):
    normed, scale, attn_in, feed_in, query, key, value, pre, cosine, sine = recompute_inputs(
        full, docs, norms, weights
    )
    length = full.shape[0]
    context, logsum = attend_forward(query, key, value, docs)
    active = jax.nn.gelu(pre, approximate=False).astype(jnp.bfloat16)
    partial_sum = jnp.dot(
        context.reshape(length, -1), weights[1], preferred_element_type=jnp.float32
    )
    partial_sum = partial_sum + jnp.dot(active, weights[3], preferred_element_type=jnp.float32)
    branch = lax.psum_scatter(
        partial_sum.astype(jnp.bfloat16), "row", scatter_dimension=0, tiled=True
    ).astype(jnp.float32)
    return ((shard.astype(jnp.float32) + branch).astype(jnp.bfloat16), logsum)


def layer_backward(docs, full, logsum, upstream, norms, weights):
    gain_a, shift_a, gain_m, shift_m = norms
    qkv_full, out_full, up_full, down_full = weights
    normed, scale, attn_in, feed_in, query, key, value, pre, cosine, sine = recompute_inputs(
        full, docs, norms, weights
    )
    length = full.shape[0]
    heads_here = query.shape[1]
    active = jax.nn.gelu(pre, approximate=False).astype(jnp.bfloat16)
    upstream_full = lax.all_gather(upstream, "row", axis=0, tiled=True)
    down_part = jnp.einsum("tf,td->fd", active, upstream_full, preferred_element_type=jnp.float32)
    act_grad = jnp.einsum("td,fd->tf", upstream_full, down_full, preferred_element_type=jnp.float32)
    pre_grad = jax.vjp(partial(jax.nn.gelu, approximate=False), pre)[1](act_grad)[0].astype(
        jnp.bfloat16
    )
    up_part = jnp.einsum("td,tf->df", feed_in, pre_grad, preferred_element_type=jnp.float32)
    feed_grad = jnp.einsum("tf,df->td", pre_grad, up_full, preferred_element_type=jnp.float32)
    context_grad = jnp.einsum(
        "td,ed->te", upstream_full, out_full, preferred_element_type=jnp.float32
    ).astype(jnp.bfloat16)
    context_grad = context_grad.reshape(length, heads_here, HEAD_DIM)
    context, query_grad, key_grad, value_grad = attend_backward(
        query, key, value, docs, logsum, context_grad
    )
    out_part = jnp.einsum("te,td->ed", context, upstream_full, preferred_element_type=jnp.float32)
    project_grad = jnp.stack(
        [
            rotate_back(query_grad, cosine, sine).reshape(length, -1),
            rotate_back(key_grad, cosine, sine).reshape(length, -1),
            value_grad.reshape(length, -1),
        ],
        axis=1,
    ).astype(jnp.bfloat16)
    qkv_part = jnp.einsum("td,tke->dke", attn_in, project_grad, preferred_element_type=jnp.float32)
    attn_grad = jnp.einsum(
        "tke,dke->td", project_grad, qkv_full, preferred_element_type=jnp.float32
    )
    own_rows = upstream.shape[0]
    offset = lax.axis_index("row") * own_rows
    normed_part = lax.dynamic_slice_in_dim(normed, offset, own_rows, 0)
    scale_part = lax.dynamic_slice_in_dim(scale, offset, own_rows, 0)
    attn_piece, feed_piece = (
        lax.psum_scatter(
            attn_grad.astype(jnp.bfloat16), "row", scatter_dimension=0, tiled=True
        ).astype(jnp.float32),
        lax.psum_scatter(
            feed_grad.astype(jnp.bfloat16), "row", scatter_dimension=0, tiled=True
        ).astype(jnp.float32),
    )
    normed_grad = attn_piece * gain_a + feed_piece * gain_m
    gain_terms = (
        jnp.sum(attn_piece * normed_part, axis=0),
        jnp.sum(attn_piece, axis=0),
        jnp.sum(feed_piece * normed_part, axis=0),
        jnp.sum(feed_piece, axis=0),
    )
    row_sum = jnp.sum(normed_grad, axis=-1)
    cross_sum = jnp.sum(normed_grad * normed_part, axis=-1)
    count = full.shape[1]
    input_grad = upstream.astype(jnp.float32) + scale_part * (
        normed_grad - row_sum[:, None] / count - normed_part * cross_sum[:, None] / count
    )
    return (input_grad, (qkv_part, out_part, up_part, down_part), gain_terms)


def general_shards(
    hidden_in,
    doc_ids,
    qkv_weight,
    out_weight,
    up_weight,
    down_weight,
    attn_gain,
    attn_shift,
    mlp_gain,
    mlp_shift,
    out_cotangent,
):
    micro = hidden_in.shape[0]
    first_section = lax.axis_index("section") == 0
    norms = (
        lax.all_gather(attn_gain[0], ("row", "col"), axis=0, tiled=True),
        lax.all_gather(attn_shift[0], ("row", "col"), axis=0, tiled=True),
        lax.all_gather(mlp_gain[0], ("row", "col"), axis=0, tiled=True),
        lax.all_gather(mlp_shift[0], ("row", "col"), axis=0, tiled=True),
    )
    weights = (
        lax.all_gather(qkv_weight[0], "col", axis=0, tiled=True),
        lax.all_gather(out_weight[0], "col", axis=1, tiled=True),
        lax.all_gather(up_weight[0], "col", axis=0, tiled=True),
        lax.all_gather(down_weight[0], "col", axis=1, tiled=True),
    )
    received = jnp.zeros_like(hidden_in[0, 0])
    tick_inputs, tick_docs, tick_fulls, tick_outputs, tick_logsums = ([], [], [], [], [])
    for tick in range(micro + 1):
        own = hidden_in[min(tick, micro - 1), 0]
        shard = jnp.where(first_section, own, received)
        docs = jnp.where(
            first_section, doc_ids[min(tick, micro - 1), 0], doc_ids[max(tick - 1, 0), 0]
        )
        full = gather_features(shard)
        result, logsum = layer_forward(shard, docs, full, norms, weights)
        tick_inputs.append(shard)
        tick_docs.append(docs)
        tick_fulls.append(full)
        tick_outputs.append(result)
        tick_logsums.append(logsum)
        if tick < micro:
            received = from_behind(result, "section", 1)
    outputs = jnp.stack(
        [
            jnp.where(first_section, tick_outputs[number], tick_outputs[number + 1])
            for number in range(micro)
        ]
    )
    received = jnp.zeros_like(hidden_in[0, 0])
    matrix_totals = None
    gain_totals = None
    tick_grads = []
    for tick in range(micro + 1):
        early = max(tick - 1, 0)
        later = min(tick + 1, micro)
        if tick < micro:
            given = out_cotangent[tick, 0]
        else:
            given = jnp.zeros_like(out_cotangent[0, 0])
        upstream = jnp.where(first_section, received, given)
        shard = jnp.where(first_section, tick_inputs[early], tick_inputs[later])
        docs = jnp.where(first_section, tick_docs[early], tick_docs[later])
        logsum = jnp.where(first_section, tick_logsums[early], tick_logsums[later])
        full = gather_features(shard)
        input_grad, matrices, gain_terms = layer_backward(
            docs, full, logsum, upstream, norms, weights
        )
        if matrix_totals is None:
            matrix_totals = matrices
            gain_totals = gain_terms
        else:
            matrix_totals = jax.tree.map(jnp.add, matrix_totals, matrices)
            gain_totals = jax.tree.map(jnp.add, gain_totals, gain_terms)
        grad_low = input_grad.astype(jnp.bfloat16)
        tick_grads.append(grad_low)
        if tick < micro:
            received = from_behind(grad_low, "section", -1)
    grads_in = jnp.stack(
        [
            jnp.where(first_section, tick_grads[number + 1], tick_grads[number])
            for number in range(micro)
        ]
    )
    qkv_sum, out_sum, up_sum, down_sum = matrix_totals
    gain_a_sum, shift_a_sum, gain_m_sum, shift_m_sum = gain_totals
    qkv_total, out_total, up_total, down_total = (
        lax.psum_scatter(
            qkv_sum.astype(jnp.bfloat16), "col", scatter_dimension=0, tiled=True
        ).astype(jnp.float32),
        lax.psum_scatter(
            out_sum.astype(jnp.bfloat16), "col", scatter_dimension=1, tiled=True
        ).astype(jnp.float32),
        lax.psum_scatter(
            up_sum.astype(jnp.bfloat16), "col", scatter_dimension=0, tiled=True
        ).astype(jnp.float32),
        lax.psum_scatter(
            down_sum.astype(jnp.bfloat16), "col", scatter_dimension=1, tiled=True
        ).astype(jnp.float32),
    )
    gain_a_total, shift_a_total, gain_m_total, shift_m_total = (
        lax.psum_scatter(gain_a_sum, ("row", "col"), scatter_dimension=0, tiled=True),
        lax.psum_scatter(shift_a_sum, ("row", "col"), scatter_dimension=0, tiled=True),
        lax.psum_scatter(gain_m_sum, ("row", "col"), scatter_dimension=0, tiled=True),
        lax.psum_scatter(shift_m_sum, ("row", "col"), scatter_dimension=0, tiled=True),
    )
    return (
        outputs[None, :, None],
        grads_in[None, :, None],
        qkv_total[None],
        out_total[None],
        up_total[None],
        down_total[None],
        gain_a_total[None],
        shift_a_total[None],
        gain_m_total[None],
        shift_m_total[None],
    )


def shards(*arrays):
    hidden_in, qkv_weight, up_weight = (arrays[0], arrays[2], arrays[4])
    micro, seqs, own_tokens, model = hidden_in.shape
    width, hidden = (qkv_weight.shape[3], up_weight.shape[2])
    sizes = tuple(lax.axis_size(axis) for axis in ("section", "row", "col"))
    fits = (
        sizes == (2, 4, 4) and (micro, seqs) == (2, 1)
        and own_tokens == TOKENS
        and width % 128 == 0
        and 4 * width == hidden
    )
    return fast_shards(*arrays) if fits else general_shards(*arrays)


def solution(mesh):
    placed = (
        P(None, "col", "row", None),
        P(None, "col", None),
        P("section", "col", None, "row"),
        P("section", "row", "col"),
        P("section", "col", "row"),
        P("section", "row", "col"),
        P("section", ("row", "col")),
        P("section", ("row", "col")),
        P("section", ("row", "col")),
        P("section", ("row", "col")),
        P(None, "col", "row", None),
    )
    return jax.shard_map(
        shards,
        mesh=mesh,
        in_specs=placed,
        out_specs=(
            P("section", None, "col", "row", None),
            P("section", None, "col", "row", None),
            P("section", "col", None, "row"),
            P("section", "row", "col"),
            P("section", "col", "row"),
            P("section", "row", "col"),
            P("section", ("row", "col")),
            P("section", ("row", "col")),
            P("section", ("row", "col")),
            P("section", ("row", "col")),
        ),
        check_vma=False,
    )
```

```python
from functools import partial
import math

import jax
import jax.numpy as jnp
from jax import lax
from jax.experimental import pallas as pl
from jax.experimental.pallas import tpu as pltpu
from jax.sharding import PartitionSpec as P

HEAD_DIM = 64
ROT = 16
EPSILON = 1e-05
NEG_FILL = -1e30
BF16 = jnp.bfloat16
F32 = jnp.float32
TOKENS = 256
LONGEST_DOC = 512


def mm(a, b):
    return lax.dot_general(a, b, (((1,), (0,)), ((), ())), preferred_element_type=F32)


def mm_nt(a, b):
    return lax.dot_general(a, b, (((1,), (1,)), ((), ())), preferred_element_type=F32)


def normalize(full):
    wide = full.astype(F32)
    center = wide - jnp.mean(wide, axis=-1, keepdims=True)
    scale = lax.rsqrt(jnp.mean(center * center, axis=-1, keepdims=True) + EPSILON)
    return (center * scale, scale)


ERFC = (
    0.17087277,
    -0.82215223,
    1.48851587,
    -1.13520398,
    0.27886807,
    -0.18628806,
    0.09678418,
    0.37409196,
    1.00002368,
    -1.26551223,
)


def gelu_and_slope(pre):
    size = jnp.abs(pre) * math.sqrt(0.5)
    t = 1.0 / (1.0 + 0.5 * size)
    poly = jnp.full_like(t, ERFC[0])
    for coefficient in ERFC[1:]:
        poly = poly * t + coefficient
    bell = jnp.exp(-(size * size))
    tail = (0.5 * t) * (bell * jnp.exp(poly))
    below = jnp.where(pre >= 0, 1.0 - tail, tail)
    return (pre * below, below + pre * (bell * (1.0 / math.sqrt(2.0 * math.pi))))


def turn(values, cosine, sine, sign):
    width = values.shape[-1]
    half = ROT // 2
    lane = lax.broadcasted_iota(jnp.int32, values.shape, 1) % HEAD_DIM
    other = jnp.where(
        lane < half, -pltpu.roll(values, width - half, 1), pltpu.roll(values, half, 1)
    )
    return values * cosine + (sign * other) * sine


def rope_tables(docs, starts):
    half = ROT // 2
    lane = jnp.arange(128, dtype=jnp.int32) % HEAD_DIM
    freqs = 10000.0 ** (-2.0 * (lane % half).astype(F32) / ROT)
    position = (jnp.arange(docs.shape[0], dtype=jnp.int32) - starts).astype(F32)
    angles = position[:, None] * freqs[None, :]
    rotated = (lane < ROT)[None, :]
    return (jnp.where(rotated, jnp.cos(angles), 1.0), jnp.where(rotated, jnp.sin(angles), 0.0))


def params(mib=24):
    return pltpu.CompilerParams(vmem_limit_bytes=mib << 20)


def chunk_call(body, name, index, outs, inputs, kept=(), place=None):
    given = len(inputs)
    number = index.reshape(1).astype(jnp.int32)
    if place is not None:
        number = jnp.concatenate([number, place])

    def kernel(number, *refs):
        body(number, *refs[:given], *refs[given + len(kept) :])

    spec = lambda block, at: pl.BlockSpec(block, lambda i, number: at(number[0]))
    return pl.pallas_call(
        kernel,
        grid_spec=pltpu.PrefetchScalarGridSpec(
            num_scalar_prefetch=1,
            grid=(1,),
            in_specs=[spec(block, at) for _, block, at in inputs]
            + [pl.BlockSpec(memory_space=pl.ANY) for _ in kept],
            out_specs=[spec(block, at) for _, _, block, at in outs],
        ),
        out_shape=[jax.ShapeDtypeStruct(shape, dtype) for shape, dtype, _, _ in outs],
        input_output_aliases={1 + given + i: i for i in range(len(kept))},
        compiler_params=params(),
        name=name,
    )(number, *[array for array, _, _ in inputs], *kept)


HERE = lambda i: (0, 0)
ROWS = lambda i: (i, 0)
LANES = lambda i: (0, i)


def added(refs):
    whole = refs[0][...]
    for ref in refs[1:]:
        whole = whole + ref[...]
    return whole


def keep_by_owner(kept, place, values):
    blocks = values.shape[1] // 128
    for block in range(blocks):
        at = (place[0] ^ (block % 2)) * (blocks // 2) + (place[1] ^ (block // 2))
        lanes = pl.ds(pl.multiple_of(at * 128, 128), 128)
        kept[:, lanes] = values[:, block * 128 : (block + 1) * 128]


def project_body(ways, number, *refs):
    norms, wqkv, wup, cosine, sine, attn_in, feed_in, qkv, value_t, active, slope = refs[ways:]
    normed, _ = normalize(added(refs[:ways]))
    attn = (normed * norms[0:1] + norms[1:2]).astype(BF16)
    feed = (normed * norms[2:3] + norms[3:4]).astype(BF16)
    place = (number[1], number[2])
    keep_by_owner(attn_in, place, attn)
    keep_by_owner(feed_in, place, feed)
    width = qkv.shape[2]
    for part in range(3):
        piece = mm(attn, wqkv[:, part * width : (part + 1) * width])
        for pair in range(width // 128):
            lanes = slice(pair * 128, (pair + 1) * 128)
            one = piece[:, lanes]
            if part < 2:
                one = turn(one, cosine[...], sine[...], 1.0)
            else:
                value_t[lanes, :] = one.T.astype(BF16)
            qkv[part, :, lanes] = one.astype(BF16)
    hidden = wup.shape[1]
    for start in range(0, hidden, 256):
        lanes = slice(start, start + 256)
        act, der = gelu_and_slope(mm(feed, wup[:, lanes]))
        active[:, lanes] = act.astype(BF16)
        slope[:, lanes] = der.astype(BF16)


def project(chunk, index, place, tokens, norms, pack, tables, width, hidden, kept):
    model = pack.shape[0]
    return chunk_call(
        partial(project_body, len(chunk)),
        "project",
        index,
        [
            ((tokens, model), BF16, (TOKENS, model), ROWS),
            ((tokens, model), BF16, (TOKENS, model), ROWS),
            ((3, tokens, width), BF16, (3, TOKENS, width), lambda i: (0, i, 0)),
            ((width, tokens), BF16, (width, TOKENS), LANES),
            ((tokens, hidden), BF16, (TOKENS, hidden), ROWS),
            ((tokens, hidden), BF16, (TOKENS, hidden), ROWS),
        ],
        [(way, (TOKENS, model), HERE) for way in chunk]
        + [
            (norms, (4, model), HERE),
            (pack, (model, 3 * width), HERE),
            (pack, (model, hidden), lambda i: (0, 1)),
            (tables[0], (TOKENS, 128), ROWS),
            (tables[1], (TOKENS, 128), ROWS),
        ],
        kept,
        place,
    )


def own_lanes(values, head, factor=None):
    lane = lax.broadcasted_iota(jnp.int32, values.shape, 1) // HEAD_DIM
    if factor is not None:
        values = values * jnp.asarray(factor, values.dtype)
    return jnp.where(lane == head, values, jnp.zeros_like(values))


def attend_body(number, starts, qkv, value_t, active, wout, wdown, context, logsum, partial_sum):
    index = number[0]
    tokens, width = (qkv.shape[1], qkv.shape[2])
    reach = min(tokens, TOKENS + LONGEST_DOC)
    first = pl.multiple_of(jnp.maximum(index * TOKENS + TOKENS - reach, 0), TOKENS)
    at = pl.multiple_of(index * TOKENS, TOKENS)
    key_at = first + lax.broadcasted_iota(jnp.int32, (reach, TOKENS), 0)
    query_at = at + lax.broadcasted_iota(jnp.int32, (reach, TOKENS), 1)
    allowed = (key_at <= query_at) & (key_at >= starts[0:1, pl.ds(at, TOKENS)])
    outs, sums = ([], [])
    for pair in range(width // 128):
        lanes = slice(pair * 128, (pair + 1) * 128)
        keys = qkv[1, pl.ds(first, reach), lanes]
        queries = qkv[0, pl.ds(at, TOKENS), lanes]
        for head in range(128 // HEAD_DIM):
            query = own_lanes(queries, head, 1.0 / math.sqrt(HEAD_DIM))
            scores = jnp.where(allowed, mm_nt(keys, query), NEG_FILL)
            peak = jnp.max(scores, axis=0, keepdims=True)
            raised = jnp.exp(scores - peak)
            total = jnp.sum(raised, axis=0, keepdims=True)
            sums.append(peak + jnp.log(total))
            begin = pair * 128 + head * HEAD_DIM
            values = value_t[begin : begin + HEAD_DIM, pl.ds(first, reach)]
            outs.append(mm(values, raised.astype(BF16)) * (1.0 / total))
    mixed = jnp.concatenate(outs, axis=0).T.astype(BF16)
    context[...] = mixed
    for head, one in enumerate(sums):
        logsum[head : head + 1, :] = one
    partial_sum[...] = (mm_nt(mixed, wout[...]) + mm_nt(active[...], wdown[...])).astype(BF16)


def attend(index, starts, qkv, value_t, active, pack, kept):
    _, tokens, width = qkv.shape
    hidden = active.shape[1]
    model = pack.shape[0]
    heads = width // HEAD_DIM
    return chunk_call(
        attend_body,
        "attend",
        index,
        [
            ((tokens, width), BF16, (TOKENS, width), ROWS),
            ((heads, tokens), F32, (heads, TOKENS), LANES),
            ((TOKENS, model), BF16, (TOKENS, model), HERE),
        ],
        [
            (starts, (1, tokens), HERE),
            (qkv, (3, tokens, width), lambda i: (0, 0, 0)),
            (value_t, (width, tokens), HERE),
            (active, (TOKENS, hidden), ROWS),
            (pack, (model, width), lambda i: (0, 3)),
            (pack, (model, hidden), lambda i: (0, 2)),
        ],
        kept,
    )


def through_branch_body(ways, number, *refs):
    wout, wdown, slope, pre_grad, context_grad, copied = refs[ways:]
    grads = added(refs[:ways])
    keep_by_owner(copied, (number[1], number[2]), grads)
    pre_grad[...] = (mm(grads, wdown[...]) * slope[...].astype(F32)).astype(BF16)
    context_grad[...] = mm(grads, wout[...]).astype(BF16)


def through_branch(chunk, index, place, pack, slope, width, kept):
    tokens, hidden = slope.shape
    model = pack.shape[0]
    return chunk_call(
        partial(through_branch_body, len(chunk)),
        "through_branch",
        index,
        [
            ((tokens, hidden), BF16, (TOKENS, hidden), ROWS),
            ((tokens, width), BF16, (TOKENS, width), ROWS),
            ((tokens, model), BF16, (TOKENS, model), ROWS),
        ],
        [(way, (TOKENS, model), HERE) for way in chunk]
        + [
            (pack, (model, width), lambda i: (0, 3)),
            (pack, (model, hidden), lambda i: (0, 2)),
            (slope, (TOKENS, hidden), ROWS),
        ],
        kept,
        place,
    )


def window_of(block, size):
    return (max(0, block * size - LONGEST_DOC), (block + 1) * size)


def attend_back_kernel(starts, qkv, grads, logsum, cosine, sine, out, key_sum, value_sum):
    size = TOKENS
    factor = 1.0 / math.sqrt(HEAD_DIM)
    tokens = qkv.shape[1]
    heads = 128 // HEAD_DIM
    key_t = qkv[1].astype(F32).T.astype(BF16)
    key_sum[...] = jnp.zeros_like(key_sum)
    value_sum[...] = jnp.zeros_like(value_sum)
    for block in range(tokens // size):
        first, last = window_of(block, size)
        rows = slice(block * size, (block + 1) * size)
        shape = (last - first, size)
        key_at = first + lax.broadcasted_iota(jnp.int32, shape, 0)
        query_at = block * size + lax.broadcasted_iota(jnp.int32, shape, 1)
        allowed = (key_at <= query_at) & (key_at >= starts[0:1, rows])
        key_part, value_part, query_parts = (0.0, 0.0, [])
        for head in range(heads):
            query = own_lanes(qkv[0, rows], head, factor)
            grad = own_lanes(grads[rows], head)
            scores = jnp.where(allowed, mm_nt(qkv[1, first:last], query), NEG_FILL)
            probs = jnp.exp(scores - logsum[0, head : head + 1, rows])
            probs_grad = mm_nt(qkv[2, first:last], grad)
            inner = jnp.sum(probs_grad * probs, axis=0, keepdims=True)
            score_grad = (probs * (probs_grad - inner)).astype(BF16)
            key_part += mm(score_grad, query)
            value_part += mm(probs.astype(BF16), grad)
            query_parts.append(
                mm(key_t[head * HEAD_DIM : (head + 1) * HEAD_DIM, first:last], score_grad)
            )
        key_sum[first:last] += key_part
        value_sum[first:last] += value_part
        query_grad = jnp.concatenate(query_parts, axis=0).T * factor
        out[0, rows] = turn(query_grad, cosine[rows], sine[rows], -1.0).astype(BF16)
    out[1] = turn(key_sum[...], cosine[...], sine[...], -1.0).astype(BF16)
    out[2] = value_sum[...].astype(BF16)


def attend_back(starts, qkv, context_grad, logsum, tables):
    _, tokens, width = qkv.shape
    pairs = width // 128
    heads = 128 // HEAD_DIM
    return pl.pallas_call(
        attend_back_kernel,
        grid=(pairs,),
        in_specs=[
            pl.BlockSpec((1, tokens), lambda p: (0, 0)),
            pl.BlockSpec((3, tokens, 128), lambda p: (0, 0, p)),
            pl.BlockSpec((tokens, 128), lambda p: (0, p)),
            pl.BlockSpec((1, heads, tokens), lambda p: (p, 0, 0)),
            pl.BlockSpec((tokens, 128), lambda p: (0, 0)),
            pl.BlockSpec((tokens, 128), lambda p: (0, 0)),
        ],
        out_specs=pl.BlockSpec((3, tokens, 128), lambda p: (0, 0, p)),
        out_shape=jax.ShapeDtypeStruct((3, tokens, width), BF16),
        scratch_shapes=[pltpu.VMEM((tokens, 128), F32), pltpu.VMEM((tokens, 128), F32)],
        compiler_params=params(),
        name="attend_back",
    )(starts, qkv, context_grad, logsum.reshape(pairs, heads, tokens), *tables)


def through_inputs_body(ways, number, *refs):
    norms, project_grad, pre_grad, wqkv, wup, normed_grad, terms = refs[ways:]
    normed, _ = normalize(added(refs[:ways]))
    width = project_grad.shape[2]
    attn = mm_nt(project_grad[0], wqkv[:, :width])
    attn += mm_nt(project_grad[1], wqkv[:, width : 2 * width])
    attn += mm_nt(project_grad[2], wqkv[:, 2 * width :])
    feed = mm_nt(pre_grad[...], wup[...])
    normed_grad[...] = (attn * norms[0:1] + feed * norms[2:3]).astype(BF16)
    terms[0:1] = jnp.sum(attn * normed, axis=0, keepdims=True)
    terms[1:2] = jnp.sum(attn, axis=0, keepdims=True)
    terms[2:3] = jnp.sum(feed * normed, axis=0, keepdims=True)
    terms[3:4] = jnp.sum(feed, axis=0, keepdims=True)


def through_inputs(chunk, index, norms, project_grad, pre_grad, pack):
    model = pack.shape[0]
    hidden = pre_grad.shape[1]
    width = project_grad.shape[2]
    return chunk_call(
        partial(through_inputs_body, len(chunk)),
        "through_inputs",
        index,
        [
            ((TOKENS, model), BF16, (TOKENS, model), HERE),
            ((4, model), F32, (4, model), HERE),
        ],
        [(way, (TOKENS, model), HERE) for way in chunk]
        + [
            (norms, (4, model), HERE),
            (project_grad, (3, TOKENS, width), lambda i: (0, i, 0)),
            (pre_grad, (TOKENS, hidden), ROWS),
            (pack, (model, 3 * width), HERE),
            (pack, (model, hidden), lambda i: (0, 1)),
        ],
    )


def outer_kernel(attn_in, feed_in, upstream, project_grad, context, pre_grad, active, out):
    step = pl.program_id(0)

    def fill(left, right, start=0):
        width = right.shape[1]
        out[:, :, start : start + width] = (
            lax.dot_general(left[...], right, (((0,), (0,)), ((), ())), preferred_element_type=F32)
            .astype(BF16)
            .reshape(*out.shape[:2], width)
        )

    @pl.when(step == 0)
    def _():
        fill(attn_in, project_grad[0])
        fill(attn_in, project_grad[1], context.shape[1])

    @pl.when(step == 1)
    def _():
        fill(attn_in, project_grad[2])
        fill(upstream, context[...], context.shape[1])

    pl.when((step == 2) | (step == 3))(lambda: fill(feed_in, pre_grad[...]))
    pl.when(step >= 4)(lambda: fill(upstream, active[...]))


def weight_grads(half, saved, upstream, pre_grad, project_grad):
    attn_in, feed_in, active, context = saved
    tokens, model = attn_in.shape
    width = context.shape[1]
    left = pl.BlockSpec((tokens, model // 2), lambda j: (0, half))
    return pl.pallas_call(
        outer_kernel,
        grid=(6,),
        in_specs=[
            left,
            left,
            left,
            pl.BlockSpec((3, tokens, width), lambda j: (0, 0, 0)),
            pl.BlockSpec((tokens, width), lambda j: (0, 0)),
            pl.BlockSpec((tokens, 2 * width), lambda j: (0, jnp.clip(j - 2, 0, 1))),
            pl.BlockSpec((tokens, 2 * width), lambda j: (0, jnp.clip(j - 4, 0, 1))),
        ],
        out_specs=pl.BlockSpec((4, model // 8, 2 * width), lambda j: (0, 0, j)),
        out_shape=jax.ShapeDtypeStruct((4, model // 8, 12 * width), BF16),
        compiler_params=params(58),
        name="weight_grads",
    )(attn_in, feed_in, upstream, project_grad, context, pre_grad, active)


def fold_kernel(kept, came, side, ahead, rest):
    half = kept.shape[1] // 2
    both = (kept[...].astype(F32) + came[...].astype(F32)).astype(BF16)
    side[0] = both[1, :half]
    side[1] = both[3, :half]
    ahead[0] = both[2, half:]
    ahead[1] = both[3, half:]
    rest[0] = both[0, :half]
    rest[1] = both[2, :half]
    rest[2] = both[0, half:]
    rest[3] = both[1, half:]


def fold(kept, came):
    _, rows, width = kept.shape
    step = width // 6
    block = lambda n, r: pl.BlockSpec((n, r, step), lambda j: (0, 0, j))
    shape = lambda n: jax.ShapeDtypeStruct((n, rows // 2, width), BF16)
    return pl.pallas_call(
        fold_kernel,
        grid=(6,),
        in_specs=[block(4, rows), block(4, rows)],
        out_specs=[block(2, rows // 2), block(2, rows // 2), block(4, rows // 2)],
        out_shape=[shape(2), shape(2), shape(4)],
        compiler_params=params(),
        name="fold",
    )(kept, came)


def assemble_kernel(place, *refs):
    pieces, whole = (refs[:-1], refs[-1])
    rows = pieces[0].shape[0]
    each = len(pieces) // 2
    for order, piece in enumerate(pieces):
        core, number = (order // each, min(order % each, 3))
        at = ((place[1] ^ number) * 2 + (place[0] ^ core)) * rows
        at = at + (rows // 2 if order % each == 4 else 0)
        whole[pl.ds(pl.multiple_of(at, rows // 2), piece.shape[0]), :] = piece[...]


def assemble(place, pieces):
    rows, width = pieces[0].shape
    step = width // 6
    return pl.pallas_call(
        assemble_kernel,
        grid_spec=pltpu.PrefetchScalarGridSpec(
            num_scalar_prefetch=1,
            grid=(6,),
            in_specs=[pl.BlockSpec((piece.shape[0], step), lambda j, place: (0, j)) for piece in pieces],
            out_specs=pl.BlockSpec((8 * rows, step), lambda j, place: (0, j)),
        ),
        out_shape=jax.ShapeDtypeStruct((8 * rows, width), BF16),
        compiler_params=params(58),
        name="assemble",
    )(place, *pieces)


def unpack_kernel(place, upper, lower, came, qkv, out, up, down):
    width, hidden = (out.shape[0], up.shape[1])
    half = came.shape[0]
    own = jnp.concatenate([upper[...], lower[...]], axis=0)
    for core, block in ((place[0], own), (1 - place[0], came[...].astype(F32))):
        rows = pl.ds(pl.multiple_of(core * half, half), half)
        qkv[rows, :] = block[:, : 3 * width]
        out[:, rows] = block[:, 3 * width : 4 * width].T
        up[rows, :] = block[:, 4 * width : 4 * width + hidden]
        down[:, rows] = block[:, 4 * width + hidden :].T


def unpack(sec, upper, lower, came, width, hidden):
    half = came.shape[0]
    shapes = [(2 * half, 3 * width), (width, 2 * half), (2 * half, hidden), (hidden, 2 * half)]
    return pl.pallas_call(
        unpack_kernel,
        grid_spec=pltpu.PrefetchScalarGridSpec(
            num_scalar_prefetch=1,
            grid=(1,),
            in_specs=[
                pl.BlockSpec(array.shape, lambda i, place: (0, 0)) for array in (upper, lower, came)
            ],
            out_specs=[pl.BlockSpec(shape, lambda i, place: (0, 0)) for shape in shapes],
        ),
        out_shape=[jax.ShapeDtypeStruct(shape, F32) for shape in shapes],
        compiler_params=params(32),
        name="unpack",
    )(sec.reshape(1).astype(jnp.int32), upper, lower, came)


def swap(block, axis, bit):
    return lax.ppermute(block, axis, [(i, i ^ bit) for i in range(lax.axis_size(axis))])


def join(*values):
    flat, tree = jax.tree.flatten(values)
    return jax.tree.unflatten(tree, lax.optimization_barrier(tuple(flat)))


def sum_over(value, axis):
    others = [swap(value, axis, bit) for bit in range(1, lax.axis_size(axis))]
    return sum(others, start=value)


def pick(stack, index):
    return lax.dynamic_index_in_dim(stack, index, 0, keepdims=False)


def send_sides(half):
    return (swap(half, "col", 1), swap(half, "col", 2))


def send_corner(side, ahead):
    rows = side.shape[0] // 2
    return [swap(side[:rows], "col", 2), swap(ahead[rows:], "col", 1)]


def add(a, b):
    return a.astype(F32) + b.astype(F32)


def along_row(block, pairs):
    return lax.ppermute(block, "row", pairs)


ONE_OVER = [(0, 1), (1, 0), (2, 3), (3, 2)]
TWO_OVER = [(0, 2), (2, 0), (1, 3), (3, 1)]
MIDDLE = [(1, 2), (2, 1)]
OUTWARD = [(1, 0), (2, 3)]
INWARD = [(0, 1), (3, 2)]


def send_own(own):
    return (along_row(own, TWO_OVER), along_row(own, ONE_OVER))


def pass_on(own, far):
    return (along_row(far, OUTWARD), along_row(own, MIDDLE))


def send_last(share):
    return (along_row(share, INWARD), along_row(share, MIDDLE))


def send_sums(far, passed, near):
    return (along_row(add(far, passed).astype(BF16), TWO_OVER), along_row(near, ONE_OVER))


def fast_shards(
    hidden_in,
    doc_ids,
    qkv_weight,
    out_weight,
    up_weight,
    down_weight,
    attn_gain,
    attn_shift,
    mlp_gain,
    mlp_shift,
    out_cotangent,
):
    sec, row, col = (lax.axis_index("section"), lax.axis_index("row"), lax.axis_index("col"))
    cols, rows = (lax.axis_size("col"), lax.axis_size("row"))
    model = hidden_in.shape[3]
    tokens = doc_ids.shape[2]
    width = qkv_weight.shape[3]
    hidden = up_weight.shape[2]
    block = qkv_weight.shape[1]
    first = sec == 0
    x_own = pick(hidden_in[:, 0], sec)
    docs = pick(doc_ids[:, 0], sec)
    given = pick(out_cotangent[:, 0], sec)

    place = jnp.stack([sec, col]).astype(jnp.int32)
    share = attn_gain.shape[1]

    def enter(kept, chunk, number, layer):
        return project(
            chunk,
            row ^ number,
            place,
            tokens,
            norms[layer],
            packs[layer],
            tables,
            width,
            hidden,
            kept,
        )

    def leave(kept, entered, number, layer):
        _, _, qkv, value_t, active, _ = entered
        *kept, share_of = attend(row ^ number, starts, qkv, value_t, active, packs[layer], kept)
        return (tuple(kept), share_of)

    def back_branch(kept, chunk, number, slope, layer):
        return through_branch(chunk, row ^ number, place, packs[layer], slope, width, kept)

    def back_inputs(chunks, number, layer, project_grad, pre_grad):
        return through_inputs(
            chunks[number], row ^ number, norms[layer], project_grad, pre_grad, packs[layer]
        )

    def input_grad(total, own, own_grads):
        normed, scale = normalize(own)
        result = own_grads.astype(F32) + scale * (
            total
            - jnp.mean(total, axis=-1, keepdims=True)
            - normed * jnp.mean(total * normed, axis=-1, keepdims=True)
        )
        return result.astype(BF16)


    vectors = jnp.stack([attn_gain[0], attn_shift[0], mlp_gain[0], mlp_shift[0]])
    norms = lax.dynamic_update_slice(
        jnp.zeros((2, 4, model), F32), vectors[None], (sec, 0, (row * cols + col) * share)
    )
    norms = sum_over(norms, "row")
    own_pack = jnp.concatenate(
        [
            qkv_weight[0].reshape(block, 3 * width),
            out_weight[0].T,
            up_weight[0],
            down_weight[0].T,
        ],
        axis=1,
    )
    half_of = lambda core: lax.dynamic_slice_in_dim(own_pack, core * (block // 2), block // 2)
    staying, leaving = (half_of(sec), half_of(1 - sec))
    norms, staying, leaving = join(norms, staying, leaving)

    came = swap(leaving, "section", 1)
    norms = sum_over(norms, "section")
    half0, half1 = (jnp.where(first, staying, came), jnp.where(first, came, staying))
    norms, half0, half1 = join(norms, half0, half1)

    norms = sum_over(norms, "col")
    side0, ahead0 = send_sides(half0)
    far_x0, near_x0 = send_own(x_own)
    starts = jnp.sum((docs[None, :] < docs[:, None]).astype(jnp.int32), axis=1)
    tables = rope_tables(docs, starts)
    starts = starts[None]
    norms, half0, side0, ahead0, starts, tables = join(
        norms, half0, side0, ahead0, starts, tables
    )

    across0 = send_corner(side0, ahead0)
    mine = [half0, side0, ahead0]
    theirs = [swap(piece, "section", 1) for piece in mine]
    mine, theirs, across0, far_x0, near_x0 = join(mine, theirs, across0, far_x0, near_x0)

    passed_x0, middle_x0 = pass_on(x_own, far_x0)
    theirs = theirs + [swap(piece, "section", 1) for piece in across0]
    packs = [assemble(place, mine + across0 + theirs), None]
    chunks_x0 = [(x_own,), (near_x0,), (far_x0,), (middle_x0, passed_x0)]
    packs, given, half1, chunks_x0 = join(packs, given, half1, chunks_x0)

    side1, ahead1 = send_sides(half1)
    far_g1, near_g1 = send_own(given)
    entered0 = ()
    for number in range(4):
        entered0 = enter(entered0, chunks_x0[number], number, 0)
    kept, last = leave((), entered0, 3, 0)
    half1, side1, ahead1, far_g1, near_g1, entered0, kept, last = join(
        half1, side1, ahead1, far_g1, near_g1, entered0, kept, last
    )

    passed_y0, middle_y0 = send_last(last)
    kept, far = leave(kept, entered0, 2, 0)
    kept, near = leave(kept, entered0, 1, 0)
    (context0, logsum0), share_of = leave(kept, entered0, 0, 0)
    passed_y0, middle_y0, far, near, share_of, context0, half1, side1, ahead1 = join(
        passed_y0, middle_y0, far, near, share_of, context0, half1, side1, ahead1
    )

    far_y0, near_y0 = send_sums(far, passed_y0, near)
    across1 = send_corner(side1, ahead1)
    mine = [half1, side1, ahead1] + across1
    theirs = [swap(piece, "section", 1) for piece in mine]
    far_y0, near_y0, mine, theirs, far_g1 = join(far_y0, near_y0, mine, theirs, far_g1)
    total = add(share_of, near_y0) + add(middle_y0, far_y0)
    y0_own = (x_own.astype(F32) + total).astype(BF16)

    far_x1, near_x1 = send_own(y0_own)
    packs[1] = assemble(place, mine + theirs)
    entered1 = enter((), (y0_own,), 0, 1)
    branch1 = back_branch((), (given,), 0, entered1[5], 1)
    far_x1, near_x1, entered1, branch1 = join(far_x1, near_x1, entered1, branch1)

    passed_x1, middle_x1 = pass_on(y0_own, far_x1)
    entered1 = enter(entered1, (near_x1,), 1, 1)
    branch1 = back_branch(branch1, (near_g1,), 1, entered1[5], 1)
    entered1 = enter(entered1, (far_x1,), 2, 1)
    branch1 = back_branch(branch1, (far_g1,), 2, entered1[5], 1)
    passed_x1, middle_x1, entered1, branch1, far_g1 = join(
        passed_x1, middle_x1, entered1, branch1, far_g1
    )

    chunks_x1 = [(y0_own,), (near_x1,), (far_x1,), (middle_x1, passed_x1)]
    entered1 = enter(entered1, chunks_x1[3], 3, 1)
    passed_g1, middle_g1 = pass_on(given, far_g1)
    kept, last_b1 = leave((), entered1, 3, 1)
    kept, far_b1 = leave(kept, entered1, 2, 1)
    kept, near_b1 = leave(kept, entered1, 1, 1)
    (context1, logsum1), share_b1 = leave(kept, entered1, 0, 1)
    passed_g1, middle_g1, last_b1, far_b1, near_b1, share_b1, context1, entered1 = join(
        passed_g1, middle_g1, last_b1, far_b1, near_b1, share_b1, context1, entered1
    )

    passed_y1, middle_y1 = send_last(last_b1)
    pre_grad1, context_grad1, grads1 = back_branch(
        branch1, (middle_g1, passed_g1), 3, entered1[5], 1
    )
    saved1 = (entered1[0], entered1[1], entered1[4], context1)
    project_grad1 = attend_back(starts, entered1[2], context_grad1, logsum1, tables)
    passed_y1, middle_y1, pre_grad1, project_grad1 = join(
        passed_y1, middle_y1, pre_grad1, project_grad1
    )

    last, terms1 = back_inputs(chunks_x1, 3, 1, project_grad1, pre_grad1)
    last, terms1, project_grad1 = join(last, terms1, project_grad1)

    passed_n1, middle_n1 = send_last(last)
    others = [back_inputs(chunks_x1, number, 1, project_grad1, pre_grad1) for number in (2, 1, 0)]
    (far, near, share_of), terms = zip(*others)
    terms1 = sum(terms, start=terms1)
    passed_n1, middle_n1, far, near, share_of, terms1, project_grad1 = join(
        passed_n1, middle_n1, far, near, share_of, terms1, project_grad1
    )

    far_n1, near_n1 = send_sums(far, passed_n1, near)
    leaving1 = weight_grads(1, saved1, grads1, pre_grad1, project_grad1)
    kept1 = weight_grads(0, saved1, grads1, pre_grad1, project_grad1)
    far_n1, near_n1, leaving1, kept1 = join(far_n1, near_n1, leaving1, kept1)
    total = add(share_of, near_n1) + add(middle_n1, far_n1)
    dx1_own = input_grad(total, y0_own, given)

    slope0 = entered0[5]
    far_g0, near_g0 = send_own(dx1_own)
    came1 = swap(leaving1, "section", 1)
    branch0 = back_branch((), (dx1_own,), 0, slope0, 0)
    far_g0, near_g0, came1, branch0 = join(far_g0, near_g0, came1, branch0)

    passed_g0, middle_g0 = pass_on(dx1_own, far_g0)
    side1, ahead1, rest1 = fold(kept1, came1)
    branch0 = back_branch(branch0, (near_g0,), 1, slope0, 0)
    branch0 = back_branch(branch0, (far_g0,), 2, slope0, 0)
    passed_g0, middle_g0, branch0, side1, ahead1, rest1, far_b1, near_b1 = join(
        passed_g0, middle_g0, branch0, side1, ahead1, rest1, far_b1, near_b1
    )

    first1, second1 = (swap(side1, "col", 1), swap(ahead1, "col", 2))
    far_y1, near_y1 = send_sums(far_b1, passed_y1, near_b1)
    pre_grad0, context_grad0, grads0 = back_branch(branch0, (middle_g0, passed_g0), 3, slope0, 0)
    saved0 = (entered0[0], entered0[1], entered0[4], context0)
    project_grad0 = attend_back(starts, entered0[2], context_grad0, logsum0, tables)
    last, terms0 = back_inputs(chunks_x0, 3, 0, project_grad0, pre_grad0)
    first1, second1, far_y1, near_y1, last, terms0, project_grad0 = join(
        first1, second1, far_y1, near_y1, last, terms0, project_grad0
    )

    passed_n0, middle_n0 = send_last(last)
    passed1 = (
        swap(add(rest1[1], first1[1]).astype(BF16), "col", 2),
        swap(add(rest1[3], second1[1]).astype(BF16), "col", 1),
    )
    sums1 = (
        add(add(rest1[0], first1[0]), passed1[0]),
        add(add(rest1[2], second1[0]), passed1[1]),
    )
    others = [back_inputs(chunks_x0, number, 0, project_grad0, pre_grad0) for number in (2, 1, 0)]
    (far, near, share_of), terms = zip(*others)
    terms0 = sum(terms, start=terms0)
    leaving0 = weight_grads(1, saved0, grads0, pre_grad0, project_grad0)
    passed_n0, middle_n0, far, near, share_of, terms0, leaving0, project_grad0, sums1 = join(
        passed_n0, middle_n0, far, near, share_of, terms0, leaving0, project_grad0, sums1
    )

    far_n0, near_n0 = send_sums(far, passed_n0, near)
    came0 = swap(leaving0, "section", 1)
    kept0 = weight_grads(0, saved0, grads0, pre_grad0, project_grad0)
    came0, kept0 = join(came0, kept0)

    side0, ahead0, rest0 = fold(kept0, came0)
    total = add(share_b1, near_y1) + add(middle_y1, far_y1)
    y1_own = (y0_own.astype(F32) + total).astype(BF16)
    terms = sum_over(jnp.stack([terms0, terms1]), "section")
    side0, ahead0, rest0, terms, y1_own = join(side0, ahead0, rest0, terms, y1_own)

    first0, second0 = (swap(side0, "col", 1), swap(ahead0, "col", 2))
    terms = sum_over(sum_over(terms, "col"), "row")
    first0, second0, far_n0, near_n0, terms = join(first0, second0, far_n0, near_n0, terms)

    total = add(share_of, near_n0) + add(middle_n0, far_n0)
    dx0_own = input_grad(total, x_own, dx1_own)
    passed0 = (
        swap(add(rest0[1], first0[1]).astype(BF16), "col", 2),
        swap(add(rest0[3], second0[1]).astype(BF16), "col", 1),
    )
    sums0 = (
        add(add(rest0[0], first0[0]), passed0[0]),
        add(add(rest0[2], second0[0]), passed0[1]),
    )

    choose = lambda here, there: jnp.where(first, here, there)
    leaving = jnp.concatenate([choose(b, a) for a, b in zip(sums0, sums1)]).astype(BF16)
    upper, lower = [choose(a, b) for a, b in zip(sums0, sums1)]
    qkv_grad, out_grad, up_grad, down_grad = unpack(
        sec, upper, lower, swap(leaving, "section", 1), width, hidden
    )
    terms = pick(terms, sec)
    terms = lax.dynamic_slice_in_dim(terms, (row * cols + col) * share, share, 1)

    def by_layer(zero, one):
        away = swap(choose(one, zero), "section", 1)
        here = choose(zero, one)
        return jnp.stack([choose(here, away), choose(away, here)])

    return (
        by_layer(y0_own, y1_own)[None, :, None],
        by_layer(dx0_own, dx1_own)[None, :, None],
        qkv_grad.reshape(1, block, 3, width),
        out_grad[None],
        up_grad[None],
        down_grad[None],
        terms[None, 0],
        terms[None, 1],
        terms[None, 2],
        terms[None, 3],
    )


def from_behind(block, axis, distance):
    devices = range(lax.axis_size(axis))
    route = [(i - distance, i) for i in devices if i - distance in devices]
    return lax.ppermute(block, axis, route)


def positions_of(docs):
    length = docs.shape[0]
    index = jnp.arange(length, dtype=jnp.int32)
    starts = jnp.concatenate([jnp.ones((1,), jnp.bool_), docs[1:] != docs[:-1]])
    first = lax.cummax(jnp.where(starts, index, 0), axis=0)
    return index - first


def rotary_tables(docs):
    half = ROT // 2
    freqs = 10000.0 ** (-2.0 * jnp.arange(half, dtype=jnp.float32) / ROT)
    angles = positions_of(docs).astype(jnp.float32)[:, None] * freqs[None, :]
    return (jnp.cos(angles)[:, None, :], jnp.sin(angles)[:, None, :])


def rotate(values, cosine, sine):
    half = ROT // 2
    front = values[..., :half]
    back = values[..., half:ROT]
    return jnp.concatenate(
        [front * cosine - back * sine, back * cosine + front * sine, values[..., ROT:]], axis=-1
    )


def rotate_back(grads, cosine, sine):
    half = ROT // 2
    front = grads[..., :half]
    back = grads[..., half:ROT]
    return jnp.concatenate(
        [front * cosine + back * sine, back * cosine - front * sine, grads[..., ROT:]], axis=-1
    )


def block_mask(docs, start, size):
    rows = start + jnp.arange(size, dtype=jnp.int32)
    cols = jnp.arange(docs.shape[0], dtype=jnp.int32)
    row_docs = lax.dynamic_slice_in_dim(docs, start, size)
    return (row_docs[:, None] == docs[None, :]) & (cols[None, :] <= rows[:, None])


def block_scores(query, key, docs, start, block):
    factor = 1.0 / math.sqrt(query.shape[2])
    rows = lax.dynamic_slice_in_dim(query, start, block)
    scores = jnp.einsum("qhd,khd->hqk", rows, key, preferred_element_type=jnp.float32) * factor
    allowed = block_mask(docs, start, block)[None]
    return (rows, jnp.where(allowed, scores, NEG_FILL))


def attend_forward(query, key, value, docs):
    length, heads, width = query.shape
    block = min(512, length)

    def one_block(number):
        start = number * block
        rows, scores = block_scores(query, key, docs, start, block)
        peak = jnp.max(scores, axis=-1, keepdims=True)
        raised = jnp.exp(scores - peak)
        total = jnp.sum(raised, axis=-1, keepdims=True)
        probs = (raised / total).astype(jnp.bfloat16)
        context = jnp.einsum(
            "hqk,khd->qhd", probs, value, preferred_element_type=jnp.float32
        ).astype(jnp.bfloat16)
        return (context, (peak + jnp.log(total))[..., 0])

    context, logsum = lax.map(one_block, jnp.arange(length // block, dtype=jnp.int32))
    return (context.reshape(length, heads, width), logsum)


def attend_backward(query, key, value, docs, logsum, context_grad):
    length, heads, width = query.shape
    block = min(512, length)
    factor = 1.0 / math.sqrt(width)

    def one_block(carry, inputs):
        key_grad, value_grad = carry
        number, block_logsum = inputs
        start = number * block
        rows, scores = block_scores(query, key, docs, start, block)
        rows_grad = lax.dynamic_slice_in_dim(context_grad, start, block)
        probs_full = jnp.exp(scores - block_logsum[:, :, None])
        probs = probs_full.astype(jnp.bfloat16)
        context = jnp.einsum(
            "hqk,khd->qhd", probs, value, preferred_element_type=jnp.float32
        ).astype(jnp.bfloat16)
        probs_grad = jnp.einsum(
            "qhd,khd->hqk", rows_grad, value, preferred_element_type=jnp.float32
        )
        inner = jnp.sum(probs_grad * probs_full, axis=-1, keepdims=True)
        score_grad = (probs_full * (probs_grad - inner)).astype(jnp.bfloat16)
        query_grad = (
            jnp.einsum("hqk,khd->qhd", score_grad, key, preferred_element_type=jnp.float32) * factor
        )
        key_grad = (
            key_grad
            + jnp.einsum("hqk,qhd->khd", score_grad, rows, preferred_element_type=jnp.float32)
            * factor
        )
        value_grad = value_grad + jnp.einsum(
            "hqk,qhd->khd", probs, rows_grad, preferred_element_type=jnp.float32
        )
        return ((key_grad, value_grad), (context, query_grad))

    zeros = jnp.zeros((length, heads, width), jnp.float32)
    numbers = jnp.arange(length // block, dtype=jnp.int32)
    (key_grad, value_grad), (context, query_grad) = lax.scan(
        one_block, (zeros, zeros), (numbers, logsum)
    )
    return (
        context.reshape(length, heads * width),
        query_grad.reshape(length, heads, width),
        key_grad,
        value_grad,
    )


def gather_features(shard):
    return lax.all_gather(shard, "row", axis=0, tiled=True)


def recompute_inputs(full, docs, norms, weights):
    gain_a, shift_a, gain_m, shift_m = norms
    qkv_full = weights[0]
    normed, scale = normalize(full)
    attn_in = (normed * gain_a + shift_a).astype(jnp.bfloat16)
    feed_in = (normed * gain_m + shift_m).astype(jnp.bfloat16)
    length = full.shape[0]
    heads_here = qkv_full.shape[2] // HEAD_DIM
    project = jnp.einsum("td,dke->tke", attn_in, qkv_full, preferred_element_type=jnp.float32)
    cosine, sine = rotary_tables(docs)
    query = rotate(project[:, 0].reshape(length, heads_here, HEAD_DIM), cosine, sine).astype(
        jnp.bfloat16
    )
    key = rotate(project[:, 1].reshape(length, heads_here, HEAD_DIM), cosine, sine).astype(
        jnp.bfloat16
    )
    value = project[:, 2].reshape(length, heads_here, HEAD_DIM).astype(jnp.bfloat16)
    pre = jnp.dot(feed_in, weights[2], preferred_element_type=jnp.float32)
    return (normed, scale, attn_in, feed_in, query, key, value, pre, cosine, sine)


def layer_forward(shard, docs, full, norms, weights):
    normed, scale, attn_in, feed_in, query, key, value, pre, cosine, sine = recompute_inputs(
        full, docs, norms, weights
    )
    length = full.shape[0]
    context, logsum = attend_forward(query, key, value, docs)
    active = jax.nn.gelu(pre, approximate=False).astype(jnp.bfloat16)
    partial_sum = jnp.dot(
        context.reshape(length, -1), weights[1], preferred_element_type=jnp.float32
    )
    partial_sum = partial_sum + jnp.dot(active, weights[3], preferred_element_type=jnp.float32)
    branch = lax.psum_scatter(
        partial_sum.astype(jnp.bfloat16), "row", scatter_dimension=0, tiled=True
    ).astype(jnp.float32)
    return ((shard.astype(jnp.float32) + branch).astype(jnp.bfloat16), logsum)


def layer_backward(docs, full, logsum, upstream, norms, weights):
    gain_a, shift_a, gain_m, shift_m = norms
    qkv_full, out_full, up_full, down_full = weights
    normed, scale, attn_in, feed_in, query, key, value, pre, cosine, sine = recompute_inputs(
        full, docs, norms, weights
    )
    length = full.shape[0]
    heads_here = query.shape[1]
    active = jax.nn.gelu(pre, approximate=False).astype(jnp.bfloat16)
    upstream_full = lax.all_gather(upstream, "row", axis=0, tiled=True)
    down_part = jnp.einsum("tf,td->fd", active, upstream_full, preferred_element_type=jnp.float32)
    act_grad = jnp.einsum("td,fd->tf", upstream_full, down_full, preferred_element_type=jnp.float32)
    pre_grad = jax.vjp(partial(jax.nn.gelu, approximate=False), pre)[1](act_grad)[0].astype(
        jnp.bfloat16
    )
    up_part = jnp.einsum("td,tf->df", feed_in, pre_grad, preferred_element_type=jnp.float32)
    feed_grad = jnp.einsum("tf,df->td", pre_grad, up_full, preferred_element_type=jnp.float32)
    context_grad = jnp.einsum(
        "td,ed->te", upstream_full, out_full, preferred_element_type=jnp.float32
    ).astype(jnp.bfloat16)
    context_grad = context_grad.reshape(length, heads_here, HEAD_DIM)
    context, query_grad, key_grad, value_grad = attend_backward(
        query, key, value, docs, logsum, context_grad
    )
    out_part = jnp.einsum("te,td->ed", context, upstream_full, preferred_element_type=jnp.float32)
    project_grad = jnp.stack(
        [
            rotate_back(query_grad, cosine, sine).reshape(length, -1),
            rotate_back(key_grad, cosine, sine).reshape(length, -1),
            value_grad.reshape(length, -1),
        ],
        axis=1,
    ).astype(jnp.bfloat16)
    qkv_part = jnp.einsum("td,tke->dke", attn_in, project_grad, preferred_element_type=jnp.float32)
    attn_grad = jnp.einsum(
        "tke,dke->td", project_grad, qkv_full, preferred_element_type=jnp.float32
    )
    own_rows = upstream.shape[0]
    offset = lax.axis_index("row") * own_rows
    normed_part = lax.dynamic_slice_in_dim(normed, offset, own_rows, 0)
    scale_part = lax.dynamic_slice_in_dim(scale, offset, own_rows, 0)
    attn_piece, feed_piece = (
        lax.psum_scatter(
            attn_grad.astype(jnp.bfloat16), "row", scatter_dimension=0, tiled=True
        ).astype(jnp.float32),
        lax.psum_scatter(
            feed_grad.astype(jnp.bfloat16), "row", scatter_dimension=0, tiled=True
        ).astype(jnp.float32),
    )
    normed_grad = attn_piece * gain_a + feed_piece * gain_m
    gain_terms = (
        jnp.sum(attn_piece * normed_part, axis=0),
        jnp.sum(attn_piece, axis=0),
        jnp.sum(feed_piece * normed_part, axis=0),
        jnp.sum(feed_piece, axis=0),
    )
    row_sum = jnp.sum(normed_grad, axis=-1)
    cross_sum = jnp.sum(normed_grad * normed_part, axis=-1)
    count = full.shape[1]
    input_grad = upstream.astype(jnp.float32) + scale_part * (
        normed_grad - row_sum[:, None] / count - normed_part * cross_sum[:, None] / count
    )
    return (input_grad, (qkv_part, out_part, up_part, down_part), gain_terms)


def general_shards(
    hidden_in,
    doc_ids,
    qkv_weight,
    out_weight,
    up_weight,
    down_weight,
    attn_gain,
    attn_shift,
    mlp_gain,
    mlp_shift,
    out_cotangent,
):
    micro = hidden_in.shape[0]
    first_section = lax.axis_index("section") == 0
    norms = (
        lax.all_gather(attn_gain[0], ("row", "col"), axis=0, tiled=True),
        lax.all_gather(attn_shift[0], ("row", "col"), axis=0, tiled=True),
        lax.all_gather(mlp_gain[0], ("row", "col"), axis=0, tiled=True),
        lax.all_gather(mlp_shift[0], ("row", "col"), axis=0, tiled=True),
    )
    weights = (
        lax.all_gather(qkv_weight[0], "col", axis=0, tiled=True),
        lax.all_gather(out_weight[0], "col", axis=1, tiled=True),
        lax.all_gather(up_weight[0], "col", axis=0, tiled=True),
        lax.all_gather(down_weight[0], "col", axis=1, tiled=True),
    )
    received = jnp.zeros_like(hidden_in[0, 0])
    tick_inputs, tick_docs, tick_fulls, tick_outputs, tick_logsums = ([], [], [], [], [])
    for tick in range(micro + 1):
        own = hidden_in[min(tick, micro - 1), 0]
        shard = jnp.where(first_section, own, received)
        docs = jnp.where(
            first_section, doc_ids[min(tick, micro - 1), 0], doc_ids[max(tick - 1, 0), 0]
        )
        full = gather_features(shard)
        result, logsum = layer_forward(shard, docs, full, norms, weights)
        tick_inputs.append(shard)
        tick_docs.append(docs)
        tick_fulls.append(full)
        tick_outputs.append(result)
        tick_logsums.append(logsum)
        if tick < micro:
            received = from_behind(result, "section", 1)
    outputs = jnp.stack(
        [
            jnp.where(first_section, tick_outputs[number], tick_outputs[number + 1])
            for number in range(micro)
        ]
    )
    received = jnp.zeros_like(hidden_in[0, 0])
    matrix_totals = None
    gain_totals = None
    tick_grads = []
    for tick in range(micro + 1):
        early = max(tick - 1, 0)
        later = min(tick + 1, micro)
        if tick < micro:
            given = out_cotangent[tick, 0]
        else:
            given = jnp.zeros_like(out_cotangent[0, 0])
        upstream = jnp.where(first_section, received, given)
        shard = jnp.where(first_section, tick_inputs[early], tick_inputs[later])
        docs = jnp.where(first_section, tick_docs[early], tick_docs[later])
        logsum = jnp.where(first_section, tick_logsums[early], tick_logsums[later])
        full = gather_features(shard)
        input_grad, matrices, gain_terms = layer_backward(
            docs, full, logsum, upstream, norms, weights
        )
        if matrix_totals is None:
            matrix_totals = matrices
            gain_totals = gain_terms
        else:
            matrix_totals = jax.tree.map(jnp.add, matrix_totals, matrices)
            gain_totals = jax.tree.map(jnp.add, gain_totals, gain_terms)
        grad_low = input_grad.astype(jnp.bfloat16)
        tick_grads.append(grad_low)
        if tick < micro:
            received = from_behind(grad_low, "section", -1)
    grads_in = jnp.stack(
        [
            jnp.where(first_section, tick_grads[number + 1], tick_grads[number])
            for number in range(micro)
        ]
    )
    qkv_sum, out_sum, up_sum, down_sum = matrix_totals
    gain_a_sum, shift_a_sum, gain_m_sum, shift_m_sum = gain_totals
    qkv_total, out_total, up_total, down_total = (
        lax.psum_scatter(
            qkv_sum.astype(jnp.bfloat16), "col", scatter_dimension=0, tiled=True
        ).astype(jnp.float32),
        lax.psum_scatter(
            out_sum.astype(jnp.bfloat16), "col", scatter_dimension=1, tiled=True
        ).astype(jnp.float32),
        lax.psum_scatter(
            up_sum.astype(jnp.bfloat16), "col", scatter_dimension=0, tiled=True
        ).astype(jnp.float32),
        lax.psum_scatter(
            down_sum.astype(jnp.bfloat16), "col", scatter_dimension=1, tiled=True
        ).astype(jnp.float32),
    )
    gain_a_total, shift_a_total, gain_m_total, shift_m_total = (
        lax.psum_scatter(gain_a_sum, ("row", "col"), scatter_dimension=0, tiled=True),
        lax.psum_scatter(shift_a_sum, ("row", "col"), scatter_dimension=0, tiled=True),
        lax.psum_scatter(gain_m_sum, ("row", "col"), scatter_dimension=0, tiled=True),
        lax.psum_scatter(shift_m_sum, ("row", "col"), scatter_dimension=0, tiled=True),
    )
    return (
        outputs[None, :, None],
        grads_in[None, :, None],
        qkv_total[None],
        out_total[None],
        up_total[None],
        down_total[None],
        gain_a_total[None],
        shift_a_total[None],
        gain_m_total[None],
        shift_m_total[None],
    )


def shards(*arrays):
    hidden_in, qkv_weight, up_weight = (arrays[0], arrays[2], arrays[4])
    micro, seqs, own_tokens, model = hidden_in.shape
    width, hidden = (qkv_weight.shape[3], up_weight.shape[2])
    sizes = tuple(lax.axis_size(axis) for axis in ("section", "row", "col"))
    fits = (
        sizes == (2, 4, 4) and (micro, seqs) == (2, 1)
        and own_tokens == TOKENS
        and width % 128 == 0
        and 4 * width == hidden
    )
    return fast_shards(*arrays) if fits else general_shards(*arrays)


def solution(mesh):
    placed = (
        P(None, "col", "row", None),
        P(None, "col", None),
        P("section", "col", None, "row"),
        P("section", "row", "col"),
        P("section", "col", "row"),
        P("section", "row", "col"),
        P("section", ("row", "col")),
        P("section", ("row", "col")),
        P("section", ("row", "col")),
        P("section", ("row", "col")),
        P(None, "col", "row", None),
    )
    return jax.shard_map(
        shards,
        mesh=mesh,
        in_specs=placed,
        out_specs=(
            P("section", None, "col", "row", None),
            P("section", None, "col", "row", None),
            P("section", "col", None, "row"),
            P("section", "row", "col"),
            P("section", "col", "row"),
            P("section", "row", "col"),
            P("section", ("row", "col")),
            P("section", ("row", "col")),
            P("section", ("row", "col")),
            P("section", ("row", "col")),
        ),
        check_vma=False,
    )
```

```python
from functools import partial
import math

import jax
import jax.numpy as jnp
from jax import lax
from jax.experimental import pallas as pl
from jax.experimental.pallas import tpu as pltpu
from jax.sharding import PartitionSpec as P

HEAD_DIM = 64
ROT = 16
EPSILON = 1e-05
NEG_FILL = -1e30
BF16 = jnp.bfloat16
F32 = jnp.float32
TOKENS = 256
LONGEST_DOC = 512


def mm(a, b):
    return lax.dot_general(a, b, (((1,), (0,)), ((), ())), preferred_element_type=F32)


def mm_nt(a, b):
    return lax.dot_general(a, b, (((1,), (1,)), ((), ())), preferred_element_type=F32)


def normalize(full):
    wide = full.astype(F32)
    center = wide - jnp.mean(wide, axis=-1, keepdims=True)
    scale = lax.rsqrt(jnp.mean(center * center, axis=-1, keepdims=True) + EPSILON)
    return (center * scale, scale)


ERFC = (
    0.17087277,
    -0.82215223,
    1.48851587,
    -1.13520398,
    0.27886807,
    -0.18628806,
    0.09678418,
    0.37409196,
    1.00002368,
    -1.26551223,
)


def gelu_and_slope(pre):
    size = jnp.abs(pre) * math.sqrt(0.5)
    t = 1.0 / (1.0 + 0.5 * size)
    poly = jnp.full_like(t, ERFC[0])
    for coefficient in ERFC[1:]:
        poly = poly * t + coefficient
    bell = jnp.exp(-(size * size))
    tail = (0.5 * t) * (bell * jnp.exp(poly))
    below = jnp.where(pre >= 0, 1.0 - tail, tail)
    return (pre * below, below + pre * (bell * (1.0 / math.sqrt(2.0 * math.pi))))


def turn(values, cosine, sine, sign):
    width = values.shape[-1]
    half = ROT // 2
    lane = lax.broadcasted_iota(jnp.int32, values.shape, 1) % HEAD_DIM
    other = jnp.where(
        lane < half, -pltpu.roll(values, width - half, 1), pltpu.roll(values, half, 1)
    )
    return values * cosine + (sign * other) * sine


def rope_tables(docs, starts):
    half = ROT // 2
    lane = jnp.arange(128, dtype=jnp.int32) % HEAD_DIM
    freqs = 10000.0 ** (-2.0 * (lane % half).astype(F32) / ROT)
    position = (jnp.arange(docs.shape[0], dtype=jnp.int32) - starts).astype(F32)
    angles = position[:, None] * freqs[None, :]
    rotated = (lane < ROT)[None, :]
    return (jnp.where(rotated, jnp.cos(angles), 1.0), jnp.where(rotated, jnp.sin(angles), 0.0))


def params(mib=18):
    return pltpu.CompilerParams(vmem_limit_bytes=mib << 20)


def cost(us):
    return pl.CostEstimate(flops=int(us * 1.1e+09), bytes_accessed=int(us * 3.2e+06), transcendentals=0)


def chunk_call(body, name, us, index, outs, inputs, kept=(), place=None):
    given = len(inputs)
    number = index.reshape(1).astype(jnp.int32)
    if place is not None:
        number = jnp.concatenate([number, place])

    def kernel(number, *refs):
        body(number, *refs[:given], *refs[given + len(kept) :])

    spec = lambda block, at: pl.BlockSpec(block, lambda i, number: at(number[0]))
    return pl.pallas_call(
        kernel,
        grid_spec=pltpu.PrefetchScalarGridSpec(
            num_scalar_prefetch=1,
            grid=(1,),
            in_specs=[spec(block, at) for _, block, at in inputs]
            + [pl.BlockSpec(memory_space=pl.ANY) for _ in kept],
            out_specs=[spec(block, at) for _, _, block, at in outs],
        ),
        out_shape=[jax.ShapeDtypeStruct(shape, dtype) for shape, dtype, _, _ in outs],
        input_output_aliases={1 + given + i: i for i in range(len(kept))},
        compiler_params=params(),
        cost_estimate=cost(us),
        name=name,
    )(number, *[array for array, _, _ in inputs], *kept)


HERE = lambda i: (0, 0)
ROWS = lambda i: (i, 0)
LANES = lambda i: (0, i)


def added(refs):
    whole = refs[0][...]
    for ref in refs[1:]:
        whole = whole + ref[...]
    return whole


def keep_by_owner(kept, place, values):
    blocks = values.shape[1] // 128
    for block in range(blocks):
        at = (place[0] ^ (block % 2)) * (blocks // 2) + (place[1] ^ (block // 2))
        lanes = pl.ds(pl.multiple_of(at * 128, 128), 128)
        kept[:, lanes] = values[:, block * 128 : (block + 1) * 128]


def project_body(ways, number, *refs):
    norms, wqkv, wup, cosine, sine, attn_in, feed_in, qkv, value_t, active, slope = refs[ways:]
    normed, _ = normalize(added(refs[:ways]))
    attn = (normed * norms[0:1] + norms[1:2]).astype(BF16)
    feed = (normed * norms[2:3] + norms[3:4]).astype(BF16)
    place = (number[1], number[2])
    keep_by_owner(attn_in, place, attn)
    keep_by_owner(feed_in, place, feed)
    width = qkv.shape[2]
    for part in range(3):
        piece = mm(attn, wqkv[:, part * width : (part + 1) * width])
        for pair in range(width // 128):
            lanes = slice(pair * 128, (pair + 1) * 128)
            one = piece[:, lanes]
            if part < 2:
                one = turn(one, cosine[...], sine[...], 1.0)
            else:
                value_t[lanes, :] = one.T.astype(BF16)
            qkv[part, :, lanes] = one.astype(BF16)
    hidden = wup.shape[1]
    for start in range(0, hidden, 256):
        lanes = slice(start, start + 256)
        act, der = gelu_and_slope(mm(feed, wup[:, lanes]))
        active[:, lanes] = act.astype(BF16)
        slope[:, lanes] = der.astype(BF16)


def project(chunk, index, place, tokens, norms, pack, tables, width, hidden, kept):
    model = pack.shape[0]
    return chunk_call(
        partial(project_body, len(chunk)),
        "project",
        3.5,
        index,
        [
            ((tokens, model), BF16, (TOKENS, model), ROWS),
            ((tokens, model), BF16, (TOKENS, model), ROWS),
            ((3, tokens, width), BF16, (3, TOKENS, width), lambda i: (0, i, 0)),
            ((width, tokens), BF16, (width, TOKENS), LANES),
            ((tokens, hidden), BF16, (TOKENS, hidden), ROWS),
            ((tokens, hidden), BF16, (TOKENS, hidden), ROWS),
        ],
        [(way, (TOKENS, model), HERE) for way in chunk]
        + [
            (norms, (4, model), HERE),
            (pack, (model, 3 * width), HERE),
            (pack, (model, hidden), lambda i: (0, 1)),
            (tables[0], (TOKENS, 128), ROWS),
            (tables[1], (TOKENS, 128), ROWS),
        ],
        kept,
        place,
    )


def own_lanes(values, head, factor=None):
    lane = lax.broadcasted_iota(jnp.int32, values.shape, 1) // HEAD_DIM
    if factor is not None:
        values = values * jnp.asarray(factor, values.dtype)
    return jnp.where(lane == head, values, jnp.zeros_like(values))


def attend_body(number, starts, qkv, value_t, active, wout, wdown, context, logsum, partial_sum):
    index = number[0]
    tokens, width = (qkv.shape[1], qkv.shape[2])
    reach = min(tokens, TOKENS + LONGEST_DOC)
    first = pl.multiple_of(jnp.maximum(index * TOKENS + TOKENS - reach, 0), TOKENS)
    at = pl.multiple_of(index * TOKENS, TOKENS)
    key_at = first + lax.broadcasted_iota(jnp.int32, (reach, TOKENS), 0)
    query_at = at + lax.broadcasted_iota(jnp.int32, (reach, TOKENS), 1)
    allowed = (key_at <= query_at) & (key_at >= starts[0:1, pl.ds(at, TOKENS)])
    outs, sums = ([], [])
    for pair in range(width // 128):
        lanes = slice(pair * 128, (pair + 1) * 128)
        keys = qkv[1, pl.ds(first, reach), lanes]
        queries = qkv[0, pl.ds(at, TOKENS), lanes]
        for head in range(128 // HEAD_DIM):
            query = own_lanes(queries, head, 1.0 / math.sqrt(HEAD_DIM))
            scores = jnp.where(allowed, mm_nt(keys, query), NEG_FILL)
            peak = jnp.max(scores, axis=0, keepdims=True)
            raised = jnp.exp(scores - peak)
            total = jnp.sum(raised, axis=0, keepdims=True)
            sums.append(peak + jnp.log(total))
            begin = pair * 128 + head * HEAD_DIM
            values = value_t[begin : begin + HEAD_DIM, pl.ds(first, reach)]
            outs.append(mm(values, raised.astype(BF16)) * (1.0 / total))
    mixed = jnp.concatenate(outs, axis=0).T.astype(BF16)
    context[...] = mixed
    for head, one in enumerate(sums):
        logsum[head : head + 1, :] = one
    partial_sum[...] = (mm_nt(mixed, wout[...]) + mm_nt(active[...], wdown[...])).astype(BF16)


def attend(index, starts, qkv, value_t, active, pack, kept):
    _, tokens, width = qkv.shape
    hidden = active.shape[1]
    model = pack.shape[0]
    heads = width // HEAD_DIM
    return chunk_call(
        attend_body,
        "attend",
        3,
        index,
        [
            ((tokens, width), BF16, (TOKENS, width), ROWS),
            ((heads, tokens), F32, (heads, TOKENS), LANES),
            ((TOKENS, model), BF16, (TOKENS, model), HERE),
        ],
        [
            (starts, (1, tokens), HERE),
            (qkv, (3, tokens, width), lambda i: (0, 0, 0)),
            (value_t, (width, tokens), HERE),
            (active, (TOKENS, hidden), ROWS),
            (pack, (model, width), lambda i: (0, 3)),
            (pack, (model, hidden), lambda i: (0, 2)),
        ],
        kept,
    )


def through_branch_body(ways, number, *refs):
    wout, wdown, slope, pre_grad, context_grad, copied = refs[ways:]
    grads = added(refs[:ways])
    keep_by_owner(copied, (number[1], number[2]), grads)
    pre_grad[...] = (mm(grads, wdown[...]) * slope[...].astype(F32)).astype(BF16)
    context_grad[...] = mm(grads, wout[...]).astype(BF16)


def through_branch(chunk, index, place, pack, slope, width, kept):
    tokens, hidden = slope.shape
    model = pack.shape[0]
    return chunk_call(
        partial(through_branch_body, len(chunk)),
        "through_branch",
        1.5,
        index,
        [
            ((tokens, hidden), BF16, (TOKENS, hidden), ROWS),
            ((tokens, width), BF16, (TOKENS, width), ROWS),
            ((tokens, model), BF16, (TOKENS, model), ROWS),
        ],
        [(way, (TOKENS, model), HERE) for way in chunk]
        + [
            (pack, (model, width), lambda i: (0, 3)),
            (pack, (model, hidden), lambda i: (0, 2)),
            (slope, (TOKENS, hidden), ROWS),
        ],
        kept,
        place,
    )


def window_of(block, size):
    return (max(0, block * size - LONGEST_DOC), (block + 1) * size)


def attend_back_kernel(starts, qkv, grads, logsum, cosine, sine, out, key_sum, value_sum):
    size = TOKENS
    factor = 1.0 / math.sqrt(HEAD_DIM)
    tokens = qkv.shape[1]
    heads = 128 // HEAD_DIM
    key_t = qkv[1].astype(F32).T.astype(BF16)
    key_sum[...] = jnp.zeros_like(key_sum)
    value_sum[...] = jnp.zeros_like(value_sum)
    for block in range(tokens // size):
        first, last = window_of(block, size)
        rows = slice(block * size, (block + 1) * size)
        shape = (last - first, size)
        key_at = first + lax.broadcasted_iota(jnp.int32, shape, 0)
        query_at = block * size + lax.broadcasted_iota(jnp.int32, shape, 1)
        allowed = (key_at <= query_at) & (key_at >= starts[0:1, rows])
        key_part, value_part, query_parts = (0.0, 0.0, [])
        for head in range(heads):
            query = own_lanes(qkv[0, rows], head, factor)
            grad = own_lanes(grads[rows], head)
            scores = jnp.where(allowed, mm_nt(qkv[1, first:last], query), NEG_FILL)
            probs = jnp.exp(scores - logsum[0, head : head + 1, rows])
            probs_grad = mm_nt(qkv[2, first:last], grad)
            inner = jnp.sum(probs_grad * probs, axis=0, keepdims=True)
            score_grad = (probs * (probs_grad - inner)).astype(BF16)
            key_part += mm(score_grad, query)
            value_part += mm(probs.astype(BF16), grad)
            query_parts.append(
                mm(key_t[head * HEAD_DIM : (head + 1) * HEAD_DIM, first:last], score_grad)
            )
        key_sum[first:last] += key_part
        value_sum[first:last] += value_part
        query_grad = jnp.concatenate(query_parts, axis=0).T * factor
        out[0, rows] = turn(query_grad, cosine[rows], sine[rows], -1.0).astype(BF16)
    out[1] = turn(key_sum[...], cosine[...], sine[...], -1.0).astype(BF16)
    out[2] = value_sum[...].astype(BF16)


def attend_back(starts, qkv, context_grad, logsum, tables):
    _, tokens, width = qkv.shape
    pairs = width // 128
    heads = 128 // HEAD_DIM
    return pl.pallas_call(
        attend_back_kernel,
        grid=(pairs,),
        in_specs=[
            pl.BlockSpec((1, tokens), lambda p: (0, 0)),
            pl.BlockSpec((3, tokens, 128), lambda p: (0, 0, p)),
            pl.BlockSpec((tokens, 128), lambda p: (0, p)),
            pl.BlockSpec((1, heads, tokens), lambda p: (p, 0, 0)),
            pl.BlockSpec((tokens, 128), lambda p: (0, 0)),
            pl.BlockSpec((tokens, 128), lambda p: (0, 0)),
        ],
        out_specs=pl.BlockSpec((3, tokens, 128), lambda p: (0, 0, p)),
        out_shape=jax.ShapeDtypeStruct((3, tokens, width), BF16),
        scratch_shapes=[pltpu.VMEM((tokens, 128), F32), pltpu.VMEM((tokens, 128), F32)],
        compiler_params=params(),
        cost_estimate=cost(11),
        name="attend_back",
    )(starts, qkv, context_grad, logsum.reshape(pairs, heads, tokens), *tables)


def through_inputs_body(ways, number, *refs):
    norms, project_grad, pre_grad, wqkv, wup, normed_grad, terms = refs[ways:]
    normed, _ = normalize(added(refs[:ways]))
    width = project_grad.shape[2]
    attn = mm_nt(project_grad[0], wqkv[:, :width])
    attn += mm_nt(project_grad[1], wqkv[:, width : 2 * width])
    attn += mm_nt(project_grad[2], wqkv[:, 2 * width :])
    feed = mm_nt(pre_grad[...], wup[...])
    normed_grad[...] = (attn * norms[0:1] + feed * norms[2:3]).astype(BF16)
    terms[0:1] = jnp.sum(attn * normed, axis=0, keepdims=True)
    terms[1:2] = jnp.sum(attn, axis=0, keepdims=True)
    terms[2:3] = jnp.sum(feed * normed, axis=0, keepdims=True)
    terms[3:4] = jnp.sum(feed, axis=0, keepdims=True)


def through_inputs(chunk, index, norms, project_grad, pre_grad, pack):
    model = pack.shape[0]
    hidden = pre_grad.shape[1]
    width = project_grad.shape[2]
    return chunk_call(
        partial(through_inputs_body, len(chunk)),
        "through_inputs",
        1.5,
        index,
        [
            ((TOKENS, model), BF16, (TOKENS, model), HERE),
            ((4, model), F32, (4, model), HERE),
        ],
        [(way, (TOKENS, model), HERE) for way in chunk]
        + [
            (norms, (4, model), HERE),
            (project_grad, (3, TOKENS, width), lambda i: (0, i, 0)),
            (pre_grad, (TOKENS, hidden), ROWS),
            (pack, (model, 3 * width), HERE),
            (pack, (model, hidden), lambda i: (0, 1)),
        ],
    )


def outer_kernel(attn_in, feed_in, upstream, project_grad, context, pre_grad, active, out):
    step = pl.program_id(0)

    def fill(left, right, start=0):
        width = right.shape[1]
        out[:, :, start : start + width] = (
            lax.dot_general(left[...], right, (((0,), (0,)), ((), ())), preferred_element_type=F32)
            .astype(BF16)
            .reshape(*out.shape[:2], width)
        )

    @pl.when(step == 0)
    def _():
        fill(attn_in, project_grad[0])
        fill(attn_in, project_grad[1], context.shape[1])

    @pl.when(step == 1)
    def _():
        fill(attn_in, project_grad[2])
        fill(upstream, context[...], context.shape[1])

    pl.when((step == 2) | (step == 3))(lambda: fill(feed_in, pre_grad[...]))
    pl.when(step >= 4)(lambda: fill(upstream, active[...]))


def weight_grads(half, saved, upstream, pre_grad, project_grad):
    attn_in, feed_in, active, context = saved
    tokens, model = attn_in.shape
    width = context.shape[1]
    left = pl.BlockSpec((tokens, model // 2), lambda j: (0, half))
    return pl.pallas_call(
        outer_kernel,
        grid=(6,),
        in_specs=[
            left,
            left,
            left,
            pl.BlockSpec((3, tokens, width), lambda j: (0, 0, 0)),
            pl.BlockSpec((tokens, width), lambda j: (0, 0)),
            pl.BlockSpec((tokens, 2 * width), lambda j: (0, jnp.clip(j - 2, 0, 1))),
            pl.BlockSpec((tokens, 2 * width), lambda j: (0, jnp.clip(j - 4, 0, 1))),
        ],
        out_specs=pl.BlockSpec((4, model // 8, 2 * width), lambda j: (0, 0, j)),
        out_shape=jax.ShapeDtypeStruct((4, model // 8, 12 * width), BF16),
        compiler_params=params(18),
        cost_estimate=cost(9),
        name="weight_grads",
    )(attn_in, feed_in, upstream, project_grad, context, pre_grad, active)


def fold_kernel(kept, came, side, ahead, rest):
    half = kept.shape[1] // 2
    both = (kept[...].astype(F32) + came[...].astype(F32)).astype(BF16)
    side[0] = both[1, :half]
    side[1] = both[3, :half]
    ahead[0] = both[2, half:]
    ahead[1] = both[3, half:]
    rest[0] = both[0, :half]
    rest[1] = both[2, :half]
    rest[2] = both[0, half:]
    rest[3] = both[1, half:]


def fold(kept, came):
    _, rows, width = kept.shape
    step = width // 6
    block = lambda n, r: pl.BlockSpec((n, r, step), lambda j: (0, 0, j))
    shape = lambda n: jax.ShapeDtypeStruct((n, rows // 2, width), BF16)
    return pl.pallas_call(
        fold_kernel,
        grid=(6,),
        in_specs=[block(4, rows), block(4, rows)],
        out_specs=[block(2, rows // 2), block(2, rows // 2), block(4, rows // 2)],
        out_shape=[shape(2), shape(2), shape(4)],
        compiler_params=params(),
        cost_estimate=cost(4),
        name="fold",
    )(kept, came)


def assemble_kernel(place, *refs):
    pieces, whole = (refs[:-1], refs[-1])
    rows = pieces[0].shape[0]
    each = len(pieces) // 2
    for order, piece in enumerate(pieces):
        core, number = (order // each, min(order % each, 3))
        at = ((place[1] ^ number) * 2 + (place[0] ^ core)) * rows
        at = at + (rows // 2 if order % each == 4 else 0)
        whole[pl.ds(pl.multiple_of(at, rows // 2), piece.shape[0]), :] = piece[...]


def assemble(place, pieces):
    rows, width = pieces[0].shape
    step = width // 6
    return pl.pallas_call(
        assemble_kernel,
        grid_spec=pltpu.PrefetchScalarGridSpec(
            num_scalar_prefetch=1,
            grid=(6,),
            in_specs=[pl.BlockSpec((piece.shape[0], step), lambda j, place: (0, j)) for piece in pieces],
            out_specs=pl.BlockSpec((8 * rows, step), lambda j, place: (0, j)),
        ),
        out_shape=jax.ShapeDtypeStruct((8 * rows, width), BF16),
        compiler_params=params(18),
        cost_estimate=cost(6),
        name="assemble",
    )(place, *pieces)


def unpack_kernel(place, upper, lower, came, qkv, out, up, down):
    width, hidden = (out.shape[0], up.shape[1])
    half = came.shape[0]
    own = jnp.concatenate([upper[...], lower[...]], axis=0)
    for core, block in ((place[0], own), (1 - place[0], came[...].astype(F32))):
        rows = pl.ds(pl.multiple_of(core * half, half), half)
        qkv[rows, :] = block[:, : 3 * width]
        out[:, rows] = block[:, 3 * width : 4 * width].T
        up[rows, :] = block[:, 4 * width : 4 * width + hidden]
        down[:, rows] = block[:, 4 * width + hidden :].T


def unpack(sec, upper, lower, came, width, hidden):
    half = came.shape[0]
    shapes = [(2 * half, 3 * width), (width, 2 * half), (2 * half, hidden), (hidden, 2 * half)]
    return pl.pallas_call(
        unpack_kernel,
        grid_spec=pltpu.PrefetchScalarGridSpec(
            num_scalar_prefetch=1,
            grid=(1,),
            in_specs=[
                pl.BlockSpec(array.shape, lambda i, place: (0, 0)) for array in (upper, lower, came)
            ],
            out_specs=[pl.BlockSpec(shape, lambda i, place: (0, 0)) for shape in shapes],
        ),
        out_shape=[jax.ShapeDtypeStruct(shape, F32) for shape in shapes],
        compiler_params=params(18),
        cost_estimate=cost(2),
        name="unpack",
    )(sec.reshape(1).astype(jnp.int32), upper, lower, came)


def swap(block, axis, bit):
    return lax.ppermute(block, axis, [(i, i ^ bit) for i in range(lax.axis_size(axis))])


def join(*values):
    flat, tree = jax.tree.flatten(values)
    return jax.tree.unflatten(tree, lax.optimization_barrier(tuple(flat)))


def sum_over(value, axis):
    others = [swap(value, axis, bit) for bit in range(1, lax.axis_size(axis))]
    return sum(others, start=value)


def pick(stack, index):
    return lax.dynamic_index_in_dim(stack, index, 0, keepdims=False)


def send_sides(half):
    return (swap(half, "col", 1), swap(half, "col", 2))


def send_corner(side, ahead):
    rows = side.shape[0] // 2
    return [swap(side[:rows], "col", 2), swap(ahead[rows:], "col", 1)]


def add(a, b):
    return a.astype(F32) + b.astype(F32)


def along_row(block, pairs):
    return lax.ppermute(block, "row", pairs)


ONE_OVER = [(0, 1), (1, 0), (2, 3), (3, 2)]
TWO_OVER = [(0, 2), (2, 0), (1, 3), (3, 1)]
MIDDLE = [(1, 2), (2, 1)]
OUTWARD = [(1, 0), (2, 3)]
INWARD = [(0, 1), (3, 2)]


def send_own(own):
    return (along_row(own, TWO_OVER), along_row(own, ONE_OVER))


def pass_on(own, far):
    return (along_row(far, OUTWARD), along_row(own, MIDDLE))


def send_last(share):
    return (along_row(share, INWARD), along_row(share, MIDDLE))


def send_sums(far, passed, near):
    return (along_row(add(far, passed).astype(BF16), TWO_OVER), along_row(near, ONE_OVER))


def fast_shards(
    hidden_in,
    doc_ids,
    qkv_weight,
    out_weight,
    up_weight,
    down_weight,
    attn_gain,
    attn_shift,
    mlp_gain,
    mlp_shift,
    out_cotangent,
):
    sec, row, col = (lax.axis_index("section"), lax.axis_index("row"), lax.axis_index("col"))
    cols, rows = (lax.axis_size("col"), lax.axis_size("row"))
    model = hidden_in.shape[3]
    tokens = doc_ids.shape[2]
    width = qkv_weight.shape[3]
    hidden = up_weight.shape[2]
    block = qkv_weight.shape[1]
    first = sec == 0
    x_own = pick(hidden_in[:, 0], sec)
    docs = pick(doc_ids[:, 0], sec)
    given = pick(out_cotangent[:, 0], sec)

    place = jnp.stack([sec, col]).astype(jnp.int32)
    share = attn_gain.shape[1]

    def enter(kept, chunk, number, layer):
        return project(
            chunk,
            row ^ number,
            place,
            tokens,
            norms[layer],
            packs[layer],
            tables,
            width,
            hidden,
            kept,
        )

    def leave(kept, entered, number, layer):
        _, _, qkv, value_t, active, _ = entered
        *kept, share_of = attend(row ^ number, starts, qkv, value_t, active, packs[layer], kept)
        return (tuple(kept), share_of)

    def back_branch(kept, chunk, number, slope, layer):
        return through_branch(chunk, row ^ number, place, packs[layer], slope, width, kept)

    def back_inputs(chunks, number, layer, project_grad, pre_grad):
        return through_inputs(
            chunks[number], row ^ number, norms[layer], project_grad, pre_grad, packs[layer]
        )

    def input_grad(total, own, own_grads):
        normed, scale = normalize(own)
        result = own_grads.astype(F32) + scale * (
            total
            - jnp.mean(total, axis=-1, keepdims=True)
            - normed * jnp.mean(total * normed, axis=-1, keepdims=True)
        )
        return result.astype(BF16)


    far_x0, near_x0 = send_own(x_own)
    vectors = jnp.stack([attn_gain[0], attn_shift[0], mlp_gain[0], mlp_shift[0]])
    norms = lax.dynamic_update_slice(
        jnp.zeros((2, 4, model), F32), vectors[None], (sec, 0, (row * cols + col) * share)
    )
    norms = sum_over(norms, "row")
    own_pack = jnp.concatenate(
        [
            qkv_weight[0].reshape(block, 3 * width),
            out_weight[0].T,
            up_weight[0],
            down_weight[0].T,
        ],
        axis=1,
    )
    half_of = lambda core: lax.dynamic_slice_in_dim(own_pack, core * (block // 2), block // 2)
    staying, leaving = (half_of(sec), half_of(1 - sec))
    norms, staying, leaving = join(norms, staying, leaving)

    came = swap(leaving, "section", 1)
    norms = sum_over(norms, "section")
    half0, half1 = (jnp.where(first, staying, came), jnp.where(first, came, staying))
    norms, half0, half1 = join(norms, half0, half1)

    norms = sum_over(norms, "col")
    norms, half0 = join(norms, half0)

    side0, ahead0 = send_sides(half0)
    starts = jnp.sum((docs[None, :] < docs[:, None]).astype(jnp.int32), axis=1)
    tables = rope_tables(docs, starts)
    starts = starts[None]
    half0, side0, ahead0, starts, tables, far_x0, near_x0 = join(
        half0, side0, ahead0, starts, tables, far_x0, near_x0
    )
    passed_x0, middle_x0 = pass_on(x_own, far_x0)
    chunks_x0 = [(x_own,), (near_x0,), (far_x0,), (middle_x0, passed_x0)]

    across0 = send_corner(side0, ahead0)
    mine = [half0, side0, ahead0]
    theirs = [swap(piece, "section", 1) for piece in mine]
    mine, theirs, across0 = join(mine, theirs, across0)

    theirs = theirs + [swap(piece, "section", 1) for piece in across0]
    mine, theirs, half1, given = join(mine + across0, theirs, half1, given)

    side1, ahead1 = send_sides(half1)
    packs = [assemble(place, mine + theirs), None]
    entered0 = ()
    for number in range(3):
        entered0 = enter(entered0, chunks_x0[number], number, 0)
    chunks_x0, entered0, packs, given = join(chunks_x0, entered0, packs, given)

    far_g1, near_g1 = send_own(given)
    entered0 = enter(entered0, chunks_x0[3], 3, 0)
    kept, last = leave((), entered0, 3, 0)
    side1, ahead1, entered0, kept, last = join(side1, ahead1, entered0, kept, last)

    passed_y0, middle_y0 = send_last(last)
    across1 = send_corner(side1, ahead1)
    kept, far = leave(kept, entered0, 2, 0)
    kept, near = leave(kept, entered0, 1, 0)
    (context0, logsum0), share_of = leave(kept, entered0, 0, 0)
    passed_y0, middle_y0, across1, far, near, share_of, context0, half1, side1, ahead1 = join(
        passed_y0, middle_y0, across1, far, near, share_of, context0, half1, side1, ahead1
    )

    far_y0, near_y0 = send_sums(far, passed_y0, near)
    mine = [half1, side1, ahead1] + across1
    theirs = [swap(piece, "section", 1) for piece in mine]
    far_y0, near_y0, mine, theirs, far_g1, near_g1 = join(
        far_y0, near_y0, mine, theirs, far_g1, near_g1
    )
    total = add(share_of, near_y0) + add(middle_y0, far_y0)
    y0_own = (x_own.astype(F32) + total).astype(BF16)

    far_x1, near_x1 = send_own(y0_own)
    packs[1] = assemble(place, mine + theirs)
    entered1 = enter((), (y0_own,), 0, 1)
    branch1 = back_branch((), (given,), 0, entered1[5], 1)
    far_x1, near_x1, entered1, branch1 = join(far_x1, near_x1, entered1, branch1)

    passed_x1, middle_x1 = pass_on(y0_own, far_x1)
    entered1 = enter(entered1, (near_x1,), 1, 1)
    branch1 = back_branch(branch1, (near_g1,), 1, entered1[5], 1)
    entered1 = enter(entered1, (far_x1,), 2, 1)
    branch1 = back_branch(branch1, (far_g1,), 2, entered1[5], 1)
    passed_x1, middle_x1, entered1, branch1, given, far_g1 = join(
        passed_x1, middle_x1, entered1, branch1, given, far_g1
    )

    chunks_x1 = [(y0_own,), (near_x1,), (far_x1,), (middle_x1, passed_x1)]
    passed_g1, middle_g1 = pass_on(given, far_g1)
    entered1 = enter(entered1, chunks_x1[3], 3, 1)
    kept, last_b1 = leave((), entered1, 3, 1)
    kept, far_b1 = leave(kept, entered1, 2, 1)
    kept, near_b1 = leave(kept, entered1, 1, 1)
    (context1, logsum1), share_b1 = leave(kept, entered1, 0, 1)
    passed_g1, middle_g1, last_b1, far_b1, near_b1, share_b1, context1, logsum1, entered1 = join(
        passed_g1, middle_g1, last_b1, far_b1, near_b1, share_b1, context1, logsum1, entered1
    )

    passed_y1, middle_y1 = send_last(last_b1)
    pre_grad1, context_grad1, grads1 = back_branch(
        branch1, (middle_g1, passed_g1), 3, entered1[5], 1
    )
    saved1 = (entered1[0], entered1[1], entered1[4], context1)
    project_grad1 = attend_back(starts, entered1[2], context_grad1, logsum1, tables)
    last, terms1 = back_inputs(chunks_x1, 3, 1, project_grad1, pre_grad1)
    last, terms1, project_grad1, pre_grad1, passed_y1, middle_y1 = join(
        last, terms1, project_grad1, pre_grad1, passed_y1, middle_y1
    )

    passed_n1, middle_n1 = send_last(last)
    others = [back_inputs(chunks_x1, number, 1, project_grad1, pre_grad1) for number in (2, 1, 0)]
    (far, near, share_of), terms = zip(*others)
    terms1 = sum(terms, start=terms1)
    leaving1 = weight_grads(1, saved1, grads1, pre_grad1, project_grad1)
    passed_n1, middle_n1, far, near, share_of, terms1, leaving1, project_grad1 = join(
        passed_n1, middle_n1, far, near, share_of, terms1, leaving1, project_grad1
    )

    far_n1, near_n1 = send_sums(far, passed_n1, near)
    came1 = swap(leaving1, "section", 1)
    kept1 = weight_grads(0, saved1, grads1, pre_grad1, project_grad1)
    far_n1, near_n1, came1, kept1 = join(far_n1, near_n1, came1, kept1)
    total = add(share_of, near_n1) + add(middle_n1, far_n1)
    dx1_own = input_grad(total, y0_own, given)

    slope0 = entered0[5]
    far_g0, near_g0 = send_own(dx1_own)
    branch0 = back_branch((), (dx1_own,), 0, slope0, 0)
    side1, ahead1, rest1 = fold(kept1, came1)
    far_g0, near_g0, branch0, side1, ahead1, rest1 = join(
        far_g0, near_g0, branch0, side1, ahead1, rest1
    )

    passed_g0, middle_g0 = pass_on(dx1_own, far_g0)
    first1, second1 = (swap(side1, "col", 1), swap(ahead1, "col", 2))
    branch0 = back_branch(branch0, (near_g0,), 1, slope0, 0)
    branch0 = back_branch(branch0, (far_g0,), 2, slope0, 0)
    far_b1 = add(far_b1, passed_y1).astype(BF16)
    passed_g0, middle_g0, branch0, far_b1, near_b1 = join(
        passed_g0, middle_g0, branch0, far_b1, near_b1
    )

    near_y1 = along_row(near_b1, ONE_OVER)
    pre_grad0, context_grad0, grads0 = back_branch(branch0, (middle_g0, passed_g0), 3, slope0, 0)
    saved0 = (entered0[0], entered0[1], entered0[4], context0)
    project_grad0 = attend_back(starts, entered0[2], context_grad0, logsum0, tables)
    last, terms0 = back_inputs(chunks_x0, 3, 0, project_grad0, pre_grad0)
    last, terms0, project_grad0, near_y1, first1, second1 = join(
        last, terms0, project_grad0, near_y1, first1, second1
    )

    passed_n0, middle_n0 = send_last(last)
    passed1 = (
        swap(add(rest1[1], first1[1]).astype(BF16), "col", 2),
        swap(add(rest1[3], second1[1]).astype(BF16), "col", 1),
    )
    leaving0 = weight_grads(1, saved0, grads0, pre_grad0, project_grad0)
    others = [back_inputs(chunks_x0, number, 0, project_grad0, pre_grad0) for number in (2, 1, 0)]
    (far, near, share_of), terms = zip(*others)
    terms = jnp.stack([sum(terms, start=terms0), terms1])
    passed_n0, middle_n0, far, near, share_of, terms, leaving0, project_grad0, passed1 = join(
        passed_n0, middle_n0, far, near, share_of, terms, leaving0, project_grad0, passed1
    )

    far_n0, near_n0 = send_sums(far, passed_n0, near)
    came0 = swap(leaving0, "section", 1)
    terms = sum_over(terms, "section")
    kept0 = weight_grads(0, saved0, grads0, pre_grad0, project_grad0)
    came0, kept0, terms = join(came0, kept0, terms)

    side0, ahead0, rest0 = fold(kept0, came0)
    terms = sum_over(terms, "col")
    side0, ahead0, rest0, terms, far_b1 = join(side0, ahead0, rest0, terms, far_b1)

    first0, second0 = (swap(side0, "col", 1), swap(ahead0, "col", 2))
    far_y1 = along_row(far_b1, TWO_OVER)
    first0, second0, far_n0, near_n0, terms = join(first0, second0, far_n0, near_n0, terms)

    passed0 = (
        swap(add(rest0[1], first0[1]).astype(BF16), "col", 2),
        swap(add(rest0[3], second0[1]).astype(BF16), "col", 1),
    )
    terms = sum_over(terms, "row")
    total = add(share_b1, near_y1) + add(middle_y1, far_y1)
    y1_own = (y0_own.astype(F32) + total).astype(BF16)
    total = add(share_of, near_n0) + add(middle_n0, far_n0)
    dx0_own = input_grad(total, x_own, dx1_own)
    sums1 = (
        add(add(rest1[0], first1[0]), passed1[0]),
        add(add(rest1[2], second1[0]), passed1[1]),
    )
    sums0 = (
        add(add(rest0[0], first0[0]), passed0[0]),
        add(add(rest0[2], second0[0]), passed0[1]),
    )

    choose = lambda here, there: jnp.where(first, here, there)
    leaving = jnp.concatenate([choose(b, a) for a, b in zip(sums0, sums1)]).astype(BF16)
    upper, lower = [choose(a, b) for a, b in zip(sums0, sums1)]
    qkv_grad, out_grad, up_grad, down_grad = unpack(
        sec, upper, lower, swap(leaving, "section", 1), width, hidden
    )
    terms = pick(terms, sec)
    terms = lax.dynamic_slice_in_dim(terms, (row * cols + col) * share, share, 1)

    def by_layer(zero, one):
        away = swap(choose(one, zero), "section", 1)
        here = choose(zero, one)
        return jnp.stack([choose(here, away), choose(away, here)])

    return (
        by_layer(y0_own, y1_own)[None, :, None],
        by_layer(dx0_own, dx1_own)[None, :, None],
        qkv_grad.reshape(1, block, 3, width),
        out_grad[None],
        up_grad[None],
        down_grad[None],
        terms[None, 0],
        terms[None, 1],
        terms[None, 2],
        terms[None, 3],
    )


def from_behind(block, axis, distance):
    devices = range(lax.axis_size(axis))
    route = [(i - distance, i) for i in devices if i - distance in devices]
    return lax.ppermute(block, axis, route)


def positions_of(docs):
    length = docs.shape[0]
    index = jnp.arange(length, dtype=jnp.int32)
    starts = jnp.concatenate([jnp.ones((1,), jnp.bool_), docs[1:] != docs[:-1]])
    first = lax.cummax(jnp.where(starts, index, 0), axis=0)
    return index - first


def rotary_tables(docs):
    half = ROT // 2
    freqs = 10000.0 ** (-2.0 * jnp.arange(half, dtype=jnp.float32) / ROT)
    angles = positions_of(docs).astype(jnp.float32)[:, None] * freqs[None, :]
    return (jnp.cos(angles)[:, None, :], jnp.sin(angles)[:, None, :])


def rotate(values, cosine, sine):
    half = ROT // 2
    front = values[..., :half]
    back = values[..., half:ROT]
    return jnp.concatenate(
        [front * cosine - back * sine, back * cosine + front * sine, values[..., ROT:]], axis=-1
    )


def rotate_back(grads, cosine, sine):
    half = ROT // 2
    front = grads[..., :half]
    back = grads[..., half:ROT]
    return jnp.concatenate(
        [front * cosine + back * sine, back * cosine - front * sine, grads[..., ROT:]], axis=-1
    )


def block_mask(docs, start, size):
    rows = start + jnp.arange(size, dtype=jnp.int32)
    cols = jnp.arange(docs.shape[0], dtype=jnp.int32)
    row_docs = lax.dynamic_slice_in_dim(docs, start, size)
    return (row_docs[:, None] == docs[None, :]) & (cols[None, :] <= rows[:, None])


def block_scores(query, key, docs, start, block):
    factor = 1.0 / math.sqrt(query.shape[2])
    rows = lax.dynamic_slice_in_dim(query, start, block)
    scores = jnp.einsum("qhd,khd->hqk", rows, key, preferred_element_type=jnp.float32) * factor
    allowed = block_mask(docs, start, block)[None]
    return (rows, jnp.where(allowed, scores, NEG_FILL))


def attend_forward(query, key, value, docs):
    length, heads, width = query.shape
    block = min(512, length)

    def one_block(number):
        start = number * block
        rows, scores = block_scores(query, key, docs, start, block)
        peak = jnp.max(scores, axis=-1, keepdims=True)
        raised = jnp.exp(scores - peak)
        total = jnp.sum(raised, axis=-1, keepdims=True)
        probs = (raised / total).astype(jnp.bfloat16)
        context = jnp.einsum(
            "hqk,khd->qhd", probs, value, preferred_element_type=jnp.float32
        ).astype(jnp.bfloat16)
        return (context, (peak + jnp.log(total))[..., 0])

    context, logsum = lax.map(one_block, jnp.arange(length // block, dtype=jnp.int32))
    return (context.reshape(length, heads, width), logsum)


def attend_backward(query, key, value, docs, logsum, context_grad):
    length, heads, width = query.shape
    block = min(512, length)
    factor = 1.0 / math.sqrt(width)

    def one_block(carry, inputs):
        key_grad, value_grad = carry
        number, block_logsum = inputs
        start = number * block
        rows, scores = block_scores(query, key, docs, start, block)
        rows_grad = lax.dynamic_slice_in_dim(context_grad, start, block)
        probs_full = jnp.exp(scores - block_logsum[:, :, None])
        probs = probs_full.astype(jnp.bfloat16)
        context = jnp.einsum(
            "hqk,khd->qhd", probs, value, preferred_element_type=jnp.float32
        ).astype(jnp.bfloat16)
        probs_grad = jnp.einsum(
            "qhd,khd->hqk", rows_grad, value, preferred_element_type=jnp.float32
        )
        inner = jnp.sum(probs_grad * probs_full, axis=-1, keepdims=True)
        score_grad = (probs_full * (probs_grad - inner)).astype(jnp.bfloat16)
        query_grad = (
            jnp.einsum("hqk,khd->qhd", score_grad, key, preferred_element_type=jnp.float32) * factor
        )
        key_grad = (
            key_grad
            + jnp.einsum("hqk,qhd->khd", score_grad, rows, preferred_element_type=jnp.float32)
            * factor
        )
        value_grad = value_grad + jnp.einsum(
            "hqk,qhd->khd", probs, rows_grad, preferred_element_type=jnp.float32
        )
        return ((key_grad, value_grad), (context, query_grad))

    zeros = jnp.zeros((length, heads, width), jnp.float32)
    numbers = jnp.arange(length // block, dtype=jnp.int32)
    (key_grad, value_grad), (context, query_grad) = lax.scan(
        one_block, (zeros, zeros), (numbers, logsum)
    )
    return (
        context.reshape(length, heads * width),
        query_grad.reshape(length, heads, width),
        key_grad,
        value_grad,
    )


def gather_features(shard):
    return lax.all_gather(shard, "row", axis=0, tiled=True)


def recompute_inputs(full, docs, norms, weights):
    gain_a, shift_a, gain_m, shift_m = norms
    qkv_full = weights[0]
    normed, scale = normalize(full)
    attn_in = (normed * gain_a + shift_a).astype(jnp.bfloat16)
    feed_in = (normed * gain_m + shift_m).astype(jnp.bfloat16)
    length = full.shape[0]
    heads_here = qkv_full.shape[2] // HEAD_DIM
    project = jnp.einsum("td,dke->tke", attn_in, qkv_full, preferred_element_type=jnp.float32)
    cosine, sine = rotary_tables(docs)
    query = rotate(project[:, 0].reshape(length, heads_here, HEAD_DIM), cosine, sine).astype(
        jnp.bfloat16
    )
    key = rotate(project[:, 1].reshape(length, heads_here, HEAD_DIM), cosine, sine).astype(
        jnp.bfloat16
    )
    value = project[:, 2].reshape(length, heads_here, HEAD_DIM).astype(jnp.bfloat16)
    pre = jnp.dot(feed_in, weights[2], preferred_element_type=jnp.float32)
    return (normed, scale, attn_in, feed_in, query, key, value, pre, cosine, sine)


def layer_forward(shard, docs, full, norms, weights):
    normed, scale, attn_in, feed_in, query, key, value, pre, cosine, sine = recompute_inputs(
        full, docs, norms, weights
    )
    length = full.shape[0]
    context, logsum = attend_forward(query, key, value, docs)
    active = jax.nn.gelu(pre, approximate=False).astype(jnp.bfloat16)
    partial_sum = jnp.dot(
        context.reshape(length, -1), weights[1], preferred_element_type=jnp.float32
    )
    partial_sum = partial_sum + jnp.dot(active, weights[3], preferred_element_type=jnp.float32)
    branch = lax.psum_scatter(
        partial_sum.astype(jnp.bfloat16), "row", scatter_dimension=0, tiled=True
    ).astype(jnp.float32)
    return ((shard.astype(jnp.float32) + branch).astype(jnp.bfloat16), logsum)


def layer_backward(docs, full, logsum, upstream, norms, weights):
    gain_a, shift_a, gain_m, shift_m = norms
    qkv_full, out_full, up_full, down_full = weights
    normed, scale, attn_in, feed_in, query, key, value, pre, cosine, sine = recompute_inputs(
        full, docs, norms, weights
    )
    length = full.shape[0]
    heads_here = query.shape[1]
    active = jax.nn.gelu(pre, approximate=False).astype(jnp.bfloat16)
    upstream_full = lax.all_gather(upstream, "row", axis=0, tiled=True)
    down_part = jnp.einsum("tf,td->fd", active, upstream_full, preferred_element_type=jnp.float32)
    act_grad = jnp.einsum("td,fd->tf", upstream_full, down_full, preferred_element_type=jnp.float32)
    pre_grad = jax.vjp(partial(jax.nn.gelu, approximate=False), pre)[1](act_grad)[0].astype(
        jnp.bfloat16
    )
    up_part = jnp.einsum("td,tf->df", feed_in, pre_grad, preferred_element_type=jnp.float32)
    feed_grad = jnp.einsum("tf,df->td", pre_grad, up_full, preferred_element_type=jnp.float32)
    context_grad = jnp.einsum(
        "td,ed->te", upstream_full, out_full, preferred_element_type=jnp.float32
    ).astype(jnp.bfloat16)
    context_grad = context_grad.reshape(length, heads_here, HEAD_DIM)
    context, query_grad, key_grad, value_grad = attend_backward(
        query, key, value, docs, logsum, context_grad
    )
    out_part = jnp.einsum("te,td->ed", context, upstream_full, preferred_element_type=jnp.float32)
    project_grad = jnp.stack(
        [
            rotate_back(query_grad, cosine, sine).reshape(length, -1),
            rotate_back(key_grad, cosine, sine).reshape(length, -1),
            value_grad.reshape(length, -1),
        ],
        axis=1,
    ).astype(jnp.bfloat16)
    qkv_part = jnp.einsum("td,tke->dke", attn_in, project_grad, preferred_element_type=jnp.float32)
    attn_grad = jnp.einsum(
        "tke,dke->td", project_grad, qkv_full, preferred_element_type=jnp.float32
    )
    own_rows = upstream.shape[0]
    offset = lax.axis_index("row") * own_rows
    normed_part = lax.dynamic_slice_in_dim(normed, offset, own_rows, 0)
    scale_part = lax.dynamic_slice_in_dim(scale, offset, own_rows, 0)
    attn_piece, feed_piece = (
        lax.psum_scatter(
            attn_grad.astype(jnp.bfloat16), "row", scatter_dimension=0, tiled=True
        ).astype(jnp.float32),
        lax.psum_scatter(
            feed_grad.astype(jnp.bfloat16), "row", scatter_dimension=0, tiled=True
        ).astype(jnp.float32),
    )
    normed_grad = attn_piece * gain_a + feed_piece * gain_m
    gain_terms = (
        jnp.sum(attn_piece * normed_part, axis=0),
        jnp.sum(attn_piece, axis=0),
        jnp.sum(feed_piece * normed_part, axis=0),
        jnp.sum(feed_piece, axis=0),
    )
    row_sum = jnp.sum(normed_grad, axis=-1)
    cross_sum = jnp.sum(normed_grad * normed_part, axis=-1)
    count = full.shape[1]
    input_grad = upstream.astype(jnp.float32) + scale_part * (
        normed_grad - row_sum[:, None] / count - normed_part * cross_sum[:, None] / count
    )
    return (input_grad, (qkv_part, out_part, up_part, down_part), gain_terms)


def general_shards(
    hidden_in,
    doc_ids,
    qkv_weight,
    out_weight,
    up_weight,
    down_weight,
    attn_gain,
    attn_shift,
    mlp_gain,
    mlp_shift,
    out_cotangent,
):
    micro = hidden_in.shape[0]
    first_section = lax.axis_index("section") == 0
    norms = (
        lax.all_gather(attn_gain[0], ("row", "col"), axis=0, tiled=True),
        lax.all_gather(attn_shift[0], ("row", "col"), axis=0, tiled=True),
        lax.all_gather(mlp_gain[0], ("row", "col"), axis=0, tiled=True),
        lax.all_gather(mlp_shift[0], ("row", "col"), axis=0, tiled=True),
    )
    weights = (
        lax.all_gather(qkv_weight[0], "col", axis=0, tiled=True),
        lax.all_gather(out_weight[0], "col", axis=1, tiled=True),
        lax.all_gather(up_weight[0], "col", axis=0, tiled=True),
        lax.all_gather(down_weight[0], "col", axis=1, tiled=True),
    )
    received = jnp.zeros_like(hidden_in[0, 0])
    tick_inputs, tick_docs, tick_fulls, tick_outputs, tick_logsums = ([], [], [], [], [])
    for tick in range(micro + 1):
        own = hidden_in[min(tick, micro - 1), 0]
        shard = jnp.where(first_section, own, received)
        docs = jnp.where(
            first_section, doc_ids[min(tick, micro - 1), 0], doc_ids[max(tick - 1, 0), 0]
        )
        full = gather_features(shard)
        result, logsum = layer_forward(shard, docs, full, norms, weights)
        tick_inputs.append(shard)
        tick_docs.append(docs)
        tick_fulls.append(full)
        tick_outputs.append(result)
        tick_logsums.append(logsum)
        if tick < micro:
            received = from_behind(result, "section", 1)
    outputs = jnp.stack(
        [
            jnp.where(first_section, tick_outputs[number], tick_outputs[number + 1])
            for number in range(micro)
        ]
    )
    received = jnp.zeros_like(hidden_in[0, 0])
    matrix_totals = None
    gain_totals = None
    tick_grads = []
    for tick in range(micro + 1):
        early = max(tick - 1, 0)
        later = min(tick + 1, micro)
        if tick < micro:
            given = out_cotangent[tick, 0]
        else:
            given = jnp.zeros_like(out_cotangent[0, 0])
        upstream = jnp.where(first_section, received, given)
        shard = jnp.where(first_section, tick_inputs[early], tick_inputs[later])
        docs = jnp.where(first_section, tick_docs[early], tick_docs[later])
        logsum = jnp.where(first_section, tick_logsums[early], tick_logsums[later])
        full = gather_features(shard)
        input_grad, matrices, gain_terms = layer_backward(
            docs, full, logsum, upstream, norms, weights
        )
        if matrix_totals is None:
            matrix_totals = matrices
            gain_totals = gain_terms
        else:
            matrix_totals = jax.tree.map(jnp.add, matrix_totals, matrices)
            gain_totals = jax.tree.map(jnp.add, gain_totals, gain_terms)
        grad_low = input_grad.astype(jnp.bfloat16)
        tick_grads.append(grad_low)
        if tick < micro:
            received = from_behind(grad_low, "section", -1)
    grads_in = jnp.stack(
        [
            jnp.where(first_section, tick_grads[number + 1], tick_grads[number])
            for number in range(micro)
        ]
    )
    qkv_sum, out_sum, up_sum, down_sum = matrix_totals
    gain_a_sum, shift_a_sum, gain_m_sum, shift_m_sum = gain_totals
    qkv_total, out_total, up_total, down_total = (
        lax.psum_scatter(
            qkv_sum.astype(jnp.bfloat16), "col", scatter_dimension=0, tiled=True
        ).astype(jnp.float32),
        lax.psum_scatter(
            out_sum.astype(jnp.bfloat16), "col", scatter_dimension=1, tiled=True
        ).astype(jnp.float32),
        lax.psum_scatter(
            up_sum.astype(jnp.bfloat16), "col", scatter_dimension=0, tiled=True
        ).astype(jnp.float32),
        lax.psum_scatter(
            down_sum.astype(jnp.bfloat16), "col", scatter_dimension=1, tiled=True
        ).astype(jnp.float32),
    )
    gain_a_total, shift_a_total, gain_m_total, shift_m_total = (
        lax.psum_scatter(gain_a_sum, ("row", "col"), scatter_dimension=0, tiled=True),
        lax.psum_scatter(shift_a_sum, ("row", "col"), scatter_dimension=0, tiled=True),
        lax.psum_scatter(gain_m_sum, ("row", "col"), scatter_dimension=0, tiled=True),
        lax.psum_scatter(shift_m_sum, ("row", "col"), scatter_dimension=0, tiled=True),
    )
    return (
        outputs[None, :, None],
        grads_in[None, :, None],
        qkv_total[None],
        out_total[None],
        up_total[None],
        down_total[None],
        gain_a_total[None],
        shift_a_total[None],
        gain_m_total[None],
        shift_m_total[None],
    )


def shards(*arrays):
    hidden_in, qkv_weight, up_weight = (arrays[0], arrays[2], arrays[4])
    micro, seqs, own_tokens, model = hidden_in.shape
    width, hidden = (qkv_weight.shape[3], up_weight.shape[2])
    sizes = tuple(lax.axis_size(axis) for axis in ("section", "row", "col"))
    fits = (
        sizes == (2, 4, 4) and (micro, seqs) == (2, 1)
        and own_tokens == TOKENS
        and width % 128 == 0
        and 4 * width == hidden
    )
    return fast_shards(*arrays) if fits else general_shards(*arrays)


def solution(mesh):
    placed = (
        P(None, "col", "row", None),
        P(None, "col", None),
        P("section", "col", None, "row"),
        P("section", "row", "col"),
        P("section", "col", "row"),
        P("section", "row", "col"),
        P("section", ("row", "col")),
        P("section", ("row", "col")),
        P("section", ("row", "col")),
        P("section", ("row", "col")),
        P(None, "col", "row", None),
    )
    return jax.shard_map(
        shards,
        mesh=mesh,
        in_specs=placed,
        out_specs=(
            P("section", None, "col", "row", None),
            P("section", None, "col", "row", None),
            P("section", "col", None, "row"),
            P("section", "row", "col"),
            P("section", "col", "row"),
            P("section", "row", "col"),
            P("section", ("row", "col")),
            P("section", ("row", "col")),
            P("section", ("row", "col")),
            P("section", ("row", "col")),
        ),
        check_vma=False,
    )
```

```python
from functools import partial
import math

import jax
import jax.numpy as jnp
from jax import lax
from jax.experimental import pallas as pl
from jax.experimental.pallas import tpu as pltpu
from jax.sharding import PartitionSpec as P

HEAD_DIM = 64
ROT = 16
EPSILON = 1e-05
NEG_FILL = -1e30
BF16 = jnp.bfloat16
F32 = jnp.float32
TOKENS = 256
LONGEST_DOC = 512


def mm(a, b):
    return lax.dot_general(a, b, (((1,), (0,)), ((), ())), preferred_element_type=F32)


def mm_nt(a, b):
    return lax.dot_general(a, b, (((1,), (1,)), ((), ())), preferred_element_type=F32)


def normalize(full):
    wide = full.astype(F32)
    center = wide - jnp.mean(wide, axis=-1, keepdims=True)
    scale = lax.rsqrt(jnp.mean(center * center, axis=-1, keepdims=True) + EPSILON)
    return (center * scale, scale)


ERFC = (
    0.17087277,
    -0.82215223,
    1.48851587,
    -1.13520398,
    0.27886807,
    -0.18628806,
    0.09678418,
    0.37409196,
    1.00002368,
    -1.26551223,
)


def gelu_and_slope(pre):
    size = jnp.abs(pre) * math.sqrt(0.5)
    t = 1.0 / (1.0 + 0.5 * size)
    poly = jnp.full_like(t, ERFC[0])
    for coefficient in ERFC[1:]:
        poly = poly * t + coefficient
    bell = jnp.exp(-(size * size))
    tail = (0.5 * t) * (bell * jnp.exp(poly))
    below = jnp.where(pre >= 0, 1.0 - tail, tail)
    return (pre * below, below + pre * (bell * (1.0 / math.sqrt(2.0 * math.pi))))


def turn(values, cosine, sine, sign):
    width = values.shape[-1]
    half = ROT // 2
    lane = lax.broadcasted_iota(jnp.int32, values.shape, 1) % HEAD_DIM
    other = jnp.where(
        lane < half, -pltpu.roll(values, width - half, 1), pltpu.roll(values, half, 1)
    )
    return values * cosine + (sign * other) * sine


def rope_tables(docs, starts):
    half = ROT // 2
    lane = jnp.arange(128, dtype=jnp.int32) % HEAD_DIM
    freqs = 10000.0 ** (-2.0 * (lane % half).astype(F32) / ROT)
    position = (jnp.arange(docs.shape[0], dtype=jnp.int32) - starts).astype(F32)
    angles = position[:, None] * freqs[None, :]
    rotated = (lane < ROT)[None, :]
    return (jnp.where(rotated, jnp.cos(angles), 1.0), jnp.where(rotated, jnp.sin(angles), 0.0))


def params(mib=18):
    return pltpu.CompilerParams(vmem_limit_bytes=mib << 20)


def cost(us):
    return pl.CostEstimate(flops=int(us * 1.1e+09), bytes_accessed=int(us * 3.2e+06), transcendentals=0)


def chunk_call(body, name, us, index, outs, inputs, kept=(), place=None):
    given = len(inputs)
    number = index.reshape(1).astype(jnp.int32)
    if place is not None:
        number = jnp.concatenate([number, place])

    def kernel(number, *refs):
        body(number, *refs[:given], *refs[given + len(kept) :])

    spec = lambda block, at: pl.BlockSpec(block, lambda i, number: at(number[0]))
    return pl.pallas_call(
        kernel,
        grid_spec=pltpu.PrefetchScalarGridSpec(
            num_scalar_prefetch=1,
            grid=(1,),
            in_specs=[spec(block, at) for _, block, at in inputs]
            + [pl.BlockSpec(memory_space=pl.ANY) for _ in kept],
            out_specs=[spec(block, at) for _, _, block, at in outs],
        ),
        out_shape=[jax.ShapeDtypeStruct(shape, dtype) for shape, dtype, _, _ in outs],
        input_output_aliases={1 + given + i: i for i in range(len(kept))},
        compiler_params=params(),
        cost_estimate=cost(us),
        name=name,
    )(number, *[array for array, _, _ in inputs], *kept)


HERE = lambda i: (0, 0)
ROWS = lambda i: (i, 0)
LANES = lambda i: (0, i)


def added(refs):
    whole = refs[0][...]
    for ref in refs[1:]:
        whole = whole + ref[...]
    return whole


def keep_by_owner(kept, place, values):
    blocks = values.shape[1] // 128
    for block in range(blocks):
        at = (place[0] ^ (block % 2)) * (blocks // 2) + (place[1] ^ (block // 2))
        lanes = pl.ds(pl.multiple_of(at * 128, 128), 128)
        kept[:, lanes] = values[:, block * 128 : (block + 1) * 128]


def project_body(ways, number, *refs):
    norms, wqkv, wup, cosine, sine, attn_in, feed_in, qkv, value_t, active, slope = refs[ways:]
    normed, _ = normalize(added(refs[:ways]))
    attn = (normed * norms[0:1] + norms[1:2]).astype(BF16)
    feed = (normed * norms[2:3] + norms[3:4]).astype(BF16)
    place = (number[1], number[2])
    keep_by_owner(attn_in, place, attn)
    keep_by_owner(feed_in, place, feed)
    width = qkv.shape[2]
    for part in range(3):
        piece = mm(attn, wqkv[:, part * width : (part + 1) * width])
        for pair in range(width // 128):
            lanes = slice(pair * 128, (pair + 1) * 128)
            one = piece[:, lanes]
            if part < 2:
                one = turn(one, cosine[...], sine[...], 1.0)
            else:
                value_t[lanes, :] = one.T.astype(BF16)
            qkv[part, :, lanes] = one.astype(BF16)
    hidden = wup.shape[1]
    for start in range(0, hidden, 256):
        lanes = slice(start, start + 256)
        act, der = gelu_and_slope(mm(feed, wup[:, lanes]))
        active[:, lanes] = act.astype(BF16)
        slope[:, lanes] = der.astype(BF16)


def project(chunk, index, place, tokens, norms, pack, tables, width, hidden, kept):
    model = pack.shape[0]
    return chunk_call(
        partial(project_body, len(chunk)),
        "project",
        3.5,
        index,
        [
            ((tokens, model), BF16, (TOKENS, model), ROWS),
            ((tokens, model), BF16, (TOKENS, model), ROWS),
            ((3, tokens, width), BF16, (3, TOKENS, width), lambda i: (0, i, 0)),
            ((width, tokens), BF16, (width, TOKENS), LANES),
            ((tokens, hidden), BF16, (TOKENS, hidden), ROWS),
            ((tokens, hidden), BF16, (TOKENS, hidden), ROWS),
        ],
        [(way, (TOKENS, model), HERE) for way in chunk]
        + [
            (norms, (4, model), HERE),
            (pack, (model, 3 * width), HERE),
            (pack, (model, hidden), lambda i: (0, 1)),
            (tables[0], (TOKENS, 128), ROWS),
            (tables[1], (TOKENS, 128), ROWS),
        ],
        kept,
        place,
    )


def own_lanes(values, head, factor=None):
    lane = lax.broadcasted_iota(jnp.int32, values.shape, 1) // HEAD_DIM
    if factor is not None:
        values = values * jnp.asarray(factor, values.dtype)
    return jnp.where(lane == head, values, jnp.zeros_like(values))


def attend_body(number, starts, qkv, value_t, active, wout, wdown, context, logsum, partial_sum):
    index = number[0]
    tokens, width = (qkv.shape[1], qkv.shape[2])
    reach = min(tokens, TOKENS + LONGEST_DOC)
    first = pl.multiple_of(jnp.maximum(index * TOKENS + TOKENS - reach, 0), TOKENS)
    at = pl.multiple_of(index * TOKENS, TOKENS)
    key_at = first + lax.broadcasted_iota(jnp.int32, (reach, TOKENS), 0)
    query_at = at + lax.broadcasted_iota(jnp.int32, (reach, TOKENS), 1)
    allowed = (key_at <= query_at) & (key_at >= starts[0:1, pl.ds(at, TOKENS)])
    outs, sums = ([], [])
    for pair in range(width // 128):
        lanes = slice(pair * 128, (pair + 1) * 128)
        keys = qkv[1, pl.ds(first, reach), lanes]
        queries = qkv[0, pl.ds(at, TOKENS), lanes]
        for head in range(128 // HEAD_DIM):
            query = own_lanes(queries, head, 1.0 / math.sqrt(HEAD_DIM))
            scores = jnp.where(allowed, mm_nt(keys, query), NEG_FILL)
            peak = jnp.max(scores, axis=0, keepdims=True)
            raised = jnp.exp(scores - peak)
            total = jnp.sum(raised, axis=0, keepdims=True)
            sums.append(peak + jnp.log(total))
            begin = pair * 128 + head * HEAD_DIM
            values = value_t[begin : begin + HEAD_DIM, pl.ds(first, reach)]
            outs.append(mm(values, raised.astype(BF16)) * (1.0 / total))
    mixed = jnp.concatenate(outs, axis=0).T.astype(BF16)
    context[...] = mixed
    for head, one in enumerate(sums):
        logsum[head : head + 1, :] = one
    partial_sum[...] = (mm_nt(mixed, wout[...]) + mm_nt(active[...], wdown[...])).astype(BF16)


def attend(index, starts, qkv, value_t, active, pack, kept):
    _, tokens, width = qkv.shape
    hidden = active.shape[1]
    model = pack.shape[0]
    heads = width // HEAD_DIM
    return chunk_call(
        attend_body,
        "attend",
        3,
        index,
        [
            ((tokens, width), BF16, (TOKENS, width), ROWS),
            ((heads, tokens), F32, (heads, TOKENS), LANES),
            ((TOKENS, model), BF16, (TOKENS, model), HERE),
        ],
        [
            (starts, (1, tokens), HERE),
            (qkv, (3, tokens, width), lambda i: (0, 0, 0)),
            (value_t, (width, tokens), HERE),
            (active, (TOKENS, hidden), ROWS),
            (pack, (model, width), lambda i: (0, 3)),
            (pack, (model, hidden), lambda i: (0, 2)),
        ],
        kept,
    )


def through_branch_body(ways, number, *refs):
    wout, wdown, slope, pre_grad, context_grad, copied = refs[ways:]
    grads = added(refs[:ways])
    keep_by_owner(copied, (number[1], number[2]), grads)
    pre_grad[...] = (mm(grads, wdown[...]) * slope[...].astype(F32)).astype(BF16)
    context_grad[...] = mm(grads, wout[...]).astype(BF16)


def through_branch(chunk, index, place, pack, slope, width, kept):
    tokens, hidden = slope.shape
    model = pack.shape[0]
    return chunk_call(
        partial(through_branch_body, len(chunk)),
        "through_branch",
        1.5,
        index,
        [
            ((tokens, hidden), BF16, (TOKENS, hidden), ROWS),
            ((tokens, width), BF16, (TOKENS, width), ROWS),
            ((tokens, model), BF16, (TOKENS, model), ROWS),
        ],
        [(way, (TOKENS, model), HERE) for way in chunk]
        + [
            (pack, (model, width), lambda i: (0, 3)),
            (pack, (model, hidden), lambda i: (0, 2)),
            (slope, (TOKENS, hidden), ROWS),
        ],
        kept,
        place,
    )


def window_of(block, size):
    return (max(0, block * size - LONGEST_DOC), (block + 1) * size)


def attend_back_kernel(starts, qkv, grads, logsum, cosine, sine, out, key_sum, value_sum):
    size = TOKENS
    factor = 1.0 / math.sqrt(HEAD_DIM)
    tokens = qkv.shape[1]
    heads = 128 // HEAD_DIM
    key_t = qkv[1].astype(F32).T.astype(BF16)
    key_sum[...] = jnp.zeros_like(key_sum)
    value_sum[...] = jnp.zeros_like(value_sum)
    for block in range(tokens // size):
        first, last = window_of(block, size)
        rows = slice(block * size, (block + 1) * size)
        shape = (last - first, size)
        key_at = first + lax.broadcasted_iota(jnp.int32, shape, 0)
        query_at = block * size + lax.broadcasted_iota(jnp.int32, shape, 1)
        allowed = (key_at <= query_at) & (key_at >= starts[0:1, rows])
        key_part, value_part, query_parts = (0.0, 0.0, [])
        for head in range(heads):
            query = own_lanes(qkv[0, rows], head, factor)
            grad = own_lanes(grads[rows], head)
            scores = jnp.where(allowed, mm_nt(qkv[1, first:last], query), NEG_FILL)
            probs = jnp.exp(scores - logsum[0, head : head + 1, rows])
            probs_grad = mm_nt(qkv[2, first:last], grad)
            inner = jnp.sum(probs_grad * probs, axis=0, keepdims=True)
            score_grad = (probs * (probs_grad - inner)).astype(BF16)
            key_part += mm(score_grad, query)
            value_part += mm(probs.astype(BF16), grad)
            query_parts.append(
                mm(key_t[head * HEAD_DIM : (head + 1) * HEAD_DIM, first:last], score_grad)
            )
        key_sum[first:last] += key_part
        value_sum[first:last] += value_part
        query_grad = jnp.concatenate(query_parts, axis=0).T * factor
        out[0, rows] = turn(query_grad, cosine[rows], sine[rows], -1.0).astype(BF16)
    out[1] = turn(key_sum[...], cosine[...], sine[...], -1.0).astype(BF16)
    out[2] = value_sum[...].astype(BF16)


def attend_back(starts, qkv, context_grad, logsum, tables):
    _, tokens, width = qkv.shape
    pairs = width // 128
    heads = 128 // HEAD_DIM
    return pl.pallas_call(
        attend_back_kernel,
        grid=(pairs,),
        in_specs=[
            pl.BlockSpec((1, tokens), lambda p: (0, 0)),
            pl.BlockSpec((3, tokens, 128), lambda p: (0, 0, p)),
            pl.BlockSpec((tokens, 128), lambda p: (0, p)),
            pl.BlockSpec((1, heads, tokens), lambda p: (p, 0, 0)),
            pl.BlockSpec((tokens, 128), lambda p: (0, 0)),
            pl.BlockSpec((tokens, 128), lambda p: (0, 0)),
        ],
        out_specs=pl.BlockSpec((3, tokens, 128), lambda p: (0, 0, p)),
        out_shape=jax.ShapeDtypeStruct((3, tokens, width), BF16),
        scratch_shapes=[pltpu.VMEM((tokens, 128), F32), pltpu.VMEM((tokens, 128), F32)],
        compiler_params=params(),
        cost_estimate=cost(11),
        name="attend_back",
    )(starts, qkv, context_grad, logsum.reshape(pairs, heads, tokens), *tables)


def through_inputs_body(ways, number, *refs):
    norms, project_grad, pre_grad, wqkv, wup, normed_grad, terms = refs[ways:]
    normed, _ = normalize(added(refs[:ways]))
    width = project_grad.shape[2]
    attn = mm_nt(project_grad[0], wqkv[:, :width])
    attn += mm_nt(project_grad[1], wqkv[:, width : 2 * width])
    attn += mm_nt(project_grad[2], wqkv[:, 2 * width :])
    feed = mm_nt(pre_grad[...], wup[...])
    normed_grad[...] = (attn * norms[0:1] + feed * norms[2:3]).astype(BF16)
    terms[0:1] = jnp.sum(attn * normed, axis=0, keepdims=True)
    terms[1:2] = jnp.sum(attn, axis=0, keepdims=True)
    terms[2:3] = jnp.sum(feed * normed, axis=0, keepdims=True)
    terms[3:4] = jnp.sum(feed, axis=0, keepdims=True)


def through_inputs(chunk, index, norms, project_grad, pre_grad, pack):
    model = pack.shape[0]
    hidden = pre_grad.shape[1]
    width = project_grad.shape[2]
    return chunk_call(
        partial(through_inputs_body, len(chunk)),
        "through_inputs",
        0.3,
        index,
        [
            ((TOKENS, model), BF16, (TOKENS, model), HERE),
            ((4, model), F32, (4, model), HERE),
        ],
        [(way, (TOKENS, model), HERE) for way in chunk]
        + [
            (norms, (4, model), HERE),
            (project_grad, (3, TOKENS, width), lambda i: (0, i, 0)),
            (pre_grad, (TOKENS, hidden), ROWS),
            (pack, (model, 3 * width), HERE),
            (pack, (model, hidden), lambda i: (0, 1)),
        ],
    )


def outer_kernel(attn_in, feed_in, upstream, project_grad, context, pre_grad, active, out):
    step = pl.program_id(0)

    def fill(left, right, start=0):
        width = right.shape[1]
        out[:, :, start : start + width] = (
            lax.dot_general(left[...], right, (((0,), (0,)), ((), ())), preferred_element_type=F32)
            .astype(BF16)
            .reshape(*out.shape[:2], width)
        )

    @pl.when(step == 0)
    def _():
        fill(attn_in, project_grad[0])
        fill(attn_in, project_grad[1], context.shape[1])

    @pl.when(step == 1)
    def _():
        fill(attn_in, project_grad[2])
        fill(upstream, context[...], context.shape[1])

    pl.when((step == 2) | (step == 3))(lambda: fill(feed_in, pre_grad[...]))
    pl.when(step >= 4)(lambda: fill(upstream, active[...]))


def weight_grads(half, saved, upstream, pre_grad, project_grad):
    attn_in, feed_in, active, context = saved
    tokens, model = attn_in.shape
    width = context.shape[1]
    left = pl.BlockSpec((tokens, model // 2), lambda j: (0, half))
    return pl.pallas_call(
        outer_kernel,
        grid=(6,),
        in_specs=[
            left,
            left,
            left,
            pl.BlockSpec((3, tokens, width), lambda j: (0, 0, 0)),
            pl.BlockSpec((tokens, width), lambda j: (0, 0)),
            pl.BlockSpec((tokens, 2 * width), lambda j: (0, jnp.clip(j - 2, 0, 1))),
            pl.BlockSpec((tokens, 2 * width), lambda j: (0, jnp.clip(j - 4, 0, 1))),
        ],
        out_specs=pl.BlockSpec((4, model // 8, 2 * width), lambda j: (0, 0, j)),
        out_shape=jax.ShapeDtypeStruct((4, model // 8, 12 * width), BF16),
        compiler_params=params(18),
        cost_estimate=cost(0.3),
        name="weight_grads",
    )(attn_in, feed_in, upstream, project_grad, context, pre_grad, active)


def fold_kernel(kept, came, side, ahead, rest):
    half = kept.shape[1] // 2
    both = (kept[...].astype(F32) + came[...].astype(F32)).astype(BF16)
    side[0] = both[1, :half]
    side[1] = both[3, :half]
    ahead[0] = both[2, half:]
    ahead[1] = both[3, half:]
    rest[0] = both[0, :half]
    rest[1] = both[2, :half]
    rest[2] = both[0, half:]
    rest[3] = both[1, half:]


def fold(kept, came):
    _, rows, width = kept.shape
    step = width // 6
    block = lambda n, r: pl.BlockSpec((n, r, step), lambda j: (0, 0, j))
    shape = lambda n: jax.ShapeDtypeStruct((n, rows // 2, width), BF16)
    return pl.pallas_call(
        fold_kernel,
        grid=(6,),
        in_specs=[block(4, rows), block(4, rows)],
        out_specs=[block(2, rows // 2), block(2, rows // 2), block(4, rows // 2)],
        out_shape=[shape(2), shape(2), shape(4)],
        compiler_params=params(),
        cost_estimate=cost(0.3),
        name="fold",
    )(kept, came)


def assemble_kernel(place, *refs):
    pieces, whole = (refs[:-1], refs[-1])
    rows = pieces[0].shape[0]
    each = len(pieces) // 2
    for order, piece in enumerate(pieces):
        core, number = (order // each, min(order % each, 3))
        at = ((place[1] ^ number) * 2 + (place[0] ^ core)) * rows
        at = at + (rows // 2 if order % each == 4 else 0)
        whole[pl.ds(pl.multiple_of(at, rows // 2), piece.shape[0]), :] = piece[...]


def assemble(place, pieces):
    rows, width = pieces[0].shape
    step = width // 6
    return pl.pallas_call(
        assemble_kernel,
        grid_spec=pltpu.PrefetchScalarGridSpec(
            num_scalar_prefetch=1,
            grid=(6,),
            in_specs=[pl.BlockSpec((piece.shape[0], step), lambda j, place: (0, j)) for piece in pieces],
            out_specs=pl.BlockSpec((8 * rows, step), lambda j, place: (0, j)),
        ),
        out_shape=jax.ShapeDtypeStruct((8 * rows, width), BF16),
        compiler_params=params(18),
        cost_estimate=cost(6),
        name="assemble",
    )(place, *pieces)


def unpack_kernel(place, upper, lower, came, qkv, out, up, down):
    width, hidden = (out.shape[0], up.shape[1])
    half = came.shape[0]
    own = jnp.concatenate([upper[...], lower[...]], axis=0)
    for core, block in ((place[0], own), (1 - place[0], came[...].astype(F32))):
        rows = pl.ds(pl.multiple_of(core * half, half), half)
        qkv[rows, :] = block[:, : 3 * width]
        out[:, rows] = block[:, 3 * width : 4 * width].T
        up[rows, :] = block[:, 4 * width : 4 * width + hidden]
        down[:, rows] = block[:, 4 * width + hidden :].T


def unpack(sec, upper, lower, came, width, hidden):
    half = came.shape[0]
    shapes = [(2 * half, 3 * width), (width, 2 * half), (2 * half, hidden), (hidden, 2 * half)]
    return pl.pallas_call(
        unpack_kernel,
        grid_spec=pltpu.PrefetchScalarGridSpec(
            num_scalar_prefetch=1,
            grid=(1,),
            in_specs=[
                pl.BlockSpec(array.shape, lambda i, place: (0, 0)) for array in (upper, lower, came)
            ],
            out_specs=[pl.BlockSpec(shape, lambda i, place: (0, 0)) for shape in shapes],
        ),
        out_shape=[jax.ShapeDtypeStruct(shape, F32) for shape in shapes],
        compiler_params=params(18),
        cost_estimate=cost(2),
        name="unpack",
    )(sec.reshape(1).astype(jnp.int32), upper, lower, came)


def swap(block, axis, bit):
    return lax.ppermute(block, axis, [(i, i ^ bit) for i in range(lax.axis_size(axis))])


def join(*values):
    flat, tree = jax.tree.flatten(values)
    return jax.tree.unflatten(tree, lax.optimization_barrier(tuple(flat)))


def sum_over(value, axis):
    others = [swap(value, axis, bit) for bit in range(1, lax.axis_size(axis))]
    return sum(others, start=value)


def pick(stack, index):
    return lax.dynamic_index_in_dim(stack, index, 0, keepdims=False)


def send_sides(half):
    return (swap(half, "col", 1), swap(half, "col", 2))


def send_corner(side, ahead):
    rows = side.shape[0] // 2
    return [swap(side[:rows], "col", 2), swap(ahead[rows:], "col", 1)]


def add(a, b):
    return a.astype(F32) + b.astype(F32)


def along_row(block, pairs):
    return lax.ppermute(block, "row", pairs)


ONE_OVER = [(0, 1), (1, 0), (2, 3), (3, 2)]
TWO_OVER = [(0, 2), (2, 0), (1, 3), (3, 1)]
MIDDLE = [(1, 2), (2, 1)]
OUTWARD = [(1, 0), (2, 3)]
INWARD = [(0, 1), (3, 2)]


def send_own(own):
    return (along_row(own, TWO_OVER), along_row(own, ONE_OVER))


def pass_on(own, far):
    return (along_row(far, OUTWARD), along_row(own, MIDDLE))


def send_last(share):
    return (along_row(share, INWARD), along_row(share, MIDDLE))


def send_sums(far, passed, near):
    return (along_row(add(far, passed).astype(BF16), TWO_OVER), along_row(near, ONE_OVER))


def fast_shards(
    hidden_in,
    doc_ids,
    qkv_weight,
    out_weight,
    up_weight,
    down_weight,
    attn_gain,
    attn_shift,
    mlp_gain,
    mlp_shift,
    out_cotangent,
):
    sec, row, col = (lax.axis_index("section"), lax.axis_index("row"), lax.axis_index("col"))
    cols, rows = (lax.axis_size("col"), lax.axis_size("row"))
    model = hidden_in.shape[3]
    tokens = doc_ids.shape[2]
    width = qkv_weight.shape[3]
    hidden = up_weight.shape[2]
    block = qkv_weight.shape[1]
    first = sec == 0
    x_own = pick(hidden_in[:, 0], sec)
    docs = pick(doc_ids[:, 0], sec)
    given = pick(out_cotangent[:, 0], sec)

    place = jnp.stack([sec, col]).astype(jnp.int32)
    share = attn_gain.shape[1]

    def enter(kept, chunk, number, layer):
        return project(
            chunk,
            row ^ number,
            place,
            tokens,
            norms[layer],
            packs[layer],
            tables,
            width,
            hidden,
            kept,
        )

    def leave(kept, entered, number, layer):
        _, _, qkv, value_t, active, _ = entered
        *kept, share_of = attend(row ^ number, starts, qkv, value_t, active, packs[layer], kept)
        return (tuple(kept), share_of)

    def back_branch(kept, chunk, number, slope, layer):
        return through_branch(chunk, row ^ number, place, packs[layer], slope, width, kept)

    def back_inputs(chunks, number, layer, project_grad, pre_grad):
        return through_inputs(
            chunks[number], row ^ number, norms[layer], project_grad, pre_grad, packs[layer]
        )

    choose = lambda here, there: jnp.where(first, here, there)

    def by_layer(zero, one):
        away = swap(choose(one, zero), "section", 1)
        here = choose(zero, one)
        return jnp.stack([choose(here, away), choose(away, here)])

    def input_grad(total, own, own_grads):
        normed, scale = normalize(own)
        result = own_grads.astype(F32) + scale * (
            total
            - jnp.mean(total, axis=-1, keepdims=True)
            - normed * jnp.mean(total * normed, axis=-1, keepdims=True)
        )
        return result.astype(BF16)


    far_x0, near_x0 = send_own(x_own)
    vectors = jnp.stack([attn_gain[0], attn_shift[0], mlp_gain[0], mlp_shift[0]])
    norms = lax.dynamic_update_slice(
        jnp.zeros((2, 4, model), F32), vectors[None], (sec, 0, (row * cols + col) * share)
    )
    norms = sum_over(norms, "row")
    own_pack = jnp.concatenate(
        [
            qkv_weight[0].reshape(block, 3 * width),
            out_weight[0].T,
            up_weight[0],
            down_weight[0].T,
        ],
        axis=1,
    )
    half_of = lambda core: lax.dynamic_slice_in_dim(own_pack, core * (block // 2), block // 2)
    staying, leaving = (half_of(sec), half_of(1 - sec))
    norms, staying, leaving = join(norms, staying, leaving)

    came = swap(leaving, "section", 1)
    norms = sum_over(norms, "section")
    half0, half1 = (jnp.where(first, staying, came), jnp.where(first, came, staying))
    norms, half0, half1 = join(norms, half0, half1)

    norms = sum_over(norms, "col")
    norms, half0 = join(norms, half0)

    side0, ahead0 = send_sides(half0)
    starts = jnp.sum((docs[None, :] < docs[:, None]).astype(jnp.int32), axis=1)
    tables = rope_tables(docs, starts)
    starts = starts[None]
    half0, side0, ahead0, starts, tables, far_x0, near_x0 = join(
        half0, side0, ahead0, starts, tables, far_x0, near_x0
    )
    passed_x0, middle_x0 = pass_on(x_own, far_x0)
    chunks_x0 = [(x_own,), (near_x0,), (far_x0,), (middle_x0, passed_x0)]

    across0 = send_corner(side0, ahead0)
    mine = [half0, side0, ahead0]
    theirs = [swap(piece, "section", 1) for piece in mine]
    mine, theirs, across0, chunks_x0, given = join(mine, theirs, across0, chunks_x0, given)

    theirs = theirs + [swap(piece, "section", 1) for piece in across0]
    mine, theirs, half1, given = join(mine + across0, theirs, half1, given)

    far_g1, near_g1 = send_own(given)
    side1, ahead1 = send_sides(half1)
    packs = [assemble(place, mine + theirs), None]
    entered0 = ()
    for number in range(4):
        entered0 = enter(entered0, chunks_x0[number], number, 0)
    kept, last = leave((), entered0, 3, 0)
    far_g1, near_g1, side1, ahead1, entered0, kept, last, packs = join(
        far_g1, near_g1, side1, ahead1, entered0, kept, last, packs
    )

    passed_y0, middle_y0 = send_last(last)
    kept, far = leave(kept, entered0, 2, 0)
    kept, near = leave(kept, entered0, 1, 0)
    (context0, logsum0), share_of = leave(kept, entered0, 0, 0)
    passed_g1, middle_g1 = pass_on(given, far_g1)
    passed_y0, middle_y0, far, near, half1, side1, ahead1, passed_g1, middle_g1 = join(
        passed_y0, middle_y0, far, near, half1, side1, ahead1, passed_g1, middle_g1
    )

    far_y0, near_y0 = send_sums(far, passed_y0, near)
    across1 = send_corner(side1, ahead1)
    mine = [half1, side1, ahead1] + across1
    theirs = [swap(piece, "section", 1) for piece in mine]
    far_y0, near_y0, mine, theirs = join(far_y0, near_y0, mine, theirs)
    total = add(share_of, near_y0) + add(middle_y0, far_y0)
    y0_own = (x_own.astype(F32) + total).astype(BF16)

    far_x1, near_x1 = send_own(y0_own)
    packs[1] = assemble(place, mine + theirs)
    entered1 = enter((), (y0_own,), 0, 1)
    branch1 = back_branch((), (given,), 0, entered1[5], 1)
    far_x1, near_x1, y0_own, entered1, branch1 = join(far_x1, near_x1, y0_own, entered1, branch1)

    passed_x1, middle_x1 = pass_on(y0_own, far_x1)
    entered1 = enter(entered1, (near_x1,), 1, 1)
    branch1 = back_branch(branch1, (near_g1,), 1, entered1[5], 1)
    entered1 = enter(entered1, (far_x1,), 2, 1)
    branch1 = back_branch(branch1, (far_g1,), 2, entered1[5], 1)
    passed_x1, middle_x1, entered1, branch1 = join(passed_x1, middle_x1, entered1, branch1)

    chunks_x1 = [(y0_own,), (near_x1,), (far_x1,), (middle_x1, passed_x1)]
    entered1 = enter(entered1, chunks_x1[3], 3, 1)
    pre_grad1, context_grad1, grads1 = back_branch(
        branch1, (middle_g1, passed_g1), 3, entered1[5], 1
    )
    context_grad1, entered1 = join(context_grad1, entered1)
    kept, last_b1 = leave((), entered1, 3, 1)
    kept, far_b1 = leave(kept, entered1, 2, 1)
    kept, near_b1 = leave(kept, entered1, 1, 1)
    (context1, logsum1), share_b1 = leave(kept, entered1, 0, 1)

    saved1 = (entered1[0], entered1[1], entered1[4], context1)
    project_grad1 = attend_back(starts, entered1[2], context_grad1, logsum1, tables)
    last, terms1 = back_inputs(chunks_x1, 3, 1, project_grad1, pre_grad1)
    last, project_grad1 = join(last, project_grad1)

    passed_n1, middle_n1 = send_last(last)
    others = [back_inputs(chunks_x1, number, 1, project_grad1, pre_grad1) for number in (2, 1, 0)]
    (far, near, share_of), terms = zip(*others)
    terms1 = sum(terms, start=terms1)
    far = add(far, passed_n1).astype(BF16)
    leaving1 = weight_grads(1, saved1, grads1, pre_grad1, project_grad1)
    far, middle_n1, near, leaving1, project_grad1 = join(
        far, middle_n1, near, leaving1, project_grad1
    )

    far_n1, near_n1 = (along_row(far, TWO_OVER), along_row(near, ONE_OVER))
    came1 = swap(leaving1, "section", 1)
    kept1 = weight_grads(0, saved1, grads1, pre_grad1, project_grad1)
    far_n1, near_n1, came1, kept1 = join(far_n1, near_n1, came1, kept1)
    total = add(share_of, near_n1) + add(middle_n1, far_n1)
    dx1_own = input_grad(total, y0_own, given)

    slope0 = entered0[5]
    far_g0, near_g0 = send_own(dx1_own)
    side1, ahead1, rest1 = fold(kept1, came1)
    first1, second1 = (swap(side1, "col", 1), swap(ahead1, "col", 2))
    branch0 = back_branch((), (dx1_own,), 0, slope0, 0)
    far_g0, near_g0, dx1_own, last_b1 = join(far_g0, near_g0, dx1_own, last_b1)

    passed_y1 = along_row(last_b1, INWARD)
    passed_g0, middle_g0 = pass_on(dx1_own, far_g0)
    branch0 = back_branch(branch0, (near_g0,), 1, slope0, 0)
    branch0 = back_branch(branch0, (far_g0,), 2, slope0, 0)
    passed_g0, middle_g0, first1, second1, last_b1, near_b1, far_b1, passed_y1 = join(
        passed_g0, middle_g0, first1, second1, last_b1, near_b1, far_b1, passed_y1
    )

    passed1 = (
        swap(add(rest1[1], first1[1]).astype(BF16), "col", 2),
        swap(add(rest1[3], second1[1]).astype(BF16), "col", 1),
    )
    far_y1, near_y1 = send_sums(far_b1, passed_y1, near_b1)
    pre_grad0, context_grad0, grads0 = back_branch(branch0, (middle_g0, passed_g0), 3, slope0, 0)
    saved0 = (entered0[0], entered0[1], entered0[4], context0)
    project_grad0 = attend_back(starts, entered0[2], context_grad0, logsum0, tables)
    last, terms0 = back_inputs(chunks_x0, 3, 0, project_grad0, pre_grad0)
    last, project_grad0, passed1, far_y1, near_y1, last_b1 = join(
        last, project_grad0, passed1, far_y1, near_y1, last_b1
    )

    passed_n0, middle_n0 = send_last(last)
    leaving0 = weight_grads(1, saved0, grads0, pre_grad0, project_grad0)
    others = [back_inputs(chunks_x0, number, 0, project_grad0, pre_grad0) for number in (2, 1, 0)]
    (far, near, share_of), terms = zip(*others)
    terms = sum_over(sum_over(jnp.stack([sum(terms, start=terms0), terms1]), "section"), "col")
    passed_n0, middle_n0, far, near, terms, leaving0, project_grad0 = join(
        passed_n0, middle_n0, far, near, terms, leaving0, project_grad0
    )

    far_n0, near_n0 = send_sums(far, passed_n0, near)
    came0 = swap(leaving0, "section", 1)
    kept0 = weight_grads(0, saved0, grads0, pre_grad0, project_grad0)
    side0, ahead0, rest0 = fold(kept0, came0)
    sums1 = (
        add(add(rest1[0], first1[0]), passed1[0]),
        add(add(rest1[2], second1[0]), passed1[1]),
    )
    far_n0, near_n0, side0, ahead0, terms, sums1, last_b1 = join(
        far_n0, near_n0, side0, ahead0, terms, sums1, last_b1
    )

    first0, second0 = (swap(side0, "col", 1), swap(ahead0, "col", 2))
    middle_y1 = along_row(last_b1, MIDDLE)
    total = add(share_of, near_n0) + add(middle_n0, far_n0)
    dx0_own = input_grad(total, x_own, dx1_own)
    terms, dx0_own = join(terms, dx0_own)
    terms = sum_over(terms, "row")
    first0, second0, dx0_own, middle_y1, terms = join(first0, second0, dx0_own, middle_y1, terms)

    passed0 = (
        swap(add(rest0[1], first0[1]).astype(BF16), "col", 2),
        swap(add(rest0[3], second0[1]).astype(BF16), "col", 1),
    )
    total = add(share_b1, near_y1) + add(middle_y1, far_y1)
    y1_own = (y0_own.astype(F32) + total).astype(BF16)
    outputs = by_layer(y0_own, y1_own)
    sums0 = (
        add(add(rest0[0], first0[0]), passed0[0]),
        add(add(rest0[2], second0[0]), passed0[1]),
    )

    leaving = jnp.concatenate([choose(b, a) for a, b in zip(sums0, sums1)]).astype(BF16)
    upper, lower = [choose(a, b) for a, b in zip(sums0, sums1)]
    qkv_grad, out_grad, up_grad, down_grad = unpack(
        sec, upper, lower, swap(leaving, "section", 1), width, hidden
    )
    terms = pick(terms, sec)
    terms = lax.dynamic_slice_in_dim(terms, (row * cols + col) * share, share, 1)

    return (
        outputs[None, :, None],
        by_layer(dx0_own, dx1_own)[None, :, None],
        qkv_grad.reshape(1, block, 3, width),
        out_grad[None],
        up_grad[None],
        down_grad[None],
        terms[None, 0],
        terms[None, 1],
        terms[None, 2],
        terms[None, 3],
    )


def from_behind(block, axis, distance):
    devices = range(lax.axis_size(axis))
    route = [(i - distance, i) for i in devices if i - distance in devices]
    return lax.ppermute(block, axis, route)


def positions_of(docs):
    length = docs.shape[0]
    index = jnp.arange(length, dtype=jnp.int32)
    starts = jnp.concatenate([jnp.ones((1,), jnp.bool_), docs[1:] != docs[:-1]])
    first = lax.cummax(jnp.where(starts, index, 0), axis=0)
    return index - first


def rotary_tables(docs):
    half = ROT // 2
    freqs = 10000.0 ** (-2.0 * jnp.arange(half, dtype=jnp.float32) / ROT)
    angles = positions_of(docs).astype(jnp.float32)[:, None] * freqs[None, :]
    return (jnp.cos(angles)[:, None, :], jnp.sin(angles)[:, None, :])


def rotate(values, cosine, sine):
    half = ROT // 2
    front = values[..., :half]
    back = values[..., half:ROT]
    return jnp.concatenate(
        [front * cosine - back * sine, back * cosine + front * sine, values[..., ROT:]], axis=-1
    )


def rotate_back(grads, cosine, sine):
    half = ROT // 2
    front = grads[..., :half]
    back = grads[..., half:ROT]
    return jnp.concatenate(
        [front * cosine + back * sine, back * cosine - front * sine, grads[..., ROT:]], axis=-1
    )


def block_mask(docs, start, size):
    rows = start + jnp.arange(size, dtype=jnp.int32)
    cols = jnp.arange(docs.shape[0], dtype=jnp.int32)
    row_docs = lax.dynamic_slice_in_dim(docs, start, size)
    return (row_docs[:, None] == docs[None, :]) & (cols[None, :] <= rows[:, None])


def block_scores(query, key, docs, start, block):
    factor = 1.0 / math.sqrt(query.shape[2])
    rows = lax.dynamic_slice_in_dim(query, start, block)
    scores = jnp.einsum("qhd,khd->hqk", rows, key, preferred_element_type=jnp.float32) * factor
    allowed = block_mask(docs, start, block)[None]
    return (rows, jnp.where(allowed, scores, NEG_FILL))


def attend_forward(query, key, value, docs):
    length, heads, width = query.shape
    block = min(512, length)

    def one_block(number):
        start = number * block
        rows, scores = block_scores(query, key, docs, start, block)
        peak = jnp.max(scores, axis=-1, keepdims=True)
        raised = jnp.exp(scores - peak)
        total = jnp.sum(raised, axis=-1, keepdims=True)
        probs = (raised / total).astype(jnp.bfloat16)
        context = jnp.einsum(
            "hqk,khd->qhd", probs, value, preferred_element_type=jnp.float32
        ).astype(jnp.bfloat16)
        return (context, (peak + jnp.log(total))[..., 0])

    context, logsum = lax.map(one_block, jnp.arange(length // block, dtype=jnp.int32))
    return (context.reshape(length, heads, width), logsum)


def attend_backward(query, key, value, docs, logsum, context_grad):
    length, heads, width = query.shape
    block = min(512, length)
    factor = 1.0 / math.sqrt(width)

    def one_block(carry, inputs):
        key_grad, value_grad = carry
        number, block_logsum = inputs
        start = number * block
        rows, scores = block_scores(query, key, docs, start, block)
        rows_grad = lax.dynamic_slice_in_dim(context_grad, start, block)
        probs_full = jnp.exp(scores - block_logsum[:, :, None])
        probs = probs_full.astype(jnp.bfloat16)
        context = jnp.einsum(
            "hqk,khd->qhd", probs, value, preferred_element_type=jnp.float32
        ).astype(jnp.bfloat16)
        probs_grad = jnp.einsum(
            "qhd,khd->hqk", rows_grad, value, preferred_element_type=jnp.float32
        )
        inner = jnp.sum(probs_grad * probs_full, axis=-1, keepdims=True)
        score_grad = (probs_full * (probs_grad - inner)).astype(jnp.bfloat16)
        query_grad = (
            jnp.einsum("hqk,khd->qhd", score_grad, key, preferred_element_type=jnp.float32) * factor
        )
        key_grad = (
            key_grad
            + jnp.einsum("hqk,qhd->khd", score_grad, rows, preferred_element_type=jnp.float32)
            * factor
        )
        value_grad = value_grad + jnp.einsum(
            "hqk,qhd->khd", probs, rows_grad, preferred_element_type=jnp.float32
        )
        return ((key_grad, value_grad), (context, query_grad))

    zeros = jnp.zeros((length, heads, width), jnp.float32)
    numbers = jnp.arange(length // block, dtype=jnp.int32)
    (key_grad, value_grad), (context, query_grad) = lax.scan(
        one_block, (zeros, zeros), (numbers, logsum)
    )
    return (
        context.reshape(length, heads * width),
        query_grad.reshape(length, heads, width),
        key_grad,
        value_grad,
    )


def gather_features(shard):
    return lax.all_gather(shard, "row", axis=0, tiled=True)


def recompute_inputs(full, docs, norms, weights):
    gain_a, shift_a, gain_m, shift_m = norms
    qkv_full = weights[0]
    normed, scale = normalize(full)
    attn_in = (normed * gain_a + shift_a).astype(jnp.bfloat16)
    feed_in = (normed * gain_m + shift_m).astype(jnp.bfloat16)
    length = full.shape[0]
    heads_here = qkv_full.shape[2] // HEAD_DIM
    project = jnp.einsum("td,dke->tke", attn_in, qkv_full, preferred_element_type=jnp.float32)
    cosine, sine = rotary_tables(docs)
    query = rotate(project[:, 0].reshape(length, heads_here, HEAD_DIM), cosine, sine).astype(
        jnp.bfloat16
    )
    key = rotate(project[:, 1].reshape(length, heads_here, HEAD_DIM), cosine, sine).astype(
        jnp.bfloat16
    )
    value = project[:, 2].reshape(length, heads_here, HEAD_DIM).astype(jnp.bfloat16)
    pre = jnp.dot(feed_in, weights[2], preferred_element_type=jnp.float32)
    return (normed, scale, attn_in, feed_in, query, key, value, pre, cosine, sine)


def layer_forward(shard, docs, full, norms, weights):
    normed, scale, attn_in, feed_in, query, key, value, pre, cosine, sine = recompute_inputs(
        full, docs, norms, weights
    )
    length = full.shape[0]
    context, logsum = attend_forward(query, key, value, docs)
    active = jax.nn.gelu(pre, approximate=False).astype(jnp.bfloat16)
    partial_sum = jnp.dot(
        context.reshape(length, -1), weights[1], preferred_element_type=jnp.float32
    )
    partial_sum = partial_sum + jnp.dot(active, weights[3], preferred_element_type=jnp.float32)
    branch = lax.psum_scatter(
        partial_sum.astype(jnp.bfloat16), "row", scatter_dimension=0, tiled=True
    ).astype(jnp.float32)
    return ((shard.astype(jnp.float32) + branch).astype(jnp.bfloat16), logsum)


def layer_backward(docs, full, logsum, upstream, norms, weights):
    gain_a, shift_a, gain_m, shift_m = norms
    qkv_full, out_full, up_full, down_full = weights
    normed, scale, attn_in, feed_in, query, key, value, pre, cosine, sine = recompute_inputs(
        full, docs, norms, weights
    )
    length = full.shape[0]
    heads_here = query.shape[1]
    active = jax.nn.gelu(pre, approximate=False).astype(jnp.bfloat16)
    upstream_full = lax.all_gather(upstream, "row", axis=0, tiled=True)
    down_part = jnp.einsum("tf,td->fd", active, upstream_full, preferred_element_type=jnp.float32)
    act_grad = jnp.einsum("td,fd->tf", upstream_full, down_full, preferred_element_type=jnp.float32)
    pre_grad = jax.vjp(partial(jax.nn.gelu, approximate=False), pre)[1](act_grad)[0].astype(
        jnp.bfloat16
    )
    up_part = jnp.einsum("td,tf->df", feed_in, pre_grad, preferred_element_type=jnp.float32)
    feed_grad = jnp.einsum("tf,df->td", pre_grad, up_full, preferred_element_type=jnp.float32)
    context_grad = jnp.einsum(
        "td,ed->te", upstream_full, out_full, preferred_element_type=jnp.float32
    ).astype(jnp.bfloat16)
    context_grad = context_grad.reshape(length, heads_here, HEAD_DIM)
    context, query_grad, key_grad, value_grad = attend_backward(
        query, key, value, docs, logsum, context_grad
    )
    out_part = jnp.einsum("te,td->ed", context, upstream_full, preferred_element_type=jnp.float32)
    project_grad = jnp.stack(
        [
            rotate_back(query_grad, cosine, sine).reshape(length, -1),
            rotate_back(key_grad, cosine, sine).reshape(length, -1),
            value_grad.reshape(length, -1),
        ],
        axis=1,
    ).astype(jnp.bfloat16)
    qkv_part = jnp.einsum("td,tke->dke", attn_in, project_grad, preferred_element_type=jnp.float32)
    attn_grad = jnp.einsum(
        "tke,dke->td", project_grad, qkv_full, preferred_element_type=jnp.float32
    )
    own_rows = upstream.shape[0]
    offset = lax.axis_index("row") * own_rows
    normed_part = lax.dynamic_slice_in_dim(normed, offset, own_rows, 0)
    scale_part = lax.dynamic_slice_in_dim(scale, offset, own_rows, 0)
    attn_piece, feed_piece = (
        lax.psum_scatter(
            attn_grad.astype(jnp.bfloat16), "row", scatter_dimension=0, tiled=True
        ).astype(jnp.float32),
        lax.psum_scatter(
            feed_grad.astype(jnp.bfloat16), "row", scatter_dimension=0, tiled=True
        ).astype(jnp.float32),
    )
    normed_grad = attn_piece * gain_a + feed_piece * gain_m
    gain_terms = (
        jnp.sum(attn_piece * normed_part, axis=0),
        jnp.sum(attn_piece, axis=0),
        jnp.sum(feed_piece * normed_part, axis=0),
        jnp.sum(feed_piece, axis=0),
    )
    row_sum = jnp.sum(normed_grad, axis=-1)
    cross_sum = jnp.sum(normed_grad * normed_part, axis=-1)
    count = full.shape[1]
    input_grad = upstream.astype(jnp.float32) + scale_part * (
        normed_grad - row_sum[:, None] / count - normed_part * cross_sum[:, None] / count
    )
    return (input_grad, (qkv_part, out_part, up_part, down_part), gain_terms)


def general_shards(
    hidden_in,
    doc_ids,
    qkv_weight,
    out_weight,
    up_weight,
    down_weight,
    attn_gain,
    attn_shift,
    mlp_gain,
    mlp_shift,
    out_cotangent,
):
    micro = hidden_in.shape[0]
    first_section = lax.axis_index("section") == 0
    norms = (
        lax.all_gather(attn_gain[0], ("row", "col"), axis=0, tiled=True),
        lax.all_gather(attn_shift[0], ("row", "col"), axis=0, tiled=True),
        lax.all_gather(mlp_gain[0], ("row", "col"), axis=0, tiled=True),
        lax.all_gather(mlp_shift[0], ("row", "col"), axis=0, tiled=True),
    )
    weights = (
        lax.all_gather(qkv_weight[0], "col", axis=0, tiled=True),
        lax.all_gather(out_weight[0], "col", axis=1, tiled=True),
        lax.all_gather(up_weight[0], "col", axis=0, tiled=True),
        lax.all_gather(down_weight[0], "col", axis=1, tiled=True),
    )
    received = jnp.zeros_like(hidden_in[0, 0])
    tick_inputs, tick_docs, tick_fulls, tick_outputs, tick_logsums = ([], [], [], [], [])
    for tick in range(micro + 1):
        own = hidden_in[min(tick, micro - 1), 0]
        shard = jnp.where(first_section, own, received)
        docs = jnp.where(
            first_section, doc_ids[min(tick, micro - 1), 0], doc_ids[max(tick - 1, 0), 0]
        )
        full = gather_features(shard)
        result, logsum = layer_forward(shard, docs, full, norms, weights)
        tick_inputs.append(shard)
        tick_docs.append(docs)
        tick_fulls.append(full)
        tick_outputs.append(result)
        tick_logsums.append(logsum)
        if tick < micro:
            received = from_behind(result, "section", 1)
    outputs = jnp.stack(
        [
            jnp.where(first_section, tick_outputs[number], tick_outputs[number + 1])
            for number in range(micro)
        ]
    )
    received = jnp.zeros_like(hidden_in[0, 0])
    matrix_totals = None
    gain_totals = None
    tick_grads = []
    for tick in range(micro + 1):
        early = max(tick - 1, 0)
        later = min(tick + 1, micro)
        if tick < micro:
            given = out_cotangent[tick, 0]
        else:
            given = jnp.zeros_like(out_cotangent[0, 0])
        upstream = jnp.where(first_section, received, given)
        shard = jnp.where(first_section, tick_inputs[early], tick_inputs[later])
        docs = jnp.where(first_section, tick_docs[early], tick_docs[later])
        logsum = jnp.where(first_section, tick_logsums[early], tick_logsums[later])
        full = gather_features(shard)
        input_grad, matrices, gain_terms = layer_backward(
            docs, full, logsum, upstream, norms, weights
        )
        if matrix_totals is None:
            matrix_totals = matrices
            gain_totals = gain_terms
        else:
            matrix_totals = jax.tree.map(jnp.add, matrix_totals, matrices)
            gain_totals = jax.tree.map(jnp.add, gain_totals, gain_terms)
        grad_low = input_grad.astype(jnp.bfloat16)
        tick_grads.append(grad_low)
        if tick < micro:
            received = from_behind(grad_low, "section", -1)
    grads_in = jnp.stack(
        [
            jnp.where(first_section, tick_grads[number + 1], tick_grads[number])
            for number in range(micro)
        ]
    )
    qkv_sum, out_sum, up_sum, down_sum = matrix_totals
    gain_a_sum, shift_a_sum, gain_m_sum, shift_m_sum = gain_totals
    qkv_total, out_total, up_total, down_total = (
        lax.psum_scatter(
            qkv_sum.astype(jnp.bfloat16), "col", scatter_dimension=0, tiled=True
        ).astype(jnp.float32),
        lax.psum_scatter(
            out_sum.astype(jnp.bfloat16), "col", scatter_dimension=1, tiled=True
        ).astype(jnp.float32),
        lax.psum_scatter(
            up_sum.astype(jnp.bfloat16), "col", scatter_dimension=0, tiled=True
        ).astype(jnp.float32),
        lax.psum_scatter(
            down_sum.astype(jnp.bfloat16), "col", scatter_dimension=1, tiled=True
        ).astype(jnp.float32),
    )
    gain_a_total, shift_a_total, gain_m_total, shift_m_total = (
        lax.psum_scatter(gain_a_sum, ("row", "col"), scatter_dimension=0, tiled=True),
        lax.psum_scatter(shift_a_sum, ("row", "col"), scatter_dimension=0, tiled=True),
        lax.psum_scatter(gain_m_sum, ("row", "col"), scatter_dimension=0, tiled=True),
        lax.psum_scatter(shift_m_sum, ("row", "col"), scatter_dimension=0, tiled=True),
    )
    return (
        outputs[None, :, None],
        grads_in[None, :, None],
        qkv_total[None],
        out_total[None],
        up_total[None],
        down_total[None],
        gain_a_total[None],
        shift_a_total[None],
        gain_m_total[None],
        shift_m_total[None],
    )


def shards(*arrays):
    hidden_in, qkv_weight, up_weight = (arrays[0], arrays[2], arrays[4])
    micro, seqs, own_tokens, model = hidden_in.shape
    width, hidden = (qkv_weight.shape[3], up_weight.shape[2])
    sizes = tuple(lax.axis_size(axis) for axis in ("section", "row", "col"))
    fits = (
        sizes == (2, 4, 4) and (micro, seqs) == (2, 1)
        and own_tokens == TOKENS
        and width % 128 == 0
        and 4 * width == hidden
    )
    return fast_shards(*arrays) if fits else general_shards(*arrays)


def solution(mesh):
    placed = (
        P(None, "col", "row", None),
        P(None, "col", None),
        P("section", "col", None, "row"),
        P("section", "row", "col"),
        P("section", "col", "row"),
        P("section", "row", "col"),
        P("section", ("row", "col")),
        P("section", ("row", "col")),
        P("section", ("row", "col")),
        P("section", ("row", "col")),
        P(None, "col", "row", None),
    )
    return jax.shard_map(
        shards,
        mesh=mesh,
        in_specs=placed,
        out_specs=(
            P("section", None, "col", "row", None),
            P("section", None, "col", "row", None),
            P("section", "col", None, "row"),
            P("section", "row", "col"),
            P("section", "col", "row"),
            P("section", "row", "col"),
            P("section", ("row", "col")),
            P("section", ("row", "col")),
            P("section", ("row", "col")),
            P("section", ("row", "col")),
        ),
        check_vma=False,
    )
```

```python
from functools import partial
import math

import jax
import jax.numpy as jnp
from jax import lax
from jax.experimental import pallas as pl
from jax.experimental.pallas import tpu as pltpu
from jax.sharding import PartitionSpec as P

HEAD_DIM = 64
ROT = 16
EPSILON = 1e-05
NEG_FILL = -1e30
BF16 = jnp.bfloat16
F32 = jnp.float32
TOKENS = 256
LONGEST_DOC = 512


def mm(a, b):
    return lax.dot_general(a, b, (((1,), (0,)), ((), ())), preferred_element_type=F32)


def mm_nt(a, b):
    return lax.dot_general(a, b, (((1,), (1,)), ((), ())), preferred_element_type=F32)


def normalize(full):
    wide = full.astype(F32)
    center = wide - jnp.mean(wide, axis=-1, keepdims=True)
    scale = lax.rsqrt(jnp.mean(center * center, axis=-1, keepdims=True) + EPSILON)
    return (center * scale, scale)


ERFC = (
    0.17087277,
    -0.82215223,
    1.48851587,
    -1.13520398,
    0.27886807,
    -0.18628806,
    0.09678418,
    0.37409196,
    1.00002368,
    -1.26551223,
)


def gelu_and_slope(pre):
    size = jnp.abs(pre) * math.sqrt(0.5)
    t = 1.0 / (1.0 + 0.5 * size)
    poly = jnp.full_like(t, ERFC[0])
    for coefficient in ERFC[1:]:
        poly = poly * t + coefficient
    bell = jnp.exp(-(size * size))
    tail = (0.5 * t) * (bell * jnp.exp(poly))
    below = jnp.where(pre >= 0, 1.0 - tail, tail)
    return (pre * below, below + pre * (bell * (1.0 / math.sqrt(2.0 * math.pi))))


def turn(values, cosine, sine, sign):
    width = values.shape[-1]
    half = ROT // 2
    lane = lax.broadcasted_iota(jnp.int32, values.shape, 1) % HEAD_DIM
    other = jnp.where(
        lane < half, -pltpu.roll(values, width - half, 1), pltpu.roll(values, half, 1)
    )
    return values * cosine + (sign * other) * sine


def rope_tables(docs, starts):
    half = ROT // 2
    lane = jnp.arange(128, dtype=jnp.int32) % HEAD_DIM
    freqs = 10000.0 ** (-2.0 * (lane % half).astype(F32) / ROT)
    position = (jnp.arange(docs.shape[0], dtype=jnp.int32) - starts).astype(F32)
    angles = position[:, None] * freqs[None, :]
    rotated = (lane < ROT)[None, :]
    return (jnp.where(rotated, jnp.cos(angles), 1.0), jnp.where(rotated, jnp.sin(angles), 0.0))


def params(mib=18):
    return pltpu.CompilerParams(vmem_limit_bytes=mib << 20)


def cost(us):
    return pl.CostEstimate(flops=int(us * 1.1e+09), bytes_accessed=int(us * 3.2e+06), transcendentals=0)


def chunk_call(body, name, us, index, outs, inputs, kept=(), place=None):
    given = len(inputs)
    number = index.reshape(1).astype(jnp.int32)
    if place is not None:
        number = jnp.concatenate([number, place])

    def kernel(number, *refs):
        body(number, *refs[:given], *refs[given + len(kept) :])

    spec = lambda block, at: pl.BlockSpec(block, lambda i, number: at(number[0]))
    return pl.pallas_call(
        kernel,
        grid_spec=pltpu.PrefetchScalarGridSpec(
            num_scalar_prefetch=1,
            grid=(1,),
            in_specs=[spec(block, at) for _, block, at in inputs]
            + [pl.BlockSpec(memory_space=pl.ANY) for _ in kept],
            out_specs=[spec(block, at) for _, _, block, at in outs],
        ),
        out_shape=[jax.ShapeDtypeStruct(shape, dtype) for shape, dtype, _, _ in outs],
        input_output_aliases={1 + given + i: i for i in range(len(kept))},
        compiler_params=params(),
        cost_estimate=cost(us),
        name=name,
    )(number, *[array for array, _, _ in inputs], *kept)


HERE = lambda i: (0, 0)
ROWS = lambda i: (i, 0)
LANES = lambda i: (0, i)


def added(refs):
    whole = refs[0][...]
    for ref in refs[1:]:
        whole = whole + ref[...]
    return whole


def keep_by_owner(kept, place, values):
    blocks = values.shape[1] // 128
    for block in range(blocks):
        at = (place[0] ^ (block % 2)) * (blocks // 2) + (place[1] ^ (block // 2))
        lanes = pl.ds(pl.multiple_of(at * 128, 128), 128)
        kept[:, lanes] = values[:, block * 128 : (block + 1) * 128]


def project_body(ways, number, *refs):
    norms, wqkv, wup, cosine, sine, attn_in, feed_in, qkv, value_t, active, slope = refs[ways:]
    normed, _ = normalize(added(refs[:ways]))
    attn = (normed * norms[0:1] + norms[1:2]).astype(BF16)
    feed = (normed * norms[2:3] + norms[3:4]).astype(BF16)
    place = (number[1], number[2])
    keep_by_owner(attn_in, place, attn)
    keep_by_owner(feed_in, place, feed)
    width = qkv.shape[2]
    for part in range(3):
        piece = mm(attn, wqkv[:, part * width : (part + 1) * width])
        for pair in range(width // 128):
            lanes = slice(pair * 128, (pair + 1) * 128)
            one = piece[:, lanes]
            if part < 2:
                one = turn(one, cosine[...], sine[...], 1.0)
            else:
                value_t[lanes, :] = one.T.astype(BF16)
            qkv[part, :, lanes] = one.astype(BF16)
    hidden = wup.shape[1]
    for start in range(0, hidden, 256):
        lanes = slice(start, start + 256)
        act, der = gelu_and_slope(mm(feed, wup[:, lanes]))
        active[:, lanes] = act.astype(BF16)
        slope[:, lanes] = der.astype(BF16)


def project(chunk, index, place, tokens, norms, pack, tables, width, hidden, kept):
    model = pack.shape[0]
    return chunk_call(
        partial(project_body, len(chunk)),
        "project",
        3.5,
        index,
        [
            ((tokens, model), BF16, (TOKENS, model), ROWS),
            ((tokens, model), BF16, (TOKENS, model), ROWS),
            ((3, tokens, width), BF16, (3, TOKENS, width), lambda i: (0, i, 0)),
            ((width, tokens), BF16, (width, TOKENS), LANES),
            ((tokens, hidden), BF16, (TOKENS, hidden), ROWS),
            ((tokens, hidden), BF16, (TOKENS, hidden), ROWS),
        ],
        [(way, (TOKENS, model), HERE) for way in chunk]
        + [
            (norms, (4, model), HERE),
            (pack, (model, 3 * width), HERE),
            (pack, (model, hidden), lambda i: (0, 1)),
            (tables[0], (TOKENS, 128), ROWS),
            (tables[1], (TOKENS, 128), ROWS),
        ],
        kept,
        place,
    )


def own_lanes(values, head, factor=None):
    lane = lax.broadcasted_iota(jnp.int32, values.shape, 1) // HEAD_DIM
    if factor is not None:
        values = values * jnp.asarray(factor, values.dtype)
    return jnp.where(lane == head, values, jnp.zeros_like(values))


def attend_body(number, starts, qkv, value_t, active, wout, wdown, context, logsum, partial_sum):
    index = number[0]
    tokens, width = (qkv.shape[1], qkv.shape[2])
    reach = min(tokens, TOKENS + LONGEST_DOC)
    first = pl.multiple_of(jnp.maximum(index * TOKENS + TOKENS - reach, 0), TOKENS)
    at = pl.multiple_of(index * TOKENS, TOKENS)
    key_at = first + lax.broadcasted_iota(jnp.int32, (reach, TOKENS), 0)
    query_at = at + lax.broadcasted_iota(jnp.int32, (reach, TOKENS), 1)
    allowed = (key_at <= query_at) & (key_at >= starts[0:1, pl.ds(at, TOKENS)])
    outs, sums = ([], [])
    for pair in range(width // 128):
        lanes = slice(pair * 128, (pair + 1) * 128)
        keys = qkv[1, pl.ds(first, reach), lanes]
        queries = qkv[0, pl.ds(at, TOKENS), lanes]
        for head in range(128 // HEAD_DIM):
            query = own_lanes(queries, head, 1.0 / math.sqrt(HEAD_DIM))
            scores = jnp.where(allowed, mm_nt(keys, query), NEG_FILL)
            peak = jnp.max(scores, axis=0, keepdims=True)
            raised = jnp.exp(scores - peak)
            total = jnp.sum(raised, axis=0, keepdims=True)
            sums.append(peak + jnp.log(total))
            begin = pair * 128 + head * HEAD_DIM
            values = value_t[begin : begin + HEAD_DIM, pl.ds(first, reach)]
            outs.append(mm(values, raised.astype(BF16)) * (1.0 / total))
    mixed = jnp.concatenate(outs, axis=0).T.astype(BF16)
    context[...] = mixed
    for head, one in enumerate(sums):
        logsum[head : head + 1, :] = one
    partial_sum[...] = (mm_nt(mixed, wout[...]) + mm_nt(active[...], wdown[...])).astype(BF16)


def attend(index, starts, qkv, value_t, active, pack, kept):
    _, tokens, width = qkv.shape
    hidden = active.shape[1]
    model = pack.shape[0]
    heads = width // HEAD_DIM
    return chunk_call(
        attend_body,
        "attend",
        3,
        index,
        [
            ((tokens, width), BF16, (TOKENS, width), ROWS),
            ((heads, tokens), F32, (heads, TOKENS), LANES),
            ((TOKENS, model), BF16, (TOKENS, model), HERE),
        ],
        [
            (starts, (1, tokens), HERE),
            (qkv, (3, tokens, width), lambda i: (0, 0, 0)),
            (value_t, (width, tokens), HERE),
            (active, (TOKENS, hidden), ROWS),
            (pack, (model, width), lambda i: (0, 3)),
            (pack, (model, hidden), lambda i: (0, 2)),
        ],
        kept,
    )


def through_branch_body(ways, number, *refs):
    wout, wdown, slope, pre_grad, context_grad, copied = refs[ways:]
    grads = added(refs[:ways])
    keep_by_owner(copied, (number[1], number[2]), grads)
    pre_grad[...] = (mm(grads, wdown[...]) * slope[...].astype(F32)).astype(BF16)
    context_grad[...] = mm(grads, wout[...]).astype(BF16)


def through_branch(chunk, index, place, pack, slope, width, kept):
    tokens, hidden = slope.shape
    model = pack.shape[0]
    return chunk_call(
        partial(through_branch_body, len(chunk)),
        "through_branch",
        1.5,
        index,
        [
            ((tokens, hidden), BF16, (TOKENS, hidden), ROWS),
            ((tokens, width), BF16, (TOKENS, width), ROWS),
            ((tokens, model), BF16, (TOKENS, model), ROWS),
        ],
        [(way, (TOKENS, model), HERE) for way in chunk]
        + [
            (pack, (model, width), lambda i: (0, 3)),
            (pack, (model, hidden), lambda i: (0, 2)),
            (slope, (TOKENS, hidden), ROWS),
        ],
        kept,
        place,
    )


def window_of(block, size):
    return (max(0, block * size - LONGEST_DOC), (block + 1) * size)


def attend_back_kernel(starts, qkv, grads, logsum, cosine, sine, out, key_sum, value_sum):
    size = TOKENS
    factor = 1.0 / math.sqrt(HEAD_DIM)
    tokens = qkv.shape[1]
    heads = 128 // HEAD_DIM
    key_t = qkv[1].astype(F32).T.astype(BF16)
    key_sum[...] = jnp.zeros_like(key_sum)
    value_sum[...] = jnp.zeros_like(value_sum)
    for block in range(tokens // size):
        first, last = window_of(block, size)
        rows = slice(block * size, (block + 1) * size)
        shape = (last - first, size)
        key_at = first + lax.broadcasted_iota(jnp.int32, shape, 0)
        query_at = block * size + lax.broadcasted_iota(jnp.int32, shape, 1)
        allowed = (key_at <= query_at) & (key_at >= starts[0:1, rows])
        key_part, value_part, query_parts = (0.0, 0.0, [])
        for head in range(heads):
            query = own_lanes(qkv[0, rows], head, factor)
            grad = own_lanes(grads[rows], head)
            scores = jnp.where(allowed, mm_nt(qkv[1, first:last], query), NEG_FILL)
            probs = jnp.exp(scores - logsum[0, head : head + 1, rows])
            probs_grad = mm_nt(qkv[2, first:last], grad)
            inner = jnp.sum(probs_grad * probs, axis=0, keepdims=True)
            score_grad = (probs * (probs_grad - inner)).astype(BF16)
            key_part += mm(score_grad, query)
            value_part += mm(probs.astype(BF16), grad)
            query_parts.append(
                mm(key_t[head * HEAD_DIM : (head + 1) * HEAD_DIM, first:last], score_grad)
            )
        key_sum[first:last] += key_part
        value_sum[first:last] += value_part
        query_grad = jnp.concatenate(query_parts, axis=0).T * factor
        out[0, rows] = turn(query_grad, cosine[rows], sine[rows], -1.0).astype(BF16)
    out[1] = turn(key_sum[...], cosine[...], sine[...], -1.0).astype(BF16)
    out[2] = value_sum[...].astype(BF16)


def attend_back(starts, qkv, context_grad, logsum, tables):
    _, tokens, width = qkv.shape
    pairs = width // 128
    heads = 128 // HEAD_DIM
    return pl.pallas_call(
        attend_back_kernel,
        grid=(pairs,),
        in_specs=[
            pl.BlockSpec((1, tokens), lambda p: (0, 0)),
            pl.BlockSpec((3, tokens, 128), lambda p: (0, 0, p)),
            pl.BlockSpec((tokens, 128), lambda p: (0, p)),
            pl.BlockSpec((1, heads, tokens), lambda p: (p, 0, 0)),
            pl.BlockSpec((tokens, 128), lambda p: (0, 0)),
            pl.BlockSpec((tokens, 128), lambda p: (0, 0)),
        ],
        out_specs=pl.BlockSpec((3, tokens, 128), lambda p: (0, 0, p)),
        out_shape=jax.ShapeDtypeStruct((3, tokens, width), BF16),
        scratch_shapes=[pltpu.VMEM((tokens, 128), F32), pltpu.VMEM((tokens, 128), F32)],
        compiler_params=params(),
        cost_estimate=cost(11),
        name="attend_back",
    )(starts, qkv, context_grad, logsum.reshape(pairs, heads, tokens), *tables)


def through_inputs_body(ways, number, *refs):
    norms, project_grad, pre_grad, wqkv, wup, normed_grad, terms = refs[ways:]
    normed, _ = normalize(added(refs[:ways]))
    width = project_grad.shape[2]
    attn = mm_nt(project_grad[0], wqkv[:, :width])
    attn += mm_nt(project_grad[1], wqkv[:, width : 2 * width])
    attn += mm_nt(project_grad[2], wqkv[:, 2 * width :])
    feed = mm_nt(pre_grad[...], wup[...])
    normed_grad[...] = (attn * norms[0:1] + feed * norms[2:3]).astype(BF16)
    terms[0:1] = jnp.sum(attn * normed, axis=0, keepdims=True)
    terms[1:2] = jnp.sum(attn, axis=0, keepdims=True)
    terms[2:3] = jnp.sum(feed * normed, axis=0, keepdims=True)
    terms[3:4] = jnp.sum(feed, axis=0, keepdims=True)


def through_inputs(chunk, index, norms, project_grad, pre_grad, pack):
    model = pack.shape[0]
    hidden = pre_grad.shape[1]
    width = project_grad.shape[2]
    return chunk_call(
        partial(through_inputs_body, len(chunk)),
        "through_inputs",
        0.3,
        index,
        [
            ((TOKENS, model), BF16, (TOKENS, model), HERE),
            ((4, model), F32, (4, model), HERE),
        ],
        [(way, (TOKENS, model), HERE) for way in chunk]
        + [
            (norms, (4, model), HERE),
            (project_grad, (3, TOKENS, width), lambda i: (0, i, 0)),
            (pre_grad, (TOKENS, hidden), ROWS),
            (pack, (model, 3 * width), HERE),
            (pack, (model, hidden), lambda i: (0, 1)),
        ],
    )


def outer_kernel(attn_in, feed_in, upstream, project_grad, context, pre_grad, active, out):
    step = pl.program_id(0)

    def fill(left, right, start=0):
        width = right.shape[1]
        out[:, :, start : start + width] = (
            lax.dot_general(left[...], right, (((0,), (0,)), ((), ())), preferred_element_type=F32)
            .astype(BF16)
            .reshape(*out.shape[:2], width)
        )

    @pl.when(step == 0)
    def _():
        fill(attn_in, project_grad[0])
        fill(attn_in, project_grad[1], context.shape[1])

    @pl.when(step == 1)
    def _():
        fill(attn_in, project_grad[2])
        fill(upstream, context[...], context.shape[1])

    pl.when((step == 2) | (step == 3))(lambda: fill(feed_in, pre_grad[...]))
    pl.when(step >= 4)(lambda: fill(upstream, active[...]))


def weight_grads(half, saved, upstream, pre_grad, project_grad):
    attn_in, feed_in, active, context = saved
    tokens, model = attn_in.shape
    width = context.shape[1]
    left = pl.BlockSpec((tokens, model // 2), lambda j: (0, half))
    return pl.pallas_call(
        outer_kernel,
        grid=(6,),
        in_specs=[
            left,
            left,
            left,
            pl.BlockSpec((3, tokens, width), lambda j: (0, 0, 0)),
            pl.BlockSpec((tokens, width), lambda j: (0, 0)),
            pl.BlockSpec((tokens, 2 * width), lambda j: (0, jnp.clip(j - 2, 0, 1))),
            pl.BlockSpec((tokens, 2 * width), lambda j: (0, jnp.clip(j - 4, 0, 1))),
        ],
        out_specs=pl.BlockSpec((4, model // 8, 2 * width), lambda j: (0, 0, j)),
        out_shape=jax.ShapeDtypeStruct((4, model // 8, 12 * width), BF16),
        compiler_params=params(18),
        cost_estimate=cost(0.3),
        name="weight_grads",
    )(attn_in, feed_in, upstream, project_grad, context, pre_grad, active)


def fold_kernel(kept, came, side, ahead, rest):
    half = kept.shape[1] // 2
    both = (kept[...].astype(F32) + came[...].astype(F32)).astype(BF16)
    side[0] = both[1, :half]
    side[1] = both[3, :half]
    ahead[0] = both[2, half:]
    ahead[1] = both[3, half:]
    rest[0] = both[0, :half]
    rest[1] = both[2, :half]
    rest[2] = both[0, half:]
    rest[3] = both[1, half:]


def fold(kept, came):
    _, rows, width = kept.shape
    step = width // 6
    block = lambda n, r: pl.BlockSpec((n, r, step), lambda j: (0, 0, j))
    shape = lambda n: jax.ShapeDtypeStruct((n, rows // 2, width), BF16)
    return pl.pallas_call(
        fold_kernel,
        grid=(6,),
        in_specs=[block(4, rows), block(4, rows)],
        out_specs=[block(2, rows // 2), block(2, rows // 2), block(4, rows // 2)],
        out_shape=[shape(2), shape(2), shape(4)],
        compiler_params=params(),
        cost_estimate=cost(0.3),
        name="fold",
    )(kept, came)


def assemble_kernel(place, *refs):
    pieces, whole = (refs[:-1], refs[-1])
    rows = pieces[0].shape[0]
    each = len(pieces) // 2
    for order, piece in enumerate(pieces):
        core, number = (order // each, min(order % each, 3))
        at = ((place[1] ^ number) * 2 + (place[0] ^ core)) * rows
        at = at + (rows // 2 if order % each == 4 else 0)
        whole[pl.ds(pl.multiple_of(at, rows // 2), piece.shape[0]), :] = piece[...]


def assemble(place, pieces):
    rows, width = pieces[0].shape
    step = width // 6
    return pl.pallas_call(
        assemble_kernel,
        grid_spec=pltpu.PrefetchScalarGridSpec(
            num_scalar_prefetch=1,
            grid=(6,),
            in_specs=[pl.BlockSpec((piece.shape[0], step), lambda j, place: (0, j)) for piece in pieces],
            out_specs=pl.BlockSpec((8 * rows, step), lambda j, place: (0, j)),
        ),
        out_shape=jax.ShapeDtypeStruct((8 * rows, width), BF16),
        compiler_params=params(18),
        cost_estimate=cost(6),
        name="assemble",
    )(place, *pieces)


def unpack_kernel(place, upper, lower, came, qkv, out, up, down):
    width, hidden = (out.shape[0], up.shape[1])
    half = came.shape[0]
    own = jnp.concatenate([upper[...], lower[...]], axis=0)
    for core, block in ((place[0], own), (1 - place[0], came[...].astype(F32))):
        rows = pl.ds(pl.multiple_of(core * half, half), half)
        qkv[rows, :] = block[:, : 3 * width]
        out[:, rows] = block[:, 3 * width : 4 * width].T
        up[rows, :] = block[:, 4 * width : 4 * width + hidden]
        down[:, rows] = block[:, 4 * width + hidden :].T


def unpack(sec, upper, lower, came, width, hidden):
    half = came.shape[0]
    shapes = [(2 * half, 3 * width), (width, 2 * half), (2 * half, hidden), (hidden, 2 * half)]
    return pl.pallas_call(
        unpack_kernel,
        grid_spec=pltpu.PrefetchScalarGridSpec(
            num_scalar_prefetch=1,
            grid=(1,),
            in_specs=[
                pl.BlockSpec(array.shape, lambda i, place: (0, 0)) for array in (upper, lower, came)
            ],
            out_specs=[pl.BlockSpec(shape, lambda i, place: (0, 0)) for shape in shapes],
        ),
        out_shape=[jax.ShapeDtypeStruct(shape, F32) for shape in shapes],
        compiler_params=params(18),
        cost_estimate=cost(2),
        name="unpack",
    )(sec.reshape(1).astype(jnp.int32), upper, lower, came)


def swap(block, axis, bit):
    return lax.ppermute(block, axis, [(i, i ^ bit) for i in range(lax.axis_size(axis))])


def join(*values):
    flat, tree = jax.tree.flatten(values)
    return jax.tree.unflatten(tree, lax.optimization_barrier(tuple(flat)))


def sum_over(value, axis):
    others = [swap(value, axis, bit) for bit in range(1, lax.axis_size(axis))]
    return sum(others, start=value)


def pick(stack, index):
    return lax.dynamic_index_in_dim(stack, index, 0, keepdims=False)


def send_sides(half):
    return (swap(half, "col", 1), swap(half, "col", 2))


def send_corner(side, ahead):
    rows = side.shape[0] // 2
    return [swap(side[:rows], "col", 2), swap(ahead[rows:], "col", 1)]


def add(a, b):
    return a.astype(F32) + b.astype(F32)


def along_row(block, pairs):
    return lax.ppermute(block, "row", pairs)


ONE_OVER = [(0, 1), (1, 0), (2, 3), (3, 2)]
TWO_OVER = [(0, 2), (2, 0), (1, 3), (3, 1)]
MIDDLE = [(1, 2), (2, 1)]
OUTWARD = [(1, 0), (2, 3)]
INWARD = [(0, 1), (3, 2)]


def send_own(own):
    return (along_row(own, TWO_OVER), along_row(own, ONE_OVER))


def pass_on(own, far):
    return (along_row(far, OUTWARD), along_row(own, MIDDLE))


def send_last(share):
    return (along_row(share, INWARD), along_row(share, MIDDLE))


def send_sums(far, passed, near):
    return (along_row(add(far, passed).astype(BF16), TWO_OVER), along_row(near, ONE_OVER))


def fast_shards(
    hidden_in,
    doc_ids,
    qkv_weight,
    out_weight,
    up_weight,
    down_weight,
    attn_gain,
    attn_shift,
    mlp_gain,
    mlp_shift,
    out_cotangent,
):
    sec, row, col = (lax.axis_index("section"), lax.axis_index("row"), lax.axis_index("col"))
    cols, rows = (lax.axis_size("col"), lax.axis_size("row"))
    model = hidden_in.shape[3]
    tokens = doc_ids.shape[2]
    width = qkv_weight.shape[3]
    hidden = up_weight.shape[2]
    block = qkv_weight.shape[1]
    first = sec == 0
    x_own = pick(hidden_in[:, 0], sec)
    docs = pick(doc_ids[:, 0], sec)
    given = pick(out_cotangent[:, 0], sec)

    place = jnp.stack([sec, col]).astype(jnp.int32)
    share = attn_gain.shape[1]

    def enter(kept, chunk, number, layer):
        return project(
            chunk,
            row ^ number,
            place,
            tokens,
            norms[layer],
            packs[layer],
            tables,
            width,
            hidden,
            kept,
        )

    def leave(kept, entered, number, layer):
        _, _, qkv, value_t, active, _ = entered
        *kept, share_of = attend(row ^ number, starts, qkv, value_t, active, packs[layer], kept)
        return (tuple(kept), share_of)

    def back_branch(kept, chunk, number, slope, layer):
        return through_branch(chunk, row ^ number, place, packs[layer], slope, width, kept)

    def back_inputs(chunks, number, layer, project_grad, pre_grad):
        return through_inputs(
            chunks[number], row ^ number, norms[layer], project_grad, pre_grad, packs[layer]
        )

    choose = lambda here, there: jnp.where(first, here, there)

    def by_layer(zero, one):
        away = swap(choose(one, zero), "section", 1)
        here = choose(zero, one)
        return jnp.stack([choose(here, away), choose(away, here)])

    def input_grad(total, own, own_grads):
        normed, scale = normalize(own)
        result = own_grads.astype(F32) + scale * (
            total
            - jnp.mean(total, axis=-1, keepdims=True)
            - normed * jnp.mean(total * normed, axis=-1, keepdims=True)
        )
        return result.astype(BF16)


    far_x0, near_x0 = send_own(x_own)
    vectors = jnp.stack([attn_gain[0], attn_shift[0], mlp_gain[0], mlp_shift[0]])
    norms = lax.dynamic_update_slice(
        jnp.zeros((2, 4, model), F32), vectors[None], (sec, 0, (row * cols + col) * share)
    )
    norms = sum_over(norms, "row")
    own_pack = jnp.concatenate(
        [
            qkv_weight[0].reshape(block, 3 * width),
            out_weight[0].T,
            up_weight[0],
            down_weight[0].T,
        ],
        axis=1,
    )
    half_of = lambda core: lax.dynamic_slice_in_dim(own_pack, core * (block // 2), block // 2)
    staying, leaving = (half_of(sec), half_of(1 - sec))
    norms, staying, leaving = join(norms, staying, leaving)

    came = swap(leaving, "section", 1)
    norms = sum_over(norms, "section")
    half0, half1 = (jnp.where(first, staying, came), jnp.where(first, came, staying))
    norms, half0, half1 = join(norms, half0, half1)

    norms = sum_over(norms, "col")
    norms, half0 = join(norms, half0)

    side0, ahead0 = send_sides(half0)
    starts = jnp.sum((docs[None, :] < docs[:, None]).astype(jnp.int32), axis=1)
    tables = rope_tables(docs, starts)
    starts = starts[None]
    half0, side0, ahead0, starts, tables, far_x0, near_x0 = join(
        half0, side0, ahead0, starts, tables, far_x0, near_x0
    )
    passed_x0, middle_x0 = pass_on(x_own, far_x0)
    chunks_x0 = [(x_own,), (near_x0,), (far_x0,), (middle_x0, passed_x0)]

    across0 = send_corner(side0, ahead0)
    mine = [half0, side0, ahead0]
    theirs = [swap(piece, "section", 1) for piece in mine]
    mine, theirs, across0, chunks_x0, given = join(mine, theirs, across0, chunks_x0, given)

    theirs = theirs + [swap(piece, "section", 1) for piece in across0]
    mine, theirs, half1, given = join(mine + across0, theirs, half1, given)

    far_g1, near_g1 = send_own(given)
    side1, ahead1 = send_sides(half1)
    packs = [assemble(place, mine + theirs), None]
    entered0 = ()
    for number in range(4):
        entered0 = enter(entered0, chunks_x0[number], number, 0)
    kept, last = leave((), entered0, 3, 0)
    far_g1, near_g1, side1, ahead1, entered0, kept, last, packs = join(
        far_g1, near_g1, side1, ahead1, entered0, kept, last, packs
    )

    passed_y0, middle_y0 = send_last(last)
    kept, far = leave(kept, entered0, 2, 0)
    kept, near = leave(kept, entered0, 1, 0)
    (context0, logsum0), share_of = leave(kept, entered0, 0, 0)
    passed_g1, middle_g1 = pass_on(given, far_g1)
    passed_y0, middle_y0, far, near, share_of, half1, side1, ahead1, passed_g1, middle_g1 = join(
        passed_y0, middle_y0, far, near, share_of, half1, side1, ahead1, passed_g1, middle_g1
    )

    far_y0, near_y0 = send_sums(far, passed_y0, near)
    across1 = send_corner(side1, ahead1)
    mine = [half1, side1, ahead1] + across1
    theirs = [swap(piece, "section", 1) for piece in mine]
    far_y0, near_y0, mine, theirs = join(far_y0, near_y0, mine, theirs)
    total = add(share_of, near_y0) + add(middle_y0, far_y0)
    y0_own = (x_own.astype(F32) + total).astype(BF16)

    far_x1, near_x1 = send_own(y0_own)
    packs[1] = assemble(place, mine + theirs)
    entered1 = enter((), (y0_own,), 0, 1)
    branch1 = back_branch((), (given,), 0, entered1[5], 1)
    far_x1, near_x1, y0_own, entered1, branch1 = join(far_x1, near_x1, y0_own, entered1, branch1)

    passed_x1, middle_x1 = pass_on(y0_own, far_x1)
    entered1 = enter(entered1, (near_x1,), 1, 1)
    branch1 = back_branch(branch1, (near_g1,), 1, entered1[5], 1)
    entered1 = enter(entered1, (far_x1,), 2, 1)
    branch1 = back_branch(branch1, (far_g1,), 2, entered1[5], 1)
    passed_x1, middle_x1, entered1, branch1 = join(passed_x1, middle_x1, entered1, branch1)

    chunks_x1 = [(y0_own,), (near_x1,), (far_x1,), (middle_x1, passed_x1)]
    entered1 = enter(entered1, chunks_x1[3], 3, 1)
    pre_grad1, context_grad1, grads1 = back_branch(
        branch1, (middle_g1, passed_g1), 3, entered1[5], 1
    )
    context_grad1, entered1 = join(context_grad1, entered1)
    kept, last_b1 = leave((), entered1, 3, 1)
    kept, far_b1 = leave(kept, entered1, 2, 1)
    kept, near_b1 = leave(kept, entered1, 1, 1)
    (context1, logsum1), share_b1 = leave(kept, entered1, 0, 1)

    saved1 = (entered1[0], entered1[1], entered1[4], context1)
    project_grad1 = attend_back(starts, entered1[2], context_grad1, logsum1, tables)
    last, terms1 = back_inputs(chunks_x1, 3, 1, project_grad1, pre_grad1)
    last, project_grad1 = join(last, project_grad1)

    passed_n1, middle_n1 = send_last(last)
    others = [back_inputs(chunks_x1, number, 1, project_grad1, pre_grad1) for number in (2, 1, 0)]
    (far, near, share_of), terms = zip(*others)
    terms1 = sum(terms, start=terms1)
    far = add(far, passed_n1).astype(BF16)
    leaving1 = weight_grads(1, saved1, grads1, pre_grad1, project_grad1)
    far, middle_n1, near, leaving1, project_grad1 = join(
        far, middle_n1, near, leaving1, project_grad1
    )

    far_n1, near_n1 = (along_row(far, TWO_OVER), along_row(near, ONE_OVER))
    came1 = swap(leaving1, "section", 1)
    kept1 = weight_grads(0, saved1, grads1, pre_grad1, project_grad1)
    far_n1, near_n1, came1, kept1 = join(far_n1, near_n1, came1, kept1)
    total = add(share_of, near_n1) + add(middle_n1, far_n1)
    dx1_own = input_grad(total, y0_own, given)

    slope0 = entered0[5]
    far_g0, near_g0 = send_own(dx1_own)
    side1, ahead1, rest1 = fold(kept1, came1)
    first1, second1 = (swap(side1, "col", 1), swap(ahead1, "col", 2))
    branch0 = back_branch((), (dx1_own,), 0, slope0, 0)
    far_g0, near_g0, dx1_own, last_b1, branch0 = join(
        far_g0, near_g0, dx1_own, last_b1, branch0
    )

    passed_y1 = along_row(last_b1, INWARD)
    passed_g0, middle_g0 = pass_on(dx1_own, far_g0)
    branch0 = back_branch(branch0, (near_g0,), 1, slope0, 0)
    branch0 = back_branch(branch0, (far_g0,), 2, slope0, 0)
    passed_g0, middle_g0, first1, second1, last_b1, near_b1, far_b1, passed_y1 = join(
        passed_g0, middle_g0, first1, second1, last_b1, near_b1, far_b1, passed_y1
    )

    passed1 = (
        swap(add(rest1[1], first1[1]).astype(BF16), "col", 2),
        swap(add(rest1[3], second1[1]).astype(BF16), "col", 1),
    )
    far_y1 = along_row(add(far_b1, passed_y1).astype(BF16), TWO_OVER)
    pre_grad0, context_grad0, grads0 = back_branch(branch0, (middle_g0, passed_g0), 3, slope0, 0)
    saved0 = (entered0[0], entered0[1], entered0[4], context0)
    project_grad0 = attend_back(starts, entered0[2], context_grad0, logsum0, tables)
    last, terms0 = back_inputs(chunks_x0, 3, 0, project_grad0, pre_grad0)
    last, project_grad0, passed1, far_y1, near_b1, last_b1 = join(
        last, project_grad0, passed1, far_y1, near_b1, last_b1
    )

    passed_n0, middle_n0 = send_last(last)
    leaving0 = weight_grads(1, saved0, grads0, pre_grad0, project_grad0)
    others = [back_inputs(chunks_x0, number, 0, project_grad0, pre_grad0) for number in (2, 1, 0)]
    (far, near, share_of), terms = zip(*others)
    terms = sum_over(sum_over(jnp.stack([sum(terms, start=terms0), terms1]), "section"), "col")
    passed_n0, middle_n0, far, near, terms, leaving0, project_grad0 = join(
        passed_n0, middle_n0, far, near, terms, leaving0, project_grad0
    )

    far_n0, near_n0 = send_sums(far, passed_n0, near)
    came0 = swap(leaving0, "section", 1)
    kept0 = weight_grads(0, saved0, grads0, pre_grad0, project_grad0)
    side0, ahead0, rest0 = fold(kept0, came0)
    sums1 = (
        add(add(rest1[0], first1[0]), passed1[0]),
        add(add(rest1[2], second1[0]), passed1[1]),
    )
    far_n0, near_n0, side0, ahead0, terms, sums1, last_b1, near_b1 = join(
        far_n0, near_n0, side0, ahead0, terms, sums1, last_b1, near_b1
    )

    first0, second0 = (swap(side0, "col", 1), swap(ahead0, "col", 2))
    middle_y1, near_y1 = (along_row(last_b1, MIDDLE), along_row(near_b1, ONE_OVER))
    total = add(share_of, near_n0) + add(middle_n0, far_n0)
    dx0_own = input_grad(total, x_own, dx1_own)
    terms, dx0_own = join(terms, dx0_own)
    terms = sum_over(terms, "row")
    grads_out = by_layer(dx0_own, dx1_own)
    first0, second0, grads_out, middle_y1, near_y1, terms = join(
        first0, second0, grads_out, middle_y1, near_y1, terms
    )

    passed0 = (
        swap(add(rest0[1], first0[1]).astype(BF16), "col", 2),
        swap(add(rest0[3], second0[1]).astype(BF16), "col", 1),
    )
    total = add(share_b1, near_y1) + add(middle_y1, far_y1)
    y1_own = (y0_own.astype(F32) + total).astype(BF16)
    outputs = by_layer(y0_own, y1_own)
    sums0 = (
        add(add(rest0[0], first0[0]), passed0[0]),
        add(add(rest0[2], second0[0]), passed0[1]),
    )

    leaving = jnp.concatenate([choose(b, a) for a, b in zip(sums0, sums1)]).astype(BF16)
    upper, lower = [choose(a, b) for a, b in zip(sums0, sums1)]
    qkv_grad, out_grad, up_grad, down_grad = unpack(
        sec, upper, lower, swap(leaving, "section", 1), width, hidden
    )
    terms = pick(terms, sec)
    terms = lax.dynamic_slice_in_dim(terms, (row * cols + col) * share, share, 1)

    return (
        outputs[None, :, None],
        grads_out[None, :, None],
        qkv_grad.reshape(1, block, 3, width),
        out_grad[None],
        up_grad[None],
        down_grad[None],
        terms[None, 0],
        terms[None, 1],
        terms[None, 2],
        terms[None, 3],
    )


def from_behind(block, axis, distance):
    devices = range(lax.axis_size(axis))
    route = [(i - distance, i) for i in devices if i - distance in devices]
    return lax.ppermute(block, axis, route)


def positions_of(docs):
    length = docs.shape[0]
    index = jnp.arange(length, dtype=jnp.int32)
    starts = jnp.concatenate([jnp.ones((1,), jnp.bool_), docs[1:] != docs[:-1]])
    first = lax.cummax(jnp.where(starts, index, 0), axis=0)
    return index - first


def rotary_tables(docs):
    half = ROT // 2
    freqs = 10000.0 ** (-2.0 * jnp.arange(half, dtype=jnp.float32) / ROT)
    angles = positions_of(docs).astype(jnp.float32)[:, None] * freqs[None, :]
    return (jnp.cos(angles)[:, None, :], jnp.sin(angles)[:, None, :])


def rotate(values, cosine, sine):
    half = ROT // 2
    front = values[..., :half]
    back = values[..., half:ROT]
    return jnp.concatenate(
        [front * cosine - back * sine, back * cosine + front * sine, values[..., ROT:]], axis=-1
    )


def rotate_back(grads, cosine, sine):
    half = ROT // 2
    front = grads[..., :half]
    back = grads[..., half:ROT]
    return jnp.concatenate(
        [front * cosine + back * sine, back * cosine - front * sine, grads[..., ROT:]], axis=-1
    )


def block_mask(docs, start, size):
    rows = start + jnp.arange(size, dtype=jnp.int32)
    cols = jnp.arange(docs.shape[0], dtype=jnp.int32)
    row_docs = lax.dynamic_slice_in_dim(docs, start, size)
    return (row_docs[:, None] == docs[None, :]) & (cols[None, :] <= rows[:, None])


def block_scores(query, key, docs, start, block):
    factor = 1.0 / math.sqrt(query.shape[2])
    rows = lax.dynamic_slice_in_dim(query, start, block)
    scores = jnp.einsum("qhd,khd->hqk", rows, key, preferred_element_type=jnp.float32) * factor
    allowed = block_mask(docs, start, block)[None]
    return (rows, jnp.where(allowed, scores, NEG_FILL))


def attend_forward(query, key, value, docs):
    length, heads, width = query.shape
    block = min(512, length)

    def one_block(number):
        start = number * block
        rows, scores = block_scores(query, key, docs, start, block)
        peak = jnp.max(scores, axis=-1, keepdims=True)
        raised = jnp.exp(scores - peak)
        total = jnp.sum(raised, axis=-1, keepdims=True)
        probs = (raised / total).astype(jnp.bfloat16)
        context = jnp.einsum(
            "hqk,khd->qhd", probs, value, preferred_element_type=jnp.float32
        ).astype(jnp.bfloat16)
        return (context, (peak + jnp.log(total))[..., 0])

    context, logsum = lax.map(one_block, jnp.arange(length // block, dtype=jnp.int32))
    return (context.reshape(length, heads, width), logsum)


def attend_backward(query, key, value, docs, logsum, context_grad):
    length, heads, width = query.shape
    block = min(512, length)
    factor = 1.0 / math.sqrt(width)

    def one_block(carry, inputs):
        key_grad, value_grad = carry
        number, block_logsum = inputs
        start = number * block
        rows, scores = block_scores(query, key, docs, start, block)
        rows_grad = lax.dynamic_slice_in_dim(context_grad, start, block)
        probs_full = jnp.exp(scores - block_logsum[:, :, None])
        probs = probs_full.astype(jnp.bfloat16)
        context = jnp.einsum(
            "hqk,khd->qhd", probs, value, preferred_element_type=jnp.float32
        ).astype(jnp.bfloat16)
        probs_grad = jnp.einsum(
            "qhd,khd->hqk", rows_grad, value, preferred_element_type=jnp.float32
        )
        inner = jnp.sum(probs_grad * probs_full, axis=-1, keepdims=True)
        score_grad = (probs_full * (probs_grad - inner)).astype(jnp.bfloat16)
        query_grad = (
            jnp.einsum("hqk,khd->qhd", score_grad, key, preferred_element_type=jnp.float32) * factor
        )
        key_grad = (
            key_grad
            + jnp.einsum("hqk,qhd->khd", score_grad, rows, preferred_element_type=jnp.float32)
            * factor
        )
        value_grad = value_grad + jnp.einsum(
            "hqk,qhd->khd", probs, rows_grad, preferred_element_type=jnp.float32
        )
        return ((key_grad, value_grad), (context, query_grad))

    zeros = jnp.zeros((length, heads, width), jnp.float32)
    numbers = jnp.arange(length // block, dtype=jnp.int32)
    (key_grad, value_grad), (context, query_grad) = lax.scan(
        one_block, (zeros, zeros), (numbers, logsum)
    )
    return (
        context.reshape(length, heads * width),
        query_grad.reshape(length, heads, width),
        key_grad,
        value_grad,
    )


def gather_features(shard):
    return lax.all_gather(shard, "row", axis=0, tiled=True)


def recompute_inputs(full, docs, norms, weights):
    gain_a, shift_a, gain_m, shift_m = norms
    qkv_full = weights[0]
    normed, scale = normalize(full)
    attn_in = (normed * gain_a + shift_a).astype(jnp.bfloat16)
    feed_in = (normed * gain_m + shift_m).astype(jnp.bfloat16)
    length = full.shape[0]
    heads_here = qkv_full.shape[2] // HEAD_DIM
    project = jnp.einsum("td,dke->tke", attn_in, qkv_full, preferred_element_type=jnp.float32)
    cosine, sine = rotary_tables(docs)
    query = rotate(project[:, 0].reshape(length, heads_here, HEAD_DIM), cosine, sine).astype(
        jnp.bfloat16
    )
    key = rotate(project[:, 1].reshape(length, heads_here, HEAD_DIM), cosine, sine).astype(
        jnp.bfloat16
    )
    value = project[:, 2].reshape(length, heads_here, HEAD_DIM).astype(jnp.bfloat16)
    pre = jnp.dot(feed_in, weights[2], preferred_element_type=jnp.float32)
    return (normed, scale, attn_in, feed_in, query, key, value, pre, cosine, sine)


def layer_forward(shard, docs, full, norms, weights):
    normed, scale, attn_in, feed_in, query, key, value, pre, cosine, sine = recompute_inputs(
        full, docs, norms, weights
    )
    length = full.shape[0]
    context, logsum = attend_forward(query, key, value, docs)
    active = jax.nn.gelu(pre, approximate=False).astype(jnp.bfloat16)
    partial_sum = jnp.dot(
        context.reshape(length, -1), weights[1], preferred_element_type=jnp.float32
    )
    partial_sum = partial_sum + jnp.dot(active, weights[3], preferred_element_type=jnp.float32)
    branch = lax.psum_scatter(
        partial_sum.astype(jnp.bfloat16), "row", scatter_dimension=0, tiled=True
    ).astype(jnp.float32)
    return ((shard.astype(jnp.float32) + branch).astype(jnp.bfloat16), logsum)


def layer_backward(docs, full, logsum, upstream, norms, weights):
    gain_a, shift_a, gain_m, shift_m = norms
    qkv_full, out_full, up_full, down_full = weights
    normed, scale, attn_in, feed_in, query, key, value, pre, cosine, sine = recompute_inputs(
        full, docs, norms, weights
    )
    length = full.shape[0]
    heads_here = query.shape[1]
    active = jax.nn.gelu(pre, approximate=False).astype(jnp.bfloat16)
    upstream_full = lax.all_gather(upstream, "row", axis=0, tiled=True)
    down_part = jnp.einsum("tf,td->fd", active, upstream_full, preferred_element_type=jnp.float32)
    act_grad = jnp.einsum("td,fd->tf", upstream_full, down_full, preferred_element_type=jnp.float32)
    pre_grad = jax.vjp(partial(jax.nn.gelu, approximate=False), pre)[1](act_grad)[0].astype(
        jnp.bfloat16
    )
    up_part = jnp.einsum("td,tf->df", feed_in, pre_grad, preferred_element_type=jnp.float32)
    feed_grad = jnp.einsum("tf,df->td", pre_grad, up_full, preferred_element_type=jnp.float32)
    context_grad = jnp.einsum(
        "td,ed->te", upstream_full, out_full, preferred_element_type=jnp.float32
    ).astype(jnp.bfloat16)
    context_grad = context_grad.reshape(length, heads_here, HEAD_DIM)
    context, query_grad, key_grad, value_grad = attend_backward(
        query, key, value, docs, logsum, context_grad
    )
    out_part = jnp.einsum("te,td->ed", context, upstream_full, preferred_element_type=jnp.float32)
    project_grad = jnp.stack(
        [
            rotate_back(query_grad, cosine, sine).reshape(length, -1),
            rotate_back(key_grad, cosine, sine).reshape(length, -1),
            value_grad.reshape(length, -1),
        ],
        axis=1,
    ).astype(jnp.bfloat16)
    qkv_part = jnp.einsum("td,tke->dke", attn_in, project_grad, preferred_element_type=jnp.float32)
    attn_grad = jnp.einsum(
        "tke,dke->td", project_grad, qkv_full, preferred_element_type=jnp.float32
    )
    own_rows = upstream.shape[0]
    offset = lax.axis_index("row") * own_rows
    normed_part = lax.dynamic_slice_in_dim(normed, offset, own_rows, 0)
    scale_part = lax.dynamic_slice_in_dim(scale, offset, own_rows, 0)
    attn_piece, feed_piece = (
        lax.psum_scatter(
            attn_grad.astype(jnp.bfloat16), "row", scatter_dimension=0, tiled=True
        ).astype(jnp.float32),
        lax.psum_scatter(
            feed_grad.astype(jnp.bfloat16), "row", scatter_dimension=0, tiled=True
        ).astype(jnp.float32),
    )
    normed_grad = attn_piece * gain_a + feed_piece * gain_m
    gain_terms = (
        jnp.sum(attn_piece * normed_part, axis=0),
        jnp.sum(attn_piece, axis=0),
        jnp.sum(feed_piece * normed_part, axis=0),
        jnp.sum(feed_piece, axis=0),
    )
    row_sum = jnp.sum(normed_grad, axis=-1)
    cross_sum = jnp.sum(normed_grad * normed_part, axis=-1)
    count = full.shape[1]
    input_grad = upstream.astype(jnp.float32) + scale_part * (
        normed_grad - row_sum[:, None] / count - normed_part * cross_sum[:, None] / count
    )
    return (input_grad, (qkv_part, out_part, up_part, down_part), gain_terms)


def general_shards(
    hidden_in,
    doc_ids,
    qkv_weight,
    out_weight,
    up_weight,
    down_weight,
    attn_gain,
    attn_shift,
    mlp_gain,
    mlp_shift,
    out_cotangent,
):
    micro = hidden_in.shape[0]
    first_section = lax.axis_index("section") == 0
    norms = (
        lax.all_gather(attn_gain[0], ("row", "col"), axis=0, tiled=True),
        lax.all_gather(attn_shift[0], ("row", "col"), axis=0, tiled=True),
        lax.all_gather(mlp_gain[0], ("row", "col"), axis=0, tiled=True),
        lax.all_gather(mlp_shift[0], ("row", "col"), axis=0, tiled=True),
    )
    weights = (
        lax.all_gather(qkv_weight[0], "col", axis=0, tiled=True),
        lax.all_gather(out_weight[0], "col", axis=1, tiled=True),
        lax.all_gather(up_weight[0], "col", axis=0, tiled=True),
        lax.all_gather(down_weight[0], "col", axis=1, tiled=True),
    )
    received = jnp.zeros_like(hidden_in[0, 0])
    tick_inputs, tick_docs, tick_fulls, tick_outputs, tick_logsums = ([], [], [], [], [])
    for tick in range(micro + 1):
        own = hidden_in[min(tick, micro - 1), 0]
        shard = jnp.where(first_section, own, received)
        docs = jnp.where(
            first_section, doc_ids[min(tick, micro - 1), 0], doc_ids[max(tick - 1, 0), 0]
        )
        full = gather_features(shard)
        result, logsum = layer_forward(shard, docs, full, norms, weights)
        tick_inputs.append(shard)
        tick_docs.append(docs)
        tick_fulls.append(full)
        tick_outputs.append(result)
        tick_logsums.append(logsum)
        if tick < micro:
            received = from_behind(result, "section", 1)
    outputs = jnp.stack(
        [
            jnp.where(first_section, tick_outputs[number], tick_outputs[number + 1])
            for number in range(micro)
        ]
    )
    received = jnp.zeros_like(hidden_in[0, 0])
    matrix_totals = None
    gain_totals = None
    tick_grads = []
    for tick in range(micro + 1):
        early = max(tick - 1, 0)
        later = min(tick + 1, micro)
        if tick < micro:
            given = out_cotangent[tick, 0]
        else:
            given = jnp.zeros_like(out_cotangent[0, 0])
        upstream = jnp.where(first_section, received, given)
        shard = jnp.where(first_section, tick_inputs[early], tick_inputs[later])
        docs = jnp.where(first_section, tick_docs[early], tick_docs[later])
        logsum = jnp.where(first_section, tick_logsums[early], tick_logsums[later])
        full = gather_features(shard)
        input_grad, matrices, gain_terms = layer_backward(
            docs, full, logsum, upstream, norms, weights
        )
        if matrix_totals is None:
            matrix_totals = matrices
            gain_totals = gain_terms
        else:
            matrix_totals = jax.tree.map(jnp.add, matrix_totals, matrices)
            gain_totals = jax.tree.map(jnp.add, gain_totals, gain_terms)
        grad_low = input_grad.astype(jnp.bfloat16)
        tick_grads.append(grad_low)
        if tick < micro:
            received = from_behind(grad_low, "section", -1)
    grads_in = jnp.stack(
        [
            jnp.where(first_section, tick_grads[number + 1], tick_grads[number])
            for number in range(micro)
        ]
    )
    qkv_sum, out_sum, up_sum, down_sum = matrix_totals
    gain_a_sum, shift_a_sum, gain_m_sum, shift_m_sum = gain_totals
    qkv_total, out_total, up_total, down_total = (
        lax.psum_scatter(
            qkv_sum.astype(jnp.bfloat16), "col", scatter_dimension=0, tiled=True
        ).astype(jnp.float32),
        lax.psum_scatter(
            out_sum.astype(jnp.bfloat16), "col", scatter_dimension=1, tiled=True
        ).astype(jnp.float32),
        lax.psum_scatter(
            up_sum.astype(jnp.bfloat16), "col", scatter_dimension=0, tiled=True
        ).astype(jnp.float32),
        lax.psum_scatter(
            down_sum.astype(jnp.bfloat16), "col", scatter_dimension=1, tiled=True
        ).astype(jnp.float32),
    )
    gain_a_total, shift_a_total, gain_m_total, shift_m_total = (
        lax.psum_scatter(gain_a_sum, ("row", "col"), scatter_dimension=0, tiled=True),
        lax.psum_scatter(shift_a_sum, ("row", "col"), scatter_dimension=0, tiled=True),
        lax.psum_scatter(gain_m_sum, ("row", "col"), scatter_dimension=0, tiled=True),
        lax.psum_scatter(shift_m_sum, ("row", "col"), scatter_dimension=0, tiled=True),
    )
    return (
        outputs[None, :, None],
        grads_in[None, :, None],
        qkv_total[None],
        out_total[None],
        up_total[None],
        down_total[None],
        gain_a_total[None],
        shift_a_total[None],
        gain_m_total[None],
        shift_m_total[None],
    )


def shards(*arrays):
    hidden_in, qkv_weight, up_weight = (arrays[0], arrays[2], arrays[4])
    micro, seqs, own_tokens, model = hidden_in.shape
    width, hidden = (qkv_weight.shape[3], up_weight.shape[2])
    sizes = tuple(lax.axis_size(axis) for axis in ("section", "row", "col"))
    fits = (
        sizes == (2, 4, 4) and (micro, seqs) == (2, 1)
        and own_tokens == TOKENS
        and width % 128 == 0
        and 4 * width == hidden
    )
    return fast_shards(*arrays) if fits else general_shards(*arrays)


def solution(mesh):
    placed = (
        P(None, "col", "row", None),
        P(None, "col", None),
        P("section", "col", None, "row"),
        P("section", "row", "col"),
        P("section", "col", "row"),
        P("section", "row", "col"),
        P("section", ("row", "col")),
        P("section", ("row", "col")),
        P("section", ("row", "col")),
        P("section", ("row", "col")),
        P(None, "col", "row", None),
    )
    return jax.shard_map(
        shards,
        mesh=mesh,
        in_specs=placed,
        out_specs=(
            P("section", None, "col", "row", None),
            P("section", None, "col", "row", None),
            P("section", "col", None, "row"),
            P("section", "row", "col"),
            P("section", "col", "row"),
            P("section", "row", "col"),
            P("section", ("row", "col")),
            P("section", ("row", "col")),
            P("section", ("row", "col")),
            P("section", ("row", "col")),
        ),
        check_vma=False,
    )
```
